512 devices in a mesh: ctx: 64 (over z, x), head: 8 (over y, core).
Axes of the slice: x: 4, y: 4, z: 16, core: 2. Of those that a mesh axis runs over, the one named last changes fastest.
Arguments:
- queries: bfloat16 [8192, 128, 192], P('ctx', 'head')
- up_weight: bfloat16 [128, 128, 512], P('head'), may hold values from -0.5 to 0.5
- index_query: bfloat16 [8192, 64, 128], P(('ctx', 'head'))
- index_weight: float32 [8192, 64], P(('ctx', 'head')), may hold values from -3 to 3
- cache_entry: bfloat16 [8, 64, 64, 576], P(None, 'ctx'), may hold values from -6 to 6
- index_key: bfloat16 [8, 64, 64, 128], P(None, 'ctx'), may hold values from -6 to 6
- block_position: int32 [128], P('ctx'), may hold values from 384 to 511, as said below
- picked_blocks: int32 [128, 32], P('ctx'), may hold values from 0 to 511, as said below
Outputs:
- key_grad: float32 [8, 64, 64, 128], P(None, 'ctx')
- weight_grad: float32 [8192, 64], P(('ctx', 'head'))
The draws below stay inside these ranges and needn't reach their ends.
Inputs may be any that keep to these rules, and one draw needn't show every extreme that they name: `block_position`: every block of the last 128 context blocks is named exactly once. `picked_blocks`: each row names 32 distinct blocks, none after the row's own block_position, and always that block itself; block 0 too, unless the own block lies on shard 0. Taking block b to lie on shard b modulo 512 / 8, a row names exactly 1 block on each of 32 distinct shards, so the 2 rows of one shard name at most 2 blocks on one shard, and shard 0 receives that many from every shard.
All inputs are finite; a program needn't handle non-finite values.
Results may differ from the reference program's by a relative error of at most 0.003.
Values may be sent and summed in bfloat16 or wider, within the bound.
A program may use at most 128 MiB of HBM per device.

```python
import jax
import jax.numpy as jnp
from jax import lax

BLK = 64
TOPK_BLK = 32
HEADS = 128
NOPE = 128
ROPE = 64
LAT = 512
IH = 64
IDX_DIM = 128
OWN_BLK = 8
NQB = 128
CTX_BLK = 512
QTOKENS = 8192
KEYS = 2048
PER_OWNER = 1


def span_positions(key):
    return (3 * NQB + jax.random.permutation(key, NQB)).astype(jnp.int32)


def draw_block_position(key, part):
    positions = span_positions(key)
    return positions


def draw_picked_blocks(key, part):
    positions = span_positions(key)
    key = jax.random.fold_in(key, 23)
    owners = CTX_BLK // OWN_BLK
    chosen = TOPK_BLK // PER_OWNER
    order_key, start_key = jax.random.split(key)
    own_shard = positions % owners
    shard_ids = jnp.arange(owners)[None, :]
    priority = jax.random.randint(order_key, (NQB, owners), 0, 65536) * owners + shard_ids
    forced = (shard_ids == own_shard[:, None]) | (shard_ids == 0)
    priority = jnp.where(forced, priority + 65536 * owners, priority)
    unused, owner_pick = lax.top_k(priority, chosen)
    available = (positions[:, None] - owner_pick) // owners + 1
    first_index = jax.random.randint(start_key, (NQB, chosen), 0, available)
    first_index = jnp.where(owner_pick == 0, 0, first_index)
    first_index = jnp.where(owner_pick == own_shard[:, None], available - PER_OWNER, first_index)
    block_index = (first_index[:, :, None] + jnp.arange(PER_OWNER)[None, None, :]) % available[:, :, None]
    blocks = owner_pick[:, :, None] + block_index * owners
    return blocks.reshape(NQB, TOPK_BLK).astype(jnp.int32)


def draw_queries(key, part):
    key = jax.random.fold_in(key, 31)
    full_shape = (QTOKENS, HEADS, NOPE + ROPE)
    values = jax.random.normal(key, full_shape, jnp.float32)
    return values.astype(jnp.bfloat16)


def draw_index_query(key, part):
    key = jax.random.fold_in(key, 47)
    full_shape = (QTOKENS, IH, IDX_DIM)
    values = jax.random.normal(key, full_shape, jnp.float32)
    return values.astype(jnp.bfloat16)


def block_levels(own_key, shape, shards, low, top_value):
    def one(axis_at, parts):
        draws = jax.random.uniform(jax.random.fold_in(jax.random.fold_in(own_key, 6), axis_at), (parts,), jnp.float32, low / len(shards), top_value / len(shards))
        return jnp.repeat(jnp.exp(draws), shape[axis_at] // parts).reshape((-1,) + (1,) * (len(shape) - axis_at - 1))

    factor_of = one(*shards[0])
    for cut in shards[1:]:
        factor_of = factor_of * one(*cut)
    return factor_of


def scatter_about(rng, shape, deviation, bound, cuts=(), held_as=jnp.bfloat16):
    array = deviation * jax.random.normal(rng, shape, jnp.float32)
    if cuts:
        array = array * block_levels(rng, shape, cuts, -0.22, 0.18)
    return jnp.clip(array, -bound, bound).astype(held_as)


def setup_inputs(seed: int = 0) -> dict:
    keys = jax.random.split(jax.random.key(seed), 9)
    queries = draw_queries(jax.random.fold_in(keys[8], 71), 0)
    up_weight = scatter_about(keys[1], (HEADS, NOPE, LAT), NOPE ** -0.5, 0.5, ((0, 8),))
    index_query = draw_index_query(jax.random.fold_in(keys[8], 71), 0)
    index_weight = scatter_about(keys[3], (QTOKENS, IH), 0.6, 3.0, ((0, 512),), jnp.float32)
    cache_entry = scatter_about(keys[4], (OWN_BLK, CTX_BLK // OWN_BLK, BLK, LAT + ROPE), 1.0, 6.0, ((1, 64),))
    index_key = scatter_about(keys[5], (OWN_BLK, CTX_BLK // OWN_BLK, BLK, IDX_DIM), 1.0, 6.0, ((1, 64),))
    block_position = draw_block_position(jax.random.fold_in(keys[8], 71), 0)
    picked_blocks = draw_picked_blocks(jax.random.fold_in(keys[8], 71), 0)
    return dict(queries=queries, up_weight=up_weight, index_query=index_query, index_weight=index_weight, cache_entry=cache_entry, index_key=index_key, block_position=block_position, picked_blocks=picked_blocks)


def masked_softmax(values, allowed):
    shifted = jnp.where(allowed, values, -jnp.inf)
    row_max = jnp.max(shifted, axis=-1, keepdims=True)
    expo = jnp.exp(shifted - row_max)
    return expo / jnp.sum(expo, axis=-1, keepdims=True)


def reference(queries, up_weight, index_query, index_weight, cache_entry, index_key, block_position, picked_blocks):
    entry_blocks = cache_entry.reshape(CTX_BLK, BLK, LAT + ROPE)
    key_blocks = index_key.reshape(CTX_BLK, BLK, IDX_DIM)
    query_blocks = queries.reshape(NQB, BLK, HEADS, NOPE + ROPE)
    index_blocks = index_query.reshape(NQB, BLK, IH, IDX_DIM)
    weight_blocks = index_weight.reshape(NQB, BLK, IH)
    up_float = up_weight.astype(jnp.float32)
    score_scale = (NOPE + ROPE) ** -0.5
    index_scale = IDX_DIM ** -0.5

    def query_step(grad_table, pieces):
        query_block, index_block, weight_block, position, pick_row = pieces
        latent = jnp.einsum("thd,hdc->thc", query_block[:, :, :NOPE].astype(jnp.float32), up_float)
        latent = lax.optimization_barrier(latent.astype(jnp.bfloat16))
        query_full = jnp.concatenate([latent, query_block[:, :, NOPE:]], axis=2).astype(jnp.float32)
        block_keys = entry_blocks[pick_row].reshape(KEYS, LAT + ROPE).astype(jnp.float32)
        key_place = (pick_row[:, None] * BLK + jnp.arange(BLK)[None, :]).reshape(KEYS)
        query_place = position * BLK + jnp.arange(BLK)
        allowed = key_place[None, :] <= query_place[:, None]
        logits = jnp.einsum("ihc,sc->his", query_full, block_keys) * score_scale
        probability = masked_softmax(logits, allowed[None])
        target = jnp.sum(probability, axis=0) / HEADS
        index_keys = key_blocks[pick_row].reshape(KEYS, IDX_DIM).astype(jnp.float32)
        index_float = index_block.astype(jnp.float32)
        raw_dot = jnp.einsum("ijd,sd->ijs", index_float, index_keys)
        activated = jnp.maximum(raw_dot, 0.0) * index_scale
        index_score = jnp.sum(weight_block[:, :, None] * activated, axis=1)
        index_soft = masked_softmax(index_score, allowed)
        score_grad = jnp.where(allowed, index_soft - target, 0.0)
        weight_part = jnp.sum(score_grad[:, None, :] * activated, axis=2)
        coefficient = jnp.where(raw_dot > 0, score_grad[:, None, :] * weight_block[:, :, None] * index_scale, 0.0)
        coefficient = lax.optimization_barrier(coefficient.astype(jnp.bfloat16)).astype(jnp.float32)
        key_part = jnp.einsum("ijs,ijd->sd", coefficient, index_float).reshape(TOPK_BLK, BLK, IDX_DIM)
        grad_table = grad_table.at[pick_row].add(key_part)
        return grad_table, weight_part

    zero_grad = jnp.zeros((CTX_BLK, BLK, IDX_DIM), jnp.float32)
    grad_table, weight_parts = lax.scan(query_step, zero_grad, (query_blocks, index_blocks, weight_blocks, block_position, picked_blocks))
    key_grad = grad_table.reshape(OWN_BLK, CTX_BLK // OWN_BLK, BLK, IDX_DIM)
    weight_grad = weight_parts.reshape(QTOKENS, IH)
    return key_grad, weight_grad
```

```python
import functools

import jax
import jax.numpy as jnp
from jax import lax
from jax.experimental import pallas as pl
from jax.experimental.pallas import tpu as pltpu
from jax.sharding import PartitionSpec as P

MESH = pl.DeviceIdType.MESH
X = 4
CORES = 2
LANES = 128


def fetch_kernel(
    zs, ys, tab_ref, own_ref, keys_ref,
    tabs_v, tabs_s, zbuf, xsend, xrecv,
    z_send, z_recv, x_send, x_recv, t_send, t_recv, y_send, y_recv, local_sem,
):
    ctx = lax.axis_index("ctx")
    head = lax.axis_index("head")
    z, x = ctx // X, ctx % X
    y, c = head // CORES, head % CORES
    own_blocks, rows, half = own_ref.shape
    z_up = (lax.rem(z + 1, zs) * X + x, head)
    z_down = (lax.rem(z + zs - 1, zs) * X + x, head)
    step = 1 - 2 * c
    y_a = lax.rem(y + step + ys, ys)
    y_b = lax.rem(y - step + ys, ys)
    x_peers = []
    for dx in range(X):
        for dc in range(CORES):
            if dx or dc:
                tx, tc = lax.rem(x + dx, X), lax.rem(c + dc, CORES)
                x_peers.append((dx, dc, tx, tc, (z * X + tx, y * CORES + tc)))

    barrier = pltpu.get_barrier_semaphore()
    peers = [z_up, z_down, (ctx, y_a * CORES + c), (ctx, y_b * CORES + c)] + [p[4] for p in x_peers]
    for peer in peers:
        pl.semaphore_signal(barrier, inc=1, device_id=peer, device_id_type=MESH)
    zbuf[z] = own_ref[...]
    tabs_v[x] = tab_ref[...]
    pl.semaphore_wait(barrier, len(peers))

    def send(src, dst, s_sem, r_sem, device):
        copy = pltpu.make_async_remote_copy(
            src_ref=src, dst_ref=dst, send_sem=s_sem, recv_sem=r_sem, device_id=device, device_id_type=MESH
        )
        return copy

    steps = zs // 2
    part = own_blocks // 2
    sent = []

    def z_piece(direction, k, i):
        owner = lax.rem(z + (zs - k if direction == 0 else k), zs)
        piece = zbuf.at[owner, pl.ds(i * part, part)]
        return send(
            piece, piece, z_send.at[direction, k, i], z_recv.at[direction, k, i],
            z_up if direction == 0 else z_down,
        )

    def z_arrived(direction, k, i):
        owner = lax.rem(z + (zs - k - 1 if direction == 0 else k + 1), zs)
        piece = zbuf.at[owner, pl.ds(i * part, part)]
        send(piece, piece, z_send.at[direction, k, i], z_recv.at[direction, k, i], z_up).wait_recv()

    tab_copies = []
    for k in range(steps):
        for i in range(2):
            for direction in range(2):
                if k == steps - 1 and i != direction:
                    continue
                if k > 0:
                    z_arrived(direction, k - 1, i)
                copy = z_piece(direction, k, i)
                copy.start()
                sent.append(copy)
        if k == 0:
            for dx in range(1, X):
                tx = lax.rem(x + dx, X)
                copy = send(tabs_v.at[x], tabs_v.at[x], t_send.at[dx - 1], t_recv.at[dx - 1], (z * X + tx, head))
                copy.start()
                tab_copies.append(copy)
    for dx in range(1, X):
        fx = lax.rem(x + X - dx, X)
        send(tabs_v.at[fx], tabs_v.at[fx], t_send.at[dx - 1], t_recv.at[dx - 1], z_up).wait_recv()
    to_scalar = pltpu.make_async_copy(tabs_v, tabs_s, local_sem)
    to_scalar.start()
    to_scalar.wait()
    z_arrived(0, steps - 2, 1)
    z_arrived(1, steps - 2, 0)
    z_arrived(0, steps - 1, 0)
    z_arrived(1, steps - 1, 1)

    def choose(tx, tc, dst):
        def body(owner, carry):
            pick = tabs_s[tx, tc, owner * X + x]
            dst[owner] = zbuf[owner, pick]
            return carry

        lax.fori_loop(0, zs, body, 0)

    x_copies = []
    for n, (dx, dc, tx, tc, device) in enumerate(x_peers):
        choose(tx, tc, xsend.at[n])
        copy = send(xsend.at[n], xrecv.at[x, c], x_send.at[n], x_recv.at[n], device)
        copy.start()
        x_copies.append(copy)
    choose(x, c, xrecv.at[x, c])
    for n, (dx, dc, tx, tc, device) in enumerate(x_peers):
        fx, fc = lax.rem(x + X - dx, X), lax.rem(c + dc, CORES)
        send(xsend.at[n], xrecv.at[fx, fc], x_send.at[n], x_recv.at[n], device).wait_recv()

    picks = keys_ref.shape[0]
    chunks = y_send.shape[1]
    chunk = picks // chunks

    def place(m, carry):
        owner = tabs_s[x, CORES + c, m]
        for fc in range(CORES):
            keys_ref[m, pl.ds(pl.multiple_of(y * rows, rows), rows), fc * half : (fc + 1) * half] = xrecv[
                lax.rem(owner, X), fc, lax.div(owner, X)
            ]
        return carry

    def quarter(owner, j):
        return keys_ref.at[pl.ds(j * chunk, chunk), pl.ds(pl.multiple_of(owner * rows, rows), rows)]

    y_far = lax.rem(y + 2, ys)
    y_copies = []

    def y_send_quarter(kind, owner, j, device):
        ref = quarter(owner, j)
        copy = send(ref, ref, y_send.at[kind, j], y_recv.at[kind, j], device)
        copy.start()
        y_copies.append(copy)

    def y_arrived(kind, owner, j):
        ref = quarter(owner, j)
        send(ref, ref, y_send.at[kind, j], y_recv.at[kind, j], (ctx, y_a * CORES + c)).wait_recv()

    for j in range(chunks):
        lax.fori_loop(j * chunk, (j + 1) * chunk, place, 0)
        y_send_quarter(0, y, j, (ctx, y_a * CORES + c))
        y_send_quarter(1, y, j, (ctx, y_b * CORES + c))
    for j in range(chunks):
        y_arrived(0, y_b, j)
        y_send_quarter(2, y_b, j, (ctx, y_a * CORES + c))
    for j in range(chunks):
        y_arrived(1, y_a, j)
        y_arrived(2, y_far, j)
    for copy in sent + tab_copies + x_copies + y_copies:
        copy.wait_send()


def fetch(table, own, zs, ys, picks, block_len):
    own_blocks, rows, half = own.shape
    steps = zs // 2
    peers = X * CORES - 1
    chunks = 4
    return pl.pallas_call(
        functools.partial(fetch_kernel, zs, ys),
        out_shape=jax.ShapeDtypeStruct((picks, block_len, half * CORES), own.dtype),
        in_specs=[pl.BlockSpec(memory_space=pltpu.VMEM)] * 2,
        out_specs=pl.BlockSpec(memory_space=pltpu.VMEM),
        scratch_shapes=[
            pltpu.VMEM((X, 8, LANES), jnp.int32),
            pltpu.SMEM((X, 8, LANES), jnp.int32),
            pltpu.VMEM((zs, own_blocks, rows, half), own.dtype),
            pltpu.VMEM((peers, zs, rows, half), own.dtype),
            pltpu.VMEM((X, CORES, zs, rows, half), own.dtype),
            pltpu.SemaphoreType.DMA((2, steps, 2)),
            pltpu.SemaphoreType.DMA((2, steps, 2)),
            pltpu.SemaphoreType.DMA((peers,)),
            pltpu.SemaphoreType.DMA((peers,)),
            pltpu.SemaphoreType.DMA((X - 1,)),
            pltpu.SemaphoreType.DMA((X - 1,)),
            pltpu.SemaphoreType.DMA((3, chunks)),
            pltpu.SemaphoreType.DMA((3, chunks)),
            pltpu.SemaphoreType.DMA,
        ],
        compiler_params=pltpu.CompilerParams(
            collective_id=0, has_side_effects=True, vmem_limit_bytes=40 * 2**20
        ),
        name="fetch_keys",
    )(table, own)


def attend_kernel(width, scale, q_ref, k_ref, bias_ref, out_ref, logits):
    group, tokens, unused = q_ref.shape
    step = pl.program_id(0)
    keys = k_ref[:, :width]
    queries = q_ref[...].reshape(group * tokens, width)
    logits[...] = lax.dot_general(
        queries, keys, (((1,), (1,)), ((), ())), preferred_element_type=jnp.float32
    )

    @pl.when(step == 0)
    def first():
        out_ref[...] = jnp.zeros_like(out_ref)

    def tile(i, carry):
        at = pl.multiple_of(i * 8, 8)
        bias = bias_ref[pl.ds(at, 8), :]
        total = out_ref[pl.ds(at, 8), :]
        for g in range(group):
            value = logits[pl.ds(pl.multiple_of(g * tokens + i * 8, 8), 8), :] * scale + bias
            expo = jnp.exp2(value - jnp.max(value, axis=1, keepdims=True))
            total = total + expo * (1.0 / jnp.sum(expo, axis=1, keepdims=True))
        out_ref[pl.ds(at, 8), :] = total
        return carry

    lax.fori_loop(0, tokens // 8, tile, 0)


def attend(query, keys, bias, width, scale):
    heads, tokens, unused = query.shape
    key_count, key_width = keys.shape
    group = 4
    return pl.pallas_call(
        functools.partial(attend_kernel, width, scale),
        grid=(heads // group,),
        out_shape=jax.ShapeDtypeStruct((tokens, key_count), jnp.float32),
        in_specs=[
            pl.BlockSpec((group, tokens, width), lambda i: (i, 0, 0)),
            pl.BlockSpec((key_count, key_width), lambda i: (0, 0)),
            pl.BlockSpec((tokens, key_count), lambda i: (0, 0)),
        ],
        out_specs=pl.BlockSpec((tokens, key_count), lambda i: (0, 0)),
        scratch_shapes=[pltpu.VMEM((group * tokens, key_count), jnp.float32)],
        compiler_params=pltpu.CompilerParams(vmem_limit_bytes=40 * 2**20),
        name="attend",
    )(query, keys, bias)


def masked_softmax(values, allowed):
    shifted = jnp.where(allowed, values, -jnp.inf)
    row_max = jnp.max(shifted, axis=-1, keepdims=True)
    expo = jnp.exp(shifted - row_max)
    return expo / jnp.sum(expo, axis=-1, keepdims=True)


def local(
    queries,
    up_weight,
    index_query,
    index_weight,
    cache_entry,
    index_key,
    block_position,
    picked_blocks,
):
    owners = lax.axis_size("ctx")
    head_devices = lax.axis_size("head")
    zs, ys = owners // X, head_devices // CORES
    ctx = lax.axis_index("ctx")
    head = lax.axis_index("head")
    y, c = head // CORES, head % CORES
    query_count, picks = picked_blocks.shape
    own_blocks, unused, block_len, entry_width = cache_entry.shape
    index_width = index_key.shape[3]
    key_count = picks * block_len
    rows = block_len // ys
    local_heads = queries.shape[1]
    nope = up_weight.shape[1]
    latent = up_weight.shape[2]
    pad_width = -(-entry_width // LANES) * LANES
    full_width = pad_width + index_width
    half = full_width // CORES

    owner_of = picked_blocks % owners
    matched = owner_of[:, :, None] == jnp.arange(owners)[None, None, :]
    request = jnp.sum(jnp.where(matched, picked_blocks[:, :, None] // owners + 1, 0), axis=1)
    table = jnp.zeros((8, LANES), jnp.int32)
    table = table.at[:query_count, :owners].set(jnp.maximum(request - 1, 0))
    table = table.at[query_count : 2 * query_count, :picks].set(owner_of)

    own = jnp.concatenate(
        [
            lax.dynamic_slice_in_dim(cache_entry[:, 0], y * rows, rows, 1),
            jnp.zeros((own_blocks, rows, pad_width - entry_width), cache_entry.dtype),
            lax.dynamic_slice_in_dim(index_key[:, 0], y * rows, rows, 1),
        ],
        axis=2,
    )
    own = lax.dynamic_slice_in_dim(own, c * half, half, 2)

    swap = [(i, i ^ 1) for i in range(head_devices)]
    to_row = [((i % CORES) * ys + i // CORES, i) for i in range(head_devices)]
    my_index_query = lax.ppermute(index_query, "head", to_row)
    my_index_weight = lax.ppermute(index_weight, "head", to_row)
    lat = jnp.einsum(
        "thd,hdc->htc", queries[:, :, :nope], up_weight, preferred_element_type=jnp.float32
    ).astype(jnp.bfloat16)
    rope = jnp.transpose(queries[:, :, nope:], (1, 0, 2))
    query_full = jnp.concatenate(
        [lat, rope, jnp.zeros(rope.shape[:2] + (pad_width - entry_width,), rope.dtype)], axis=2
    )
    mine = lax.dynamic_slice_in_dim(query_full, c * block_len, block_len, 1)
    other = lax.dynamic_slice_in_dim(query_full, (1 - c) * block_len, block_len, 1)
    query_row = jnp.concatenate([mine, lax.ppermute(other, "head", swap)], axis=0)

    keys = fetch(table, own, zs, ys, picks, block_len).reshape(key_count, full_width)

    my_picks = lax.dynamic_index_in_dim(picked_blocks, c, 0, keepdims=False)
    my_owner = lax.dynamic_index_in_dim(owner_of, c, 0, keepdims=False)
    my_position = lax.dynamic_index_in_dim(block_position, c, 0, keepdims=False)
    key_place = (my_picks[:, None] * block_len + jnp.arange(block_len)[None, :]).reshape(key_count)
    query_place = my_position * block_len + jnp.arange(block_len)
    allowed = key_place[None, :] <= query_place[:, None]
    bias = jnp.where(allowed, 0.0, -jnp.inf).astype(jnp.float32)
    scale = queries.shape[2] ** (-0.5) * 1.4426950408889634
    prob_sum = attend(query_row, keys, bias, pad_width, scale)

    y_groups = [[k * CORES + j for k in range(ys)] for j in range(CORES)]
    core_groups = [[k * CORES + j for j in range(CORES)] for k in range(ys)]
    target = lax.psum_scatter(
        prob_sum, "head", scatter_dimension=0, axis_index_groups=y_groups, tiled=True
    ) / (local_heads * head_devices)

    index_keys = keys[:, pad_width:]
    my_allowed = lax.dynamic_slice_in_dim(allowed, y * rows, rows, 0)
    index_scale = index_width ** (-0.5)
    raw = jnp.einsum("ijd,sd->ijs", my_index_query, index_keys, preferred_element_type=jnp.float32)
    act = jnp.maximum(raw, 0.0) * index_scale
    score = jnp.sum(my_index_weight[:, :, None] * act, axis=1)
    soft = masked_softmax(score, my_allowed)
    score_grad = jnp.where(my_allowed, soft - target, 0.0)
    weight_part = jnp.sum(score_grad[:, None, :] * act, axis=2)
    coefficient = jnp.where(
        raw > 0, score_grad[:, None, :] * my_index_weight[:, :, None] * index_scale, 0.0
    ).astype(jnp.bfloat16)
    key_part = jnp.einsum(
        "ijs,ijd->sd", coefficient, my_index_query, preferred_element_type=jnp.float32
    )
    weight_grad = lax.ppermute(weight_part, "head", [(b, a) for a, b in to_row])

    quarter = lax.psum_scatter(
        key_part.reshape(picks, ys, rows * index_width),
        "head", scatter_dimension=1, axis_index_groups=y_groups, tiled=True,
    ).reshape(picks, rows * index_width)
    one_hot = (my_owner[None, :] == jnp.arange(owners)[:, None]).astype(jnp.float32)
    outgoing = jnp.einsum("om,mf->of", one_hot, quarter, precision=lax.Precision.HIGHEST)
    arrived = lax.all_to_all(outgoing, "ctx", split_axis=0, concat_axis=0, tiled=True)
    all_requests = lax.all_gather(request, "ctx")
    theirs = lax.dynamic_index_in_dim(all_requests, c, 1, keepdims=False)
    theirs = lax.dynamic_index_in_dim(theirs, ctx, 1, keepdims=False) - 1
    block_hot = (theirs[None, :] == jnp.arange(own_blocks)[:, None]).astype(jnp.float32)
    summed = jnp.einsum("rn,nf->rf", block_hot, arrived, precision=lax.Precision.HIGHEST)
    summed = lax.psum(summed, "head", axis_index_groups=core_groups)
    gathered = lax.all_gather(summed, "head", axis_index_groups=y_groups)
    key_grad = jnp.transpose(
        gathered.reshape(ys, own_blocks, rows, index_width), (1, 0, 2, 3)
    ).reshape(own_blocks, 1, block_len, index_width)
    return (key_grad, weight_grad)


def solution(mesh):
    return jax.shard_map(
        local,
        mesh=mesh,
        in_specs=(
            P("ctx", "head", None),
            P("head", None, None),
            P(("ctx", "head"), None, None),
            P(("ctx", "head"), None),
            P(None, "ctx", None, None),
            P(None, "ctx", None, None),
            P("ctx"),
            P("ctx", None),
        ),
        out_specs=(P(None, "ctx", None, None), P(("ctx", "head"), None)),
        check_vma=False,
    )
```

```python
import functools

import jax
import jax.numpy as jnp
from jax import lax
from jax.experimental import pallas as pl
from jax.experimental.pallas import tpu as pltpu
from jax.sharding import PartitionSpec as P

MESH = pl.DeviceIdType.MESH
X = 4
CORES = 2
LANES = 128


def fetch_kernel(
    zs, ys, tab_ref, own_ref, keys_ref, tabs_ref,
    tabs_v, tabs_s, zbuf, xsend, xrecv,
    z_send, z_recv, x_send, x_recv, t_send, t_recv, y_send, y_recv, local_sem,
):
    ctx = lax.axis_index("ctx")
    head = lax.axis_index("head")
    z, x = ctx // X, ctx % X
    y, c = head // CORES, head % CORES
    own_blocks, rows, half = own_ref.shape
    z_up = (lax.rem(z + 1, zs) * X + x, head)
    z_down = (lax.rem(z + zs - 1, zs) * X + x, head)
    step = 1 - 2 * c
    y_a = lax.rem(y + step + ys, ys)
    y_b = lax.rem(y - step + ys, ys)
    x_peers = []
    for dx in range(X):
        for dc in range(CORES):
            if dx or dc:
                tx, tc = lax.rem(x + dx, X), lax.rem(c + dc, CORES)
                x_peers.append((dx, dc, tx, tc, (z * X + tx, y * CORES + tc)))

    barrier = pltpu.get_barrier_semaphore()
    peers = [z_up, z_down, (ctx, y_a * CORES + c), (ctx, y_b * CORES + c)] + [p[4] for p in x_peers]
    for peer in peers:
        pl.semaphore_signal(barrier, inc=1, device_id=peer, device_id_type=MESH)
    zbuf[z] = own_ref[...]
    tabs_v[x] = tab_ref[...]
    pl.semaphore_wait(barrier, len(peers))

    def send(src, dst, s_sem, r_sem, device):
        copy = pltpu.make_async_remote_copy(
            src_ref=src, dst_ref=dst, send_sem=s_sem, recv_sem=r_sem, device_id=device, device_id_type=MESH
        )
        return copy

    steps = zs // 2
    part = own_blocks // 2
    sent = []

    def z_piece(direction, k, i):
        owner = lax.rem(z + (zs - k if direction == 0 else k), zs)
        piece = zbuf.at[owner, pl.ds(i * part, part)]
        return send(
            piece, piece, z_send.at[direction, k, i], z_recv.at[direction, k, i],
            z_up if direction == 0 else z_down,
        )

    def z_arrived(direction, k, i):
        owner = lax.rem(z + (zs - k - 1 if direction == 0 else k + 1), zs)
        piece = zbuf.at[owner, pl.ds(i * part, part)]
        send(piece, piece, z_send.at[direction, k, i], z_recv.at[direction, k, i], z_up).wait_recv()

    tab_copies = []
    for k in range(steps):
        for i in range(2):
            for direction in range(2):
                if k == steps - 1 and i != direction:
                    continue
                if k > 0:
                    z_arrived(direction, k - 1, i)
                copy = z_piece(direction, k, i)
                copy.start()
                sent.append(copy)
        if k == 0:
            for dx in range(1, X):
                tx = lax.rem(x + dx, X)
                copy = send(tabs_v.at[x], tabs_v.at[x], t_send.at[dx - 1], t_recv.at[dx - 1], (z * X + tx, head))
                copy.start()
                tab_copies.append(copy)
    for dx in range(1, X):
        fx = lax.rem(x + X - dx, X)
        send(tabs_v.at[fx], tabs_v.at[fx], t_send.at[dx - 1], t_recv.at[dx - 1], z_up).wait_recv()
    to_scalar = pltpu.make_async_copy(tabs_v, tabs_s, local_sem)
    to_scalar.start()
    to_scalar.wait()
    tabs_ref[...] = tabs_v[...]
    z_arrived(0, steps - 2, 1)
    z_arrived(1, steps - 2, 0)
    z_arrived(0, steps - 1, 0)
    z_arrived(1, steps - 1, 1)

    def choose(tx, tc, dst):
        def body(owner, carry):
            pick = tabs_s[tx, tc, owner * X + x]
            dst[owner] = zbuf[owner, pick]
            return carry

        lax.fori_loop(0, zs, body, 0)

    x_copies = []
    for n, (dx, dc, tx, tc, device) in enumerate(x_peers):
        choose(tx, tc, xsend.at[n])
        copy = send(xsend.at[n], xrecv.at[x, c], x_send.at[n], x_recv.at[n], device)
        copy.start()
        x_copies.append(copy)
    choose(x, c, xrecv.at[x, c])
    for n, (dx, dc, tx, tc, device) in enumerate(x_peers):
        fx, fc = lax.rem(x + X - dx, X), lax.rem(c + dc, CORES)
        send(xsend.at[n], xrecv.at[fx, fc], x_send.at[n], x_recv.at[n], device).wait_recv()

    picks = keys_ref.shape[0]
    chunks = y_send.shape[1]
    chunk = picks // chunks

    def place(m, carry):
        owner = tabs_s[x, CORES + c, m]
        for fc in range(CORES):
            keys_ref[m, pl.ds(pl.multiple_of(y * rows, rows), rows), fc * half : (fc + 1) * half] = xrecv[
                lax.rem(owner, X), fc, lax.div(owner, X)
            ]
        return carry

    def quarter(owner, j):
        return keys_ref.at[pl.ds(j * chunk, chunk), pl.ds(pl.multiple_of(owner * rows, rows), rows)]

    y_far = lax.rem(y + 2, ys)
    y_copies = []

    def y_send_quarter(kind, owner, j, device):
        ref = quarter(owner, j)
        copy = send(ref, ref, y_send.at[kind, j], y_recv.at[kind, j], device)
        copy.start()
        y_copies.append(copy)

    def y_arrived(kind, owner, j):
        ref = quarter(owner, j)
        send(ref, ref, y_send.at[kind, j], y_recv.at[kind, j], (ctx, y_a * CORES + c)).wait_recv()

    for j in range(chunks):
        lax.fori_loop(j * chunk, (j + 1) * chunk, place, 0)
        y_send_quarter(0, y, j, (ctx, y_a * CORES + c))
        y_send_quarter(1, y, j, (ctx, y_b * CORES + c))
    for j in range(chunks):
        y_arrived(0, y_b, j)
        y_send_quarter(2, y_b, j, (ctx, y_a * CORES + c))
    for j in range(chunks):
        y_arrived(1, y_a, j)
        y_arrived(2, y_far, j)
    for copy in sent + tab_copies + x_copies + y_copies:
        copy.wait_send()


def fetch(table, own, zs, ys, picks, block_len):
    own_blocks, rows, half = own.shape
    steps = zs // 2
    peers = X * CORES - 1
    chunks = 4
    return pl.pallas_call(
        functools.partial(fetch_kernel, zs, ys),
        out_shape=(
            jax.ShapeDtypeStruct((picks, block_len, half * CORES), own.dtype),
            jax.ShapeDtypeStruct((X, 8, LANES), jnp.int32),
        ),
        in_specs=[pl.BlockSpec(memory_space=pltpu.VMEM)] * 2,
        out_specs=[pl.BlockSpec(memory_space=pltpu.VMEM)] * 2,
        scratch_shapes=[
            pltpu.VMEM((X, 8, LANES), jnp.int32),
            pltpu.SMEM((X, 8, LANES), jnp.int32),
            pltpu.VMEM((zs, own_blocks, rows, half), own.dtype),
            pltpu.VMEM((peers, zs, rows, half), own.dtype),
            pltpu.VMEM((X, CORES, zs, rows, half), own.dtype),
            pltpu.SemaphoreType.DMA((2, steps, 2)),
            pltpu.SemaphoreType.DMA((2, steps, 2)),
            pltpu.SemaphoreType.DMA((peers,)),
            pltpu.SemaphoreType.DMA((peers,)),
            pltpu.SemaphoreType.DMA((X - 1,)),
            pltpu.SemaphoreType.DMA((X - 1,)),
            pltpu.SemaphoreType.DMA((3, chunks)),
            pltpu.SemaphoreType.DMA((3, chunks)),
            pltpu.SemaphoreType.DMA,
        ],
        compiler_params=pltpu.CompilerParams(
            collective_id=0, has_side_effects=True, vmem_limit_bytes=40 * 2**20
        ),
        name="fetch_keys",
    )(table, own)


def attend_kernel(width, scale, q_ref, k_ref, bias_ref, out_ref, logits):
    group, tokens, unused = q_ref.shape
    step = pl.program_id(0)
    keys = k_ref[:, :width]
    queries = q_ref[...].reshape(group * tokens, width)
    logits[...] = lax.dot_general(
        queries, keys, (((1,), (1,)), ((), ())), preferred_element_type=jnp.float32
    )

    @pl.when(step == 0)
    def first():
        out_ref[...] = jnp.zeros_like(out_ref)

    def tile(i, carry):
        at = pl.multiple_of(i * 8, 8)
        bias = bias_ref[pl.ds(at, 8), :]
        total = out_ref[pl.ds(at, 8), :]
        for g in range(group):
            value = logits[pl.ds(pl.multiple_of(g * tokens + i * 8, 8), 8), :] * scale + bias
            expo = jnp.exp2(value - jnp.max(value, axis=1, keepdims=True))
            total = total + expo * (1.0 / jnp.sum(expo, axis=1, keepdims=True))
        out_ref[pl.ds(at, 8), :] = total
        return carry

    lax.fori_loop(0, tokens // 8, tile, 0)


def attend(query, keys, bias, width, scale):
    heads, tokens, unused = query.shape
    key_count, key_width = keys.shape
    group = 4
    return pl.pallas_call(
        functools.partial(attend_kernel, width, scale),
        grid=(heads // group,),
        out_shape=jax.ShapeDtypeStruct((tokens, key_count), jnp.float32),
        in_specs=[
            pl.BlockSpec((group, tokens, width), lambda i: (i, 0, 0)),
            pl.BlockSpec((key_count, key_width), lambda i: (0, 0)),
            pl.BlockSpec((tokens, key_count), lambda i: (0, 0)),
        ],
        out_specs=pl.BlockSpec((tokens, key_count), lambda i: (0, 0)),
        scratch_shapes=[pltpu.VMEM((group * tokens, key_count), jnp.float32)],
        compiler_params=pltpu.CompilerParams(vmem_limit_bytes=40 * 2**20),
        name="attend",
    )(query, keys, bias)


def remote(src, dst, s_sem, r_sem, device):
    return pltpu.make_async_remote_copy(
        src_ref=src, dst_ref=dst, send_sem=s_sem, recv_sem=r_sem, device_id=device, device_id_type=MESH
    )


def enter(peers):
    barrier = pltpu.get_barrier_semaphore()
    for peer in peers:
        pl.semaphore_signal(barrier, inc=1, device_id=peer, device_id_type=MESH)
    pl.semaphore_wait(barrier, len(peers))


def y_sides(ys):
    head = lax.axis_index("head")
    y, c = head // CORES, head % CORES
    step = 1 - 2 * c
    return y, c, lax.rem(y + step + ys, ys), lax.rem(y - step + ys, ys), lax.rem(y + 2, ys)


def target_kernel(ys, prob_ref, out_ref, arrived, middle, s_sem, r_sem):
    ctx = lax.axis_index("ctx")
    y, c, y_a, y_b, y_far = y_sides(ys)
    rows = out_ref.shape[0]
    to_a, to_b = (ctx, y_a * CORES + c), (ctx, y_b * CORES + c)
    enter([to_a, to_b])

    def quarter(k):
        return prob_ref.at[pl.ds(pl.multiple_of(k * rows, rows), rows)]

    far = remote(quarter(y_far), arrived.at[0], s_sem.at[0], r_sem.at[0], to_a)
    near = remote(quarter(y_b), arrived.at[1], s_sem.at[1], r_sem.at[1], to_b)
    far.start()
    near.start()
    far.wait_recv()
    middle[...] = quarter(y_a)[...] + arrived[0]
    last = remote(middle, arrived.at[2], s_sem.at[2], r_sem.at[2], to_a)
    last.start()
    near.wait_recv()
    last.wait_recv()
    out_ref[...] = quarter(y)[...] + arrived[1] + arrived[2]
    for copy in (far, near, last):
        copy.wait_send()


def sum_target(prob_sum, ys):
    tokens, key_count = prob_sum.shape
    rows = tokens // ys
    return pl.pallas_call(
        functools.partial(target_kernel, ys),
        out_shape=jax.ShapeDtypeStruct((rows, key_count), jnp.float32),
        in_specs=[pl.BlockSpec(memory_space=pltpu.VMEM)],
        out_specs=pl.BlockSpec(memory_space=pltpu.VMEM),
        scratch_shapes=[
            pltpu.VMEM((3, rows, key_count), jnp.float32),
            pltpu.VMEM((rows, key_count), jnp.float32),
            pltpu.SemaphoreType.DMA((3,)),
            pltpu.SemaphoreType.DMA((3,)),
        ],
        compiler_params=pltpu.CompilerParams(
            collective_id=1, has_side_effects=True, vmem_limit_bytes=40 * 2**20
        ),
        name="sum_target",
    )(prob_sum)


def return_kernel(
    zs, ys, tabs_ref, part_ref, out_ref,
    y_out, y_in, quarter, x_out, x_in, z_out, z_in, mine, theirs,
    ys_sem, yr_sem, xs_sem, xr_sem, zs_sem, zr_sem, cs_sem, cr_sem, os_sem, or_sem,
):
    ctx = lax.axis_index("ctx")
    z, x = ctx // X, ctx % X
    y, c, y_a, y_b, y_far = y_sides(ys)
    head = y * CORES + c
    picks, block_len, width = part_ref.shape
    own_blocks = out_ref.shape[0]
    rows = block_len // ys
    slots = X * rows
    to_a, to_b, to_far = (ctx, y_a * CORES + c), (ctx, y_b * CORES + c), (ctx, y_far * CORES + c)
    to_core = (ctx, y * CORES + 1 - c)
    x_peers = [(lax.rem(x + d, X), (z * X + lax.rem(x + d, X), head)) for d in range(1, X)]
    z_peers = [(lax.rem(z + d, zs), (lax.rem(z + d, zs) * X + x, head)) for d in range(1, zs)]
    enter([to_a, to_b, to_far, to_core] + [p[1] for p in x_peers] + [p[1] for p in z_peers])

    def span(k):
        return pl.ds(pl.multiple_of(k * rows, rows), rows)

    y_out[0] = part_ref[:, span(y_far), :].astype(y_out.dtype)
    far = remote(y_out.at[0], y_in.at[0], ys_sem.at[0], yr_sem.at[0], to_a)
    far.start()
    y_out[1] = part_ref[:, span(y_b), :].astype(y_out.dtype)
    near = remote(y_out.at[1], y_in.at[1], ys_sem.at[1], yr_sem.at[1], to_b)
    near.start()
    far.wait_recv()
    y_out[2] = (part_ref[:, span(y_a), :] + y_in[0].astype(jnp.float32)).astype(y_out.dtype)
    last = remote(y_out.at[2], y_in.at[2], ys_sem.at[2], yr_sem.at[2], to_a)
    last.start()
    near.wait_recv()
    last.wait_recv()
    quarter[...] = (
        part_ref[:, span(y), :] + y_in[1].astype(jnp.float32) + y_in[2].astype(jnp.float32)
    )

    def choose(tx, dst):
        def body(owner, carry):
            place = tabs_ref[x, 3 * CORES + c, owner * X + tx]
            value = quarter[jnp.maximum(place - 1, 0)]
            dst[owner] = jnp.where(place > 0, value, 0.0).astype(dst.dtype)
            return carry

        lax.fori_loop(0, zs, body, 0)

    x_copies = []
    for n, (tx, device) in enumerate(x_peers):
        choose(tx, x_out.at[n])
        copy = remote(x_out.at[n], x_in.at[x], xs_sem.at[n], xr_sem.at[n], device)
        copy.start()
        x_copies.append(copy)
    choose(x, x_in.at[x])
    for n in range(X - 1):
        fx = lax.rem(x + X - n - 1, X)
        remote(x_out.at[n], x_in.at[fx], xs_sem.at[n], xr_sem.at[n], to_a).wait_recv()

    line = lax.broadcasted_iota(jnp.int32, (rows, width), 0)

    def gather(owner, dst):
        ids = jnp.zeros((rows, width), jnp.float32)
        for fx in range(X):
            dst[fx * rows : (fx + 1) * rows] = x_in[fx, owner]
            block = tabs_ref[fx, 2 * CORES + c, owner * X + x]
            ids = jnp.where(line == fx, block.astype(jnp.float32), ids)
        dst[slots : slots + rows] = ids.astype(dst.dtype)

    z_copies = []
    order = sorted(range(1, zs), key=lambda d: -min(d, zs - d))
    for d in order:
        tz, device = z_peers[d - 1]
        gather(tz, z_out.at[d - 1])
        copy = remote(z_out.at[d - 1], z_in.at[z], zs_sem.at[d - 1], zr_sem.at[d - 1], device)
        copy.start()
        z_copies.append(copy)
    gather(z, z_in.at[z])
    for d in order:
        fz = lax.rem(z + zs - d, zs)
        remote(z_out.at[d - 1], z_in.at[fz], zs_sem.at[d - 1], zr_sem.at[d - 1], to_a).wait_recv()

    def add(fz, totals):
        ids = z_in[fz, slots : slots + rows].astype(jnp.float32)
        totals = list(totals)
        for fx in range(X):
            value = z_in[fz, fx * rows : (fx + 1) * rows].astype(jnp.float32)
            block = jnp.broadcast_to(ids[fx : fx + 1], value.shape)
            for r in range(own_blocks):
                totals[r] = totals[r] + jnp.where(block == r + 1.0, value, 0.0)
        return tuple(totals)

    totals = lax.fori_loop(
        0, zs, add, tuple(jnp.zeros((rows, width), jnp.float32) for r in range(own_blocks))
    )
    for r in range(own_blocks):
        mine[r] = totals[r]
    core = remote(mine, theirs, cs_sem, cr_sem, to_core)
    core.start()
    core.wait_recv()
    out_ref[:, span(y), :] = mine[...] + theirs[...]
    o_copies = []
    for n, device in enumerate((to_a, to_b, to_far)):
        ref = out_ref.at[:, span(y), :]
        copy = remote(ref, ref, os_sem.at[n], or_sem.at[n], device)
        copy.start()
        o_copies.append(copy)
    for n, fy in enumerate((y_b, y_a, y_far)):
        ref = out_ref.at[:, span(fy), :]
        remote(ref, ref, os_sem.at[n], or_sem.at[n], to_a).wait_recv()
    for copy in [far, near, last, core] + x_copies + z_copies + o_copies:
        copy.wait_send()


def give_back(tables, key_part, zs, ys, own_blocks):
    picks, block_len, width = key_part.shape
    rows = block_len // ys
    half = jnp.bfloat16
    dma = pltpu.SemaphoreType.DMA
    return pl.pallas_call(
        functools.partial(return_kernel, zs, ys),
        out_shape=jax.ShapeDtypeStruct((own_blocks, block_len, width), jnp.float32),
        in_specs=[
            pl.BlockSpec(memory_space=pltpu.SMEM),
            pl.BlockSpec(memory_space=pltpu.VMEM),
        ],
        out_specs=pl.BlockSpec(memory_space=pltpu.VMEM),
        scratch_shapes=[
            pltpu.VMEM((3, picks, rows, width), half),
            pltpu.VMEM((3, picks, rows, width), half),
            pltpu.VMEM((picks, rows, width), jnp.float32),
            pltpu.VMEM((X - 1, zs, rows, width), half),
            pltpu.VMEM((X, zs, rows, width), half),
            pltpu.VMEM((zs - 1, (X + 1) * rows, width), half),
            pltpu.VMEM((zs, (X + 1) * rows, width), half),
            pltpu.VMEM((own_blocks, rows, width), jnp.float32),
            pltpu.VMEM((own_blocks, rows, width), jnp.float32),
            dma((3,)), dma((3,)), dma((X - 1,)), dma((X - 1,)), dma((zs - 1,)), dma((zs - 1,)),
            dma, dma, dma((3,)), dma((3,)),
        ],
        compiler_params=pltpu.CompilerParams(
            collective_id=2, has_side_effects=True, vmem_limit_bytes=40 * 2**20
        ),
        name="give_back",
    )(tables, key_part)


def masked_softmax(values, allowed):
    shifted = jnp.where(allowed, values, -jnp.inf)
    row_max = jnp.max(shifted, axis=-1, keepdims=True)
    expo = jnp.exp(shifted - row_max)
    return expo / jnp.sum(expo, axis=-1, keepdims=True)


def local(
    queries,
    up_weight,
    index_query,
    index_weight,
    cache_entry,
    index_key,
    block_position,
    picked_blocks,
):
    owners = lax.axis_size("ctx")
    head_devices = lax.axis_size("head")
    zs, ys = owners // X, head_devices // CORES
    ctx = lax.axis_index("ctx")
    head = lax.axis_index("head")
    y, c = head // CORES, head % CORES
    query_count, picks = picked_blocks.shape
    own_blocks, unused, block_len, entry_width = cache_entry.shape
    index_width = index_key.shape[3]
    key_count = picks * block_len
    rows = block_len // ys
    local_heads = queries.shape[1]
    nope = up_weight.shape[1]
    latent = up_weight.shape[2]
    pad_width = -(-entry_width // LANES) * LANES
    full_width = pad_width + index_width
    half = full_width // CORES

    owner_of = picked_blocks % owners
    matched = owner_of[:, :, None] == jnp.arange(owners)[None, None, :]
    request = jnp.sum(jnp.where(matched, picked_blocks[:, :, None] // owners + 1, 0), axis=1)
    table = jnp.zeros((8, LANES), jnp.int32)
    table = table.at[:query_count, :owners].set(jnp.maximum(request - 1, 0))
    table = table.at[query_count : 2 * query_count, :picks].set(owner_of)
    table = table.at[2 * query_count : 3 * query_count, :owners].set(request)
    place = jnp.sum(jnp.where(matched, jnp.arange(1, picks + 1)[None, :, None], 0), axis=1)
    table = table.at[3 * query_count : 4 * query_count, :owners].set(place)

    own = jnp.concatenate(
        [
            lax.dynamic_slice_in_dim(cache_entry[:, 0], y * rows, rows, 1),
            jnp.zeros((own_blocks, rows, pad_width - entry_width), cache_entry.dtype),
            lax.dynamic_slice_in_dim(index_key[:, 0], y * rows, rows, 1),
        ],
        axis=2,
    )
    own = lax.dynamic_slice_in_dim(own, c * half, half, 2)

    swap = [(i, i ^ 1) for i in range(head_devices)]
    to_row = [((i % CORES) * ys + i // CORES, i) for i in range(head_devices)]
    my_index_query = lax.ppermute(index_query, "head", to_row)
    my_index_weight = lax.ppermute(index_weight, "head", to_row)
    lat = jnp.einsum(
        "thd,hdc->htc", queries[:, :, :nope], up_weight, preferred_element_type=jnp.float32
    ).astype(jnp.bfloat16)
    rope = jnp.transpose(queries[:, :, nope:], (1, 0, 2))
    query_full = jnp.concatenate(
        [lat, rope, jnp.zeros(rope.shape[:2] + (pad_width - entry_width,), rope.dtype)], axis=2
    )
    mine = lax.dynamic_slice_in_dim(query_full, c * block_len, block_len, 1)
    other = lax.dynamic_slice_in_dim(query_full, (1 - c) * block_len, block_len, 1)
    query_row = jnp.concatenate([mine, lax.ppermute(other, "head", swap)], axis=0)

    keys, tables = fetch(table, own, zs, ys, picks, block_len)
    keys = keys.reshape(key_count, full_width)

    my_picks = lax.dynamic_index_in_dim(picked_blocks, c, 0, keepdims=False)
    my_position = lax.dynamic_index_in_dim(block_position, c, 0, keepdims=False)
    key_place = (my_picks[:, None] * block_len + jnp.arange(block_len)[None, :]).reshape(key_count)
    query_place = my_position * block_len + jnp.arange(block_len)
    allowed = key_place[None, :] <= query_place[:, None]
    bias = jnp.where(allowed, 0.0, -jnp.inf).astype(jnp.float32)
    scale = queries.shape[2] ** (-0.5) * 1.4426950408889634
    prob_sum = attend(query_row, keys, bias, pad_width, scale)

    target = sum_target(prob_sum, ys) / (local_heads * head_devices)

    index_keys = keys[:, pad_width:]
    my_allowed = lax.dynamic_slice_in_dim(allowed, y * rows, rows, 0)
    index_scale = index_width ** (-0.5)
    raw = jnp.einsum("ijd,sd->ijs", my_index_query, index_keys, preferred_element_type=jnp.float32)
    act = jnp.maximum(raw, 0.0) * index_scale
    score = jnp.sum(my_index_weight[:, :, None] * act, axis=1)
    soft = masked_softmax(score, my_allowed)
    score_grad = jnp.where(my_allowed, soft - target, 0.0)
    weight_part = jnp.sum(score_grad[:, None, :] * act, axis=2)
    coefficient = jnp.where(
        raw > 0, score_grad[:, None, :] * my_index_weight[:, :, None] * index_scale, 0.0
    ).astype(jnp.bfloat16)
    key_part = jnp.einsum(
        "ijs,ijd->sd", coefficient, my_index_query, preferred_element_type=jnp.float32
    )
    weight_grad = lax.ppermute(weight_part, "head", [(b, a) for a, b in to_row])

    key_grad = give_back(
        tables, key_part.reshape(picks, block_len, index_width), zs, ys, own_blocks
    ).reshape(own_blocks, 1, block_len, index_width)
    return (key_grad, weight_grad)


def solution(mesh):
    return jax.shard_map(
        local,
        mesh=mesh,
        in_specs=(
            P("ctx", "head", None),
            P("head", None, None),
            P(("ctx", "head"), None, None),
            P(("ctx", "head"), None),
            P(None, "ctx", None, None),
            P(None, "ctx", None, None),
            P("ctx"),
            P("ctx", None),
        ),
        out_specs=(P(None, "ctx", None, None), P(("ctx", "head"), None)),
        check_vma=False,
    )
```

```python
import functools

import jax
import jax.numpy as jnp
from jax import lax
from jax.experimental import pallas as pl
from jax.experimental.pallas import tpu as pltpu
from jax.sharding import PartitionSpec as P

MESH = pl.DeviceIdType.MESH
X = 4
CORES = 2
LANES = 128


def remote(src, dst, s_sem, r_sem, device):
    return pltpu.make_async_remote_copy(
        src_ref=src, dst_ref=dst, send_sem=s_sem, recv_sem=r_sem, device_id=device, device_id_type=MESH
    )


def enter(peers):
    barrier = pltpu.get_barrier_semaphore()
    for peer in peers:
        pl.semaphore_signal(barrier, inc=1, device_id=peer, device_id_type=MESH)
    pl.semaphore_wait(barrier, len(peers))


def y_sides(ys):
    head = lax.axis_index("head")
    y, c = head // CORES, head % CORES
    step = 1 - 2 * c
    return y, c, lax.rem(y + step + ys, ys), lax.rem(y - step + ys, ys), lax.rem(y + 2, ys)


def attend_kernel(
    zs, ys, scale, heads_total,
    tab_ref, own_ref, q_ref, up_ref, bias_ref,
    target_ref, index_keys_ref, tabs_ref,
    tabs_v, tabs_s, z_low, z_high, x_out, x_in, x_all, keys, query, query_out,
    logits_a, logits_b, expo, top, total, part, middle, t_in,
    zs_sem, zr_sem, xs_sem, xr_sem, ts_sem, tr_sem, ys_sem, yr_sem, qs_sem, qr_sem, ps_sem, pr_sem, local_sem,
):
    ctx = lax.axis_index("ctx")
    z, x = ctx // X, ctx % X
    y, c, y_a, y_b, y_far = y_sides(ys)
    head = y * CORES + c
    own_blocks, rows, half = own_ref.shape
    picks, block_len, full = keys.shape
    local_heads, unused, nope = up_ref.shape[0], up_ref.shape[2], up_ref.shape[1]
    latent = up_ref.shape[2]
    width = query.shape[2]
    steps = zs // 2
    halves = 2
    part_blocks = own_blocks // halves
    z_up = (lax.rem(z + 1, zs) * X + x, head)
    z_down = (lax.rem(z + zs - 1, zs) * X + x, head)
    to_a, to_b = (ctx, y_a * CORES + c), (ctx, y_b * CORES + c)
    to_core = (ctx, y * CORES + 1 - c)
    x_peers = []
    for dx in range(X):
        for dc in range(CORES):
            if dx or dc:
                tx, tc = lax.rem(x + dx, X), lax.rem(c + dc, CORES)
                x_peers.append((dx, dc, tx, tc, (z * X + tx, y * CORES + tc)))
    tabs_v[x] = tab_ref[...]
    enter([z_up, z_down, to_a, to_b] + [p[4] for p in x_peers])
    pending = []

    def start(copy):
        copy.start()
        pending.append(copy)

    def piece(direction, k, i):
        span = pl.ds(i * part_blocks, part_blocks)
        if k == 0:
            return own_ref.at[span]
        if direction == 0 or k == steps:
            return z_low[k - 1].at[span]
        return z_high[k - 1].at[span]

    def z_copy(direction, k, i):
        return remote(
            piece(direction, k - 1, i), piece(direction, k, i),
            zs_sem.at[direction, k - 1, i], zr_sem.at[direction, k - 1, i],
            z_up if direction == 0 else z_down,
        )

    def z_lanes(k):
        return [(d, i) for i in range(halves) for d in range(2) if k < steps or (i == d)]

    for d, i in z_lanes(1):
        start(z_copy(d, 1, i))
    for dx in range(1, X):
        tx = lax.rem(x + dx, X)
        start(remote(tabs_v.at[x], tabs_v.at[x], ts_sem.at[dx - 1], tr_sem.at[dx - 1], (z * X + tx, head)))
    for dx in range(1, X):
        fx = lax.rem(x + X - dx, X)
        remote(tabs_v.at[fx], tabs_v.at[fx], ts_sem.at[dx - 1], tr_sem.at[dx - 1], z_up).wait_recv()
    to_scalar = pltpu.make_async_copy(tabs_v, tabs_s, local_sem)
    to_scalar.start()
    to_scalar.wait()
    tabs_ref[...] = tabs_v[...]

    def sources(k):
        if k == 0:
            return [(own_ref, 0)]
        if k == steps:
            return [(z_low[k - 1], zs - k)]
        return [(z_low[k - 1], zs - k), (z_high[k - 1], k)]

    def x_step(k):
        found = [(ref, rel, lax.rem(z + rel, zs) * X + x) for ref, rel in sources(k)]
        for n, (dx, dc, tx, tc, device) in enumerate(x_peers):
            for i, (ref, rel, shard) in enumerate(found):
                x_out[k, n, i] = ref[tabs_s[tx, tc, shard]]
            span = pl.ds(0, len(found))
            start(remote(x_out.at[k, n, span], x_in.at[k, n, span], xs_sem.at[k, n], xr_sem.at[k, n], device))
        for ref, rel, shard in found:
            x_all[rel * X + x, c] = ref[tabs_s[x, c, shard]]

    def x_finish(k):
        for n, (dx, dc, tx, tc, device) in enumerate(x_peers):
            fx, fc = lax.rem(x + X - dx, X), lax.rem(c + dc, CORES)
            span = pl.ds(0, len(sources(k)))
            remote(x_out.at[k, n, span], x_in.at[k, n, span], xs_sem.at[k, n], xr_sem.at[k, n], device).wait_recv()
            for i, (unused_ref, rel) in enumerate(sources(k)):
                x_all[rel * X + fx, fc] = x_in[k, n, i]

    chunks = ys_sem.shape[1]
    chunk = picks // chunks

    def y_copy(kind, owner, j, device):
        ref = keys.at[pl.ds(j * chunk, chunk), pl.ds(pl.multiple_of(owner * rows, rows), rows)]
        return remote(ref, ref, ys_sem.at[kind, j], yr_sem.at[kind, j], device)

    def y_start(j):
        def place(m, carry):
            slot = tabs_s[x, CORES + c, m]
            for fc in range(CORES):
                keys[m, pl.ds(pl.multiple_of(y * rows, rows), rows), fc * half : (fc + 1) * half] = x_all[slot, fc]
            return carry

        lax.fori_loop(j * chunk, (j + 1) * chunk, place, 0)
        start(y_copy(0, y, j, to_a))
        start(y_copy(1, y, j, to_b))

    def y_forward(j):
        y_copy(0, y_b, j, to_a).wait_recv()
        y_copy(2, y_b, j, to_a).start()

    def make_query(h):
        for mine, ref in ((True, query), (False, query_out)):
            at = pl.ds(pl.multiple_of((c if mine else 1 - c) * block_len, block_len), block_len)
            ref[h, :, :latent] = jnp.dot(
                q_ref[h, at, :nope], up_ref[h], preferred_element_type=jnp.float32
            ).astype(query.dtype)
            ref[h, :, latent:] = q_ref[h, at, nope:]

    swap = remote(query_out, query.at[pl.ds(local_heads, local_heads)], qs_sem, qr_sem, to_core)
    first = steps + 1 - chunks
    per_step = local_heads // steps
    x_step(0)
    for k in range(1, steps + 1):
        for h in range((k - 1) * per_step, k * per_step):
            make_query(h)
        if k == steps:
            start(swap)
        for d, i in z_lanes(k):
            z_copy(d, k, i).wait_recv()
            if (d, i) in z_lanes(k + 1) and k < steps:
                start(z_copy(d, k + 1, i))
        x_step(k)
        x_finish(k - 1)
        if k - 1 >= first:
            y_start(k - 1 - first)
        if k - 2 >= first:
            y_forward(k - 2 - first)
    x_finish(steps)
    y_start(chunks - 1)
    y_forward(chunks - 2)
    swap.wait_recv()

    group = logits_a.shape[0] // block_len
    groups = query.shape[0] // group
    pieces = chunk * block_len // LANES

    def dot(j, g, dst):
        block = query[pl.ds(g * group, group)].reshape(group * block_len, width)
        these = keys[pl.ds(j * chunk, chunk)].reshape(chunk * block_len, full)[:, :width]
        dst[...] = lax.dot_general(
            block, these, (((1,), (1,)), ((), ())), preferred_element_type=jnp.float32
        )

    def soften(j, g, src):
        for i in range(block_len // 8):
            bias = bias_ref[j, i * 8 : (i + 1) * 8, :]
            for h in range(group):
                value = src[h * block_len + i * 8 : h * block_len + i * 8 + 8, :] * scale + bias
                cuts = [value[:, n * LANES : (n + 1) * LANES] for n in range(pieces)]
                high = functools.reduce(jnp.maximum, cuts)
                high = jnp.maximum(high, -1e30)
                raised = [jnp.exp2(cut - high) for cut in cuts]
                at = pl.ds(pl.multiple_of((g * group + h) * block_len + i * 8, 8), 8)
                for n in range(pieces):
                    expo[j, at, n * LANES : (n + 1) * LANES] = raised[n]
                top[j, at, :] = high
                total[j, at, :] = functools.reduce(jnp.add, raised)

    def attend_chunk(j, carry):
        @pl.when(j == 1)
        def forward_last():
            y_forward(chunks - 1)

        y_copy(1, y_a, j, to_a).wait_recv()
        y_copy(2, y_far, j, to_a).wait_recv()
        dot(j, 0, logits_a)

        def pair(p, inner):
            dot(j, 2 * p + 1, logits_b)
            soften(j, 2 * p, logits_a)
            dot(j, lax.rem(2 * p + 2, groups), logits_a)
            soften(j, 2 * p + 1, logits_b)
            return inner

        lax.fori_loop(0, groups // 2, pair, 0)
        return carry

    lax.fori_loop(0, chunks, attend_chunk, 0)
    index_keys_ref[...] = keys[:, :, width:]

    def sum_heads(at):
        def one(h, sums):
            here = pl.ds(pl.multiple_of(h * block_len + at, 8), 8)
            highs = [top[j, here, :] for j in range(chunks)]
            high = jnp.max(functools.reduce(jnp.maximum, highs), axis=1, keepdims=True)
            factors = [jnp.exp2(value - high) for value in highs]
            mass = functools.reduce(
                jnp.add, [total[j, here, :] * factors[j] for j in range(chunks)]
            )
            share = 1.0 / jnp.sum(mass, axis=1, keepdims=True)
            sums = list(sums)
            for j in range(chunks):
                factor = factors[j] * share
                for n in range(pieces):
                    sums[j * pieces + n] += expo[j, here, n * LANES : (n + 1) * LANES] * factor
            return tuple(sums)

        zero = jnp.zeros((8, LANES), jnp.float32)
        return lax.fori_loop(0, query.shape[0], one, (zero,) * (chunks * pieces), unroll=4)

    def quarter(owner, dst):
        for i in range(rows // 8):
            sums = sum_heads(pl.multiple_of(owner * rows + i * 8, 8))
            for n, value in enumerate(sums):
                dst[i * 8 : (i + 1) * 8, n * LANES : (n + 1) * LANES] = value

    quarter(y_far, part.at[0])
    far = remote(part.at[0], t_in.at[0], ps_sem.at[0], pr_sem.at[0], to_a)
    start(far)
    quarter(y_b, part.at[1])
    near = remote(part.at[1], t_in.at[1], ps_sem.at[1], pr_sem.at[1], to_b)
    start(near)
    quarter(y_a, middle)
    far.wait_recv()
    part[2] = middle[...] + t_in[0]
    last = remote(part.at[2], t_in.at[2], ps_sem.at[2], pr_sem.at[2], to_a)
    start(last)
    quarter(y, middle)
    near.wait_recv()
    last.wait_recv()
    target_ref[...] = (middle[...] + t_in[1] + t_in[2]) * (1.0 / heads_total)
    for j in range(chunks):
        y_copy(2, y_b, j, to_a).wait_send()
    for copy in pending:
        copy.wait_send()


def attend(table, own, query, up_weight, bias, zs, ys, picks, block_len, heads_total, scale):
    own_blocks, rows, half = own.shape
    local_heads, unused, q_width = query.shape
    nope, latent = up_weight.shape[1:]
    width = latent + q_width - nope
    full = half * CORES
    heads = local_heads * CORES
    steps = zs // 2
    peers = X * CORES - 1
    chunks = bias.shape[0]
    chunk_keys = bias.shape[2]
    group = 8
    keep = own.dtype
    single = jnp.float32
    dma = pltpu.SemaphoreType.DMA
    return pl.pallas_call(
        functools.partial(attend_kernel, zs, ys, scale, heads_total),
        out_shape=(
            jax.ShapeDtypeStruct((rows, picks * block_len), single),
            jax.ShapeDtypeStruct((picks, block_len, full - width), keep),
            jax.ShapeDtypeStruct((X, 8, LANES), jnp.int32),
        ),
        in_specs=[pl.BlockSpec(memory_space=pltpu.VMEM)] * 5,
        out_specs=[pl.BlockSpec(memory_space=pltpu.VMEM)] * 3,
        scratch_shapes=[
            pltpu.VMEM((X, 8, LANES), jnp.int32),
            pltpu.SMEM((X, 8, LANES), jnp.int32),
            [pltpu.VMEM((own_blocks, rows, half), keep) for k in range(steps)],
            [pltpu.VMEM((own_blocks, rows, half), keep) for k in range(steps - 1)],
            pltpu.VMEM((steps + 1, peers, 2, rows, half), keep),
            pltpu.VMEM((steps + 1, peers, 2, rows, half), keep),
            pltpu.VMEM((zs * X, CORES, rows, half), keep),
            pltpu.VMEM((picks, block_len, full), keep),
            pltpu.VMEM((heads, block_len, width), keep),
            pltpu.VMEM((local_heads, block_len, width), keep),
            pltpu.VMEM((group * block_len, chunk_keys), single),
            pltpu.VMEM((group * block_len, chunk_keys), single),
            pltpu.VMEM((chunks, heads * block_len, chunk_keys), single),
            pltpu.VMEM((chunks, heads * block_len, LANES), single),
            pltpu.VMEM((chunks, heads * block_len, LANES), single),
            pltpu.VMEM((3, rows, picks * block_len), single),
            pltpu.VMEM((rows, picks * block_len), single),
            pltpu.VMEM((3, rows, picks * block_len), single),
            dma((2, steps, 2)), dma((2, steps, 2)),
            dma((steps + 1, peers)), dma((steps + 1, peers)),
            dma((X - 1,)), dma((X - 1,)),
            dma((3, chunks)), dma((3, chunks)),
            dma, dma, dma((3,)), dma((3,)), dma,
        ],
        compiler_params=pltpu.CompilerParams(
            collective_id=0, has_side_effects=True, vmem_limit_bytes=56 * 2**20
        ),
        name="attend",
    )(table, own, query, up_weight, bias)


def return_kernel(
    zs, ys, tabs_ref, part_ref, out_ref,
    y_out, y_in, quarter, x_out, x_in, z_out, z_in, mine, theirs,
    ys_sem, yr_sem, xs_sem, xr_sem, zs_sem, zr_sem, cs_sem, cr_sem, os_sem, or_sem,
):
    ctx = lax.axis_index("ctx")
    z, x = ctx // X, ctx % X
    y, c, y_a, y_b, y_far = y_sides(ys)
    head = y * CORES + c
    picks, block_len, width = part_ref.shape
    own_blocks = out_ref.shape[0]
    rows = block_len // ys
    slots = X * rows
    to_a, to_b, to_far = (ctx, y_a * CORES + c), (ctx, y_b * CORES + c), (ctx, y_far * CORES + c)
    to_core = (ctx, y * CORES + 1 - c)
    x_peers = [(lax.rem(x + d, X), (z * X + lax.rem(x + d, X), head)) for d in range(1, X)]
    z_peers = [(lax.rem(z + d, zs), (lax.rem(z + d, zs) * X + x, head)) for d in range(1, zs)]
    enter([to_a, to_b, to_far, to_core] + [p[1] for p in x_peers] + [p[1] for p in z_peers])

    def span(k):
        return pl.ds(pl.multiple_of(k * rows, rows), rows)

    y_out[0] = part_ref[:, span(y_far), :].astype(y_out.dtype)
    far = remote(y_out.at[0], y_in.at[0], ys_sem.at[0], yr_sem.at[0], to_a)
    far.start()
    y_out[1] = part_ref[:, span(y_b), :].astype(y_out.dtype)
    near = remote(y_out.at[1], y_in.at[1], ys_sem.at[1], yr_sem.at[1], to_b)
    near.start()
    far.wait_recv()
    y_out[2] = (part_ref[:, span(y_a), :] + y_in[0].astype(jnp.float32)).astype(y_out.dtype)
    last = remote(y_out.at[2], y_in.at[2], ys_sem.at[2], yr_sem.at[2], to_a)
    last.start()
    near.wait_recv()
    last.wait_recv()
    quarter[...] = (
        part_ref[:, span(y), :] + y_in[1].astype(jnp.float32) + y_in[2].astype(jnp.float32)
    )

    def choose(tx, dst):
        def body(owner, carry):
            place = tabs_ref[x, 3 * CORES + c, owner * X + tx]
            value = quarter[jnp.maximum(place - 1, 0)]
            dst[owner] = jnp.where(place > 0, value, 0.0).astype(dst.dtype)
            return carry

        lax.fori_loop(0, zs, body, 0)

    x_copies = []
    for n, (tx, device) in enumerate(x_peers):
        choose(tx, x_out.at[n])
        copy = remote(x_out.at[n], x_in.at[x], xs_sem.at[n], xr_sem.at[n], device)
        copy.start()
        x_copies.append(copy)
    choose(x, x_in.at[x])
    for n in range(X - 1):
        fx = lax.rem(x + X - n - 1, X)
        remote(x_out.at[n], x_in.at[fx], xs_sem.at[n], xr_sem.at[n], to_a).wait_recv()

    line = lax.broadcasted_iota(jnp.int32, (rows, width), 0)

    def gather(owner, dst):
        ids = jnp.zeros((rows, width), jnp.float32)
        for fx in range(X):
            dst[fx * rows : (fx + 1) * rows] = x_in[fx, owner]
            block = tabs_ref[fx, 2 * CORES + c, owner * X + x]
            ids = jnp.where(line == fx, block.astype(jnp.float32), ids)
        dst[slots : slots + rows] = ids.astype(dst.dtype)

    z_copies = []
    order = sorted(range(1, zs), key=lambda d: -min(d, zs - d))
    for d in order:
        tz, device = z_peers[d - 1]
        gather(tz, z_out.at[d - 1])
        copy = remote(z_out.at[d - 1], z_in.at[z], zs_sem.at[d - 1], zr_sem.at[d - 1], device)
        copy.start()
        z_copies.append(copy)
    gather(z, z_in.at[z])
    for d in order:
        fz = lax.rem(z + zs - d, zs)
        remote(z_out.at[d - 1], z_in.at[fz], zs_sem.at[d - 1], zr_sem.at[d - 1], to_a).wait_recv()

    def add(fz, totals):
        ids = z_in[fz, slots : slots + rows].astype(jnp.float32)
        totals = list(totals)
        for fx in range(X):
            value = z_in[fz, fx * rows : (fx + 1) * rows].astype(jnp.float32)
            block = jnp.broadcast_to(ids[fx : fx + 1], value.shape)
            for r in range(own_blocks):
                totals[r] = totals[r] + jnp.where(block == r + 1.0, value, 0.0)
        return tuple(totals)

    totals = lax.fori_loop(
        0, zs, add, tuple(jnp.zeros((rows, width), jnp.float32) for r in range(own_blocks))
    )
    for r in range(own_blocks):
        mine[r] = totals[r]
    core = remote(mine, theirs, cs_sem, cr_sem, to_core)
    core.start()
    core.wait_recv()
    out_ref[:, span(y), :] = mine[...] + theirs[...]
    o_copies = []
    for n, device in enumerate((to_a, to_b, to_far)):
        ref = out_ref.at[:, span(y), :]
        copy = remote(ref, ref, os_sem.at[n], or_sem.at[n], device)
        copy.start()
        o_copies.append(copy)
    for n, fy in enumerate((y_b, y_a, y_far)):
        ref = out_ref.at[:, span(fy), :]
        remote(ref, ref, os_sem.at[n], or_sem.at[n], to_a).wait_recv()
    for copy in [far, near, last, core] + x_copies + z_copies + o_copies:
        copy.wait_send()


def give_back(tables, key_part, zs, ys, own_blocks):
    picks, block_len, width = key_part.shape
    rows = block_len // ys
    half = jnp.bfloat16
    dma = pltpu.SemaphoreType.DMA
    return pl.pallas_call(
        functools.partial(return_kernel, zs, ys),
        out_shape=jax.ShapeDtypeStruct((own_blocks, block_len, width), jnp.float32),
        in_specs=[
            pl.BlockSpec(memory_space=pltpu.SMEM),
            pl.BlockSpec(memory_space=pltpu.VMEM),
        ],
        out_specs=pl.BlockSpec(memory_space=pltpu.VMEM),
        scratch_shapes=[
            pltpu.VMEM((3, picks, rows, width), half),
            pltpu.VMEM((3, picks, rows, width), half),
            pltpu.VMEM((picks, rows, width), jnp.float32),
            pltpu.VMEM((X - 1, zs, rows, width), half),
            pltpu.VMEM((X, zs, rows, width), half),
            pltpu.VMEM((zs - 1, (X + 1) * rows, width), half),
            pltpu.VMEM((zs, (X + 1) * rows, width), half),
            pltpu.VMEM((own_blocks, rows, width), jnp.float32),
            pltpu.VMEM((own_blocks, rows, width), jnp.float32),
            dma((3,)), dma((3,)), dma((X - 1,)), dma((X - 1,)), dma((zs - 1,)), dma((zs - 1,)),
            dma, dma, dma((3,)), dma((3,)),
        ],
        compiler_params=pltpu.CompilerParams(
            collective_id=2, has_side_effects=True, vmem_limit_bytes=40 * 2**20
        ),
        name="give_back",
    )(tables, key_part)


def masked_softmax(values, allowed):
    shifted = jnp.where(allowed, values, -jnp.inf)
    row_max = jnp.max(shifted, axis=-1, keepdims=True)
    expo = jnp.exp(shifted - row_max)
    return expo / jnp.sum(expo, axis=-1, keepdims=True)


def local(
    queries,
    up_weight,
    index_query,
    index_weight,
    cache_entry,
    index_key,
    block_position,
    picked_blocks,
):
    owners = lax.axis_size("ctx")
    head_devices = lax.axis_size("head")
    zs, ys = owners // X, head_devices // CORES
    ctx = lax.axis_index("ctx")
    head = lax.axis_index("head")
    y, c = head // CORES, head % CORES
    query_count, picks = picked_blocks.shape
    own_blocks, unused, block_len, entry_width = cache_entry.shape
    index_width = index_key.shape[3]
    key_count = picks * block_len
    rows = block_len // ys
    local_heads = queries.shape[1]
    pad_width = -(-entry_width // LANES) * LANES
    full_width = pad_width + index_width
    half = full_width // CORES

    shard_of = picked_blocks % owners
    behind = (shard_of // X - ctx // X + zs) % zs
    distance = jnp.minimum(behind, zs - behind) * picks + jnp.arange(picks)[None, :]
    rank = jnp.sum((distance[:, None, :] < distance[:, :, None]).astype(jnp.int32), axis=2)
    ordered = rank[:, :, None] == jnp.arange(picks)[None, None, :]
    blocks = jnp.sum(jnp.where(ordered, picked_blocks[:, :, None], 0), axis=1)
    owner_of = blocks % owners
    slot = (owner_of // X - ctx // X + zs) % zs * X + owner_of % X

    matched = owner_of[:, :, None] == jnp.arange(owners)[None, None, :]
    request = jnp.sum(jnp.where(matched, blocks[:, :, None] // owners + 1, 0), axis=1)
    place = jnp.sum(jnp.where(matched, jnp.arange(1, picks + 1)[None, :, None], 0), axis=1)
    wide = [(0, 0), (0, LANES - owners)]
    table = jnp.concatenate(
        [
            jnp.pad(jnp.maximum(request - 1, 0), wide),
            jnp.pad(slot, [(0, 0), (0, LANES - picks)]),
            jnp.pad(request, wide),
            jnp.pad(place, wide),
        ],
        axis=0,
    )

    own = jnp.concatenate(
        [
            lax.dynamic_slice_in_dim(cache_entry[:, 0], y * rows, rows, 1),
            jnp.zeros((own_blocks, rows, pad_width - entry_width), cache_entry.dtype),
            lax.dynamic_slice_in_dim(index_key[:, 0], y * rows, rows, 1),
        ],
        axis=2,
    )
    own = lax.dynamic_slice_in_dim(own, c * half, half, 2)

    to_row = [((i % CORES) * ys + i // CORES, i) for i in range(head_devices)]
    my_index_query = lax.ppermute(index_query, "head", to_row)
    my_index_weight = lax.ppermute(index_weight, "head", to_row)
    heads_first = jnp.pad(
        jnp.transpose(queries, (1, 0, 2)), [(0, 0), (0, 0), (0, pad_width - entry_width)]
    )

    my_picks = lax.dynamic_index_in_dim(blocks, c, 0, keepdims=False)
    my_position = lax.dynamic_index_in_dim(block_position, c, 0, keepdims=False)
    key_place = (my_picks[:, None] * block_len + jnp.arange(block_len)[None, :]).reshape(key_count)
    query_place = my_position * block_len + jnp.arange(block_len)
    allowed = key_place[None, :] <= query_place[:, None]
    chunks = 4
    chunk_place = key_place.reshape(chunks, 1, key_count // chunks)
    bias = jnp.where(chunk_place <= query_place[None, :, None], 0.0, -jnp.inf).astype(jnp.float32)
    scale = queries.shape[2] ** (-0.5) * 1.4426950408889634
    target, index_keys, tables = attend(
        table, own, heads_first, up_weight, bias,
        zs, ys, picks, block_len, local_heads * head_devices, scale,
    )
    index_keys = index_keys.reshape(key_count, index_width)
    my_allowed = lax.dynamic_slice_in_dim(allowed, y * rows, rows, 0)
    index_scale = index_width ** (-0.5)
    raw = jnp.einsum("ijd,sd->ijs", my_index_query, index_keys, preferred_element_type=jnp.float32)
    act = jnp.maximum(raw, 0.0) * index_scale
    score = jnp.sum(my_index_weight[:, :, None] * act, axis=1)
    soft = masked_softmax(score, my_allowed)
    score_grad = jnp.where(my_allowed, soft - target, 0.0)
    weight_part = jnp.sum(score_grad[:, None, :] * act, axis=2)
    coefficient = jnp.where(
        raw > 0, score_grad[:, None, :] * my_index_weight[:, :, None] * index_scale, 0.0
    ).astype(jnp.bfloat16)
    key_part = jnp.einsum(
        "ijs,ijd->sd", coefficient, my_index_query, preferred_element_type=jnp.float32
    )
    weight_grad = lax.ppermute(weight_part, "head", [(b, a) for a, b in to_row])

    key_grad = give_back(
        tables, key_part.reshape(picks, block_len, index_width), zs, ys, own_blocks
    ).reshape(own_blocks, 1, block_len, index_width)
    return (key_grad, weight_grad)


def solution(mesh):
    return jax.shard_map(
        local,
        mesh=mesh,
        in_specs=(
            P("ctx", "head", None),
            P("head", None, None),
            P(("ctx", "head"), None, None),
            P(("ctx", "head"), None),
            P(None, "ctx", None, None),
            P(None, "ctx", None, None),
            P("ctx"),
            P("ctx", None),
        ),
        out_specs=(P(None, "ctx", None, None), P(("ctx", "head"), None)),
        check_vma=False,
    )
```

```python
import functools

import jax
import jax.numpy as jnp
from jax import lax
from jax.experimental import pallas as pl
from jax.experimental.pallas import tpu as pltpu
from jax.sharding import PartitionSpec as P

MESH = pl.DeviceIdType.MESH
X = 4
CORES = 2
LANES = 128
JUMP = 1


def z_plan(steps):
    jump = min(JUMP, steps)
    plan = []
    for hop in range(1, max(jump, steps - jump + 2)):
        plan.append(
            ([(hop, hop - 1)] if hop < jump else [])
            + ([(jump + hop - 1, jump + hop - 2 if hop > 1 else 0)] if jump + hop - 1 <= steps else [])
        )
    return plan


def remote(src, dst, s_sem, r_sem, device):
    return pltpu.make_async_remote_copy(
        src_ref=src, dst_ref=dst, send_sem=s_sem, recv_sem=r_sem, device_id=device, device_id_type=MESH
    )


def enter(peers, more=0):
    barrier = pltpu.get_barrier_semaphore()
    for peer in peers:
        pl.semaphore_signal(barrier, inc=1, device_id=peer, device_id_type=MESH)
    pl.semaphore_wait(barrier, len(peers) + more)


def y_sides(ys):
    head = lax.axis_index("head")
    y, c = head // CORES, head % CORES
    step = 1 - 2 * c
    return y, c, lax.rem(y + step + ys, ys), lax.rem(y - step + ys, ys), lax.rem(y + 2, ys)


def attend_kernel(
    zs, ys, scale, heads_total,
    picked_ref, position_ref, cache_ref, index_ref, raw_ref, up_ref, iq_ref, iw_ref,
    target_ref, index_keys_ref, tabs_ref, mask_ref, my_iq_ref, my_iw_ref,
    tabs_v, tabs_s, slots_v, slots_s, own_ref, q_ref, bias_ref, z_low, z_high, x_out, x_in, x_all, keys, query, query_out,
    logits_a, logits_b, expo, top, total, part, t_in,
    zs_sem, zr_sem, xs_sem, xr_sem, ts_sem, tr_sem, ys_sem, yr_sem, is_sem, ir_sem, qs_sem, qr_sem, ps_sem, pr_sem, ms_sem, mr_sem, local_sem,
):
    ctx = lax.axis_index("ctx")
    z, x = ctx // X, ctx % X
    y, c, y_a, y_b, y_far = y_sides(ys)
    head = y * CORES + c
    own_blocks, rows, half = own_ref.shape
    picks, block_len, full = keys.shape
    local_heads, unused, nope = up_ref.shape[0], up_ref.shape[2], up_ref.shape[1]
    latent = up_ref.shape[2]
    width = query.shape[2]
    steps = zs // 2
    halves = 2
    part_blocks = own_blocks // halves
    plan = z_plan(steps)
    jumps = sorted({d - f for hop in plan for d, f in hop})

    def z_device(shift):
        return (lax.rem(z + shift + zs, zs) * X + x, head)

    to_a, to_b, to_far = [(ctx, k * CORES + c) for k in (y_a, y_b, y_far)]
    to_core = (ctx, y * CORES + 1 - c)
    x_peers = []
    for dx in range(X):
        for dc in range(CORES):
            if dx or dc:
                tx, tc = lax.rem(x + dx, X), lax.rem(c + dc, CORES)
                x_peers.append((dx, dc, tx, tc, (z * X + tx, y * CORES + tc)))
    row_to = lax.rem(head, ys) * CORES + head // ys
    row_from = c * ys + y
    moves = row_to != head

    entry = cache_ref.shape[2]
    mine_rows = pl.ds(pl.multiple_of(y * rows, rows), rows)

    @pl.when(c == 0)
    def low_half():
        own_ref[...] = cache_ref[:, mine_rows, :half]

    @pl.when(c == 1)
    def high_half():
        own_ref[:, :, : entry - half] = cache_ref[:, mine_rows, half:]
        own_ref[:, :, entry - half : width - half] = jnp.zeros(
            (own_blocks, rows, width - entry), own_ref.dtype
        )
        own_ref[:, :, width - half :] = index_ref[:, mine_rows, :]

    z_peers = [z_device(sign * jump) for jump in jumps for sign in (1, -1)]
    barrier = pltpu.get_barrier_semaphore()

    @pl.when(moves)
    def greet_movers():
        for other in (row_to, row_from):
            pl.semaphore_signal(barrier, inc=1, device_id=(ctx, other), device_id_type=MESH)

    enter(z_peers + [to_a, to_b, to_far] + [p[4] for p in x_peers], 2 * moves.astype(jnp.int32))

    pending = []

    def start(copy):
        copy.start()
        pending.append(copy)

    def piece(direction, k, i):
        span = pl.ds(i * part_blocks, part_blocks)
        if k == 0:
            return own_ref.at[span]
        if direction == 0 or k == steps:
            return z_low[k - 1].at[span]
        return z_high[k - 1].at[span]

    def z_copy(direction, d, f, i):
        return remote(
            piece(direction, f, i), piece(direction, d, i),
            zs_sem.at[direction, d - 1, i], zr_sem.at[direction, d - 1, i],
            z_device(d - f if direction == 0 else f - d),
        )

    def z_lanes(hop):
        return [
            (direction, d, f, i)
            for i in range(halves)
            for d, f in plan[hop]
            for direction in range(2)
            if d < steps or i == direction
        ]

    for lane in z_lanes(0):
        start(z_copy(*lane))

    shards = zs * X
    lane_id = lax.broadcasted_iota(jnp.int32, (8, LANES), 1)
    line_id = lax.broadcasted_iota(jnp.int32, (8, LANES), 0)

    def ring(shard):
        behind = lax.rem(lax.div(shard, X) - z + zs, zs)
        return behind, jnp.minimum(behind, zs - behind)

    lane_shard = jnp.minimum(lane_id, shards - 1)
    lane_behind, lane_far = ring(lane_shard)
    lane_key = lane_far * LANES + lane_shard
    requests, places = [], []
    for row in range(CORES):
        request = jnp.zeros((8, LANES), jnp.int32)
        place = jnp.zeros((8, LANES), jnp.int32)
        for m in range(picks):
            block = picked_ref[row, m]
            shard = lax.rem(block, shards)
            key = ring(shard)[1] * LANES + shard
            request = jnp.where(lane_id == shard, lax.div(block, shards) + 1, request)
            place = place + jnp.where(key < lane_key, 1, 0)
        requests.append(request)
        places.append(jnp.where(request > 0, place + 1, 0))
    table = jnp.zeros((8, LANES), jnp.int32)
    for row in range(CORES):
        table = jnp.where(line_id == row, jnp.maximum(requests[row] - 1, 0), table)
        table = jnp.where(line_id == 2 * CORES + row, requests[row], table)
        table = jnp.where(line_id == 3 * CORES + row, places[row], table)
    tabs_v[x] = table
    for dx in range(1, X):
        tx = lax.rem(x + dx, X)
        start(remote(tabs_v.at[x], tabs_v.at[x], ts_sem.at[dx - 1], tr_sem.at[dx - 1], (z * X + tx, head)))
    for dx in range(1, X):
        fx = lax.rem(x + X - dx, X)
        remote(tabs_v.at[fx], tabs_v.at[fx], ts_sem.at[dx - 1], tr_sem.at[dx - 1], to_a).wait_recv()
    my_place = jnp.where(c == 0, places[0], places[1])
    lane_slot = lane_behind * X + lax.rem(lane_shard, X)
    for i in range(picks // 8):
        hit = my_place == line_id + (i * 8 + 1)
        slot = jnp.sum(jnp.where(hit, lane_slot, 0), axis=1, keepdims=True)
        slots_v[i * 8 : (i + 1) * 8, :] = jnp.broadcast_to(slot, (8, LANES))
    slots_copy = pltpu.make_async_copy(slots_v, slots_s, local_sem)
    slots_copy.start()
    slots_copy.wait()
    to_scalar = pltpu.make_async_copy(tabs_v, tabs_s, local_sem)
    to_scalar.start()
    to_scalar.wait()
    tabs_ref[...] = tabs_v[...]

    def sources(hop):
        if hop == 0:
            return [(own_ref, 0)]
        found = []
        for d, f in plan[hop - 1]:
            found.append((z_low[d - 1], zs - d))
            if d < steps:
                found.append((z_high[d - 1], d))
        return found

    def x_step(k):
        found = [(ref, rel, lax.rem(z + rel, zs) * X + x) for ref, rel in sources(k)]
        for n, (dx, dc, tx, tc, device) in enumerate(x_peers):
            for i, (ref, rel, shard) in enumerate(found):
                x_out[k, n, i] = ref[tabs_s[tx, tc, shard]]
            span = pl.ds(0, len(found))
            start(remote(x_out.at[k, n, span], x_in.at[k, n, span], xs_sem.at[k, n], xr_sem.at[k, n], device))
        for ref, rel, shard in found:
            x_all[rel * X + x, c] = ref[tabs_s[x, c, shard]]

    def x_finish(k):
        for n, (dx, dc, tx, tc, device) in enumerate(x_peers):
            fx, fc = lax.rem(x + X - dx, X), lax.rem(c + dc, CORES)
            span = pl.ds(0, len(sources(k)))
            remote(x_out.at[k, n, span], x_in.at[k, n, span], xs_sem.at[k, n], xr_sem.at[k, n], device).wait_recv()
            for i, (unused_ref, rel) in enumerate(sources(k)):
                x_all[rel * X + fx, fc] = x_in[k, n, i]

    chunks = ys_sem.shape[1]
    chunk = picks // chunks

    def y_copy(kind, owner, j, device):
        here = pl.ds(pl.multiple_of(owner * rows, rows), rows)
        ref = keys.at[pl.ds(j * chunk, chunk), here, pl.ds(0, width)]
        return remote(ref, ref, ys_sem.at[kind, j], yr_sem.at[kind, j], device)

    def index_copy(kind, owner, device):
        here = pl.ds(pl.multiple_of(owner * rows, rows), rows)
        ref = keys.at[:, here, pl.ds(width, full - width)]
        return remote(ref, ref, is_sem.at[kind], ir_sem.at[kind], device)

    def y_start(j):
        def place(m, carry):
            slot = slots_s[m, 0]
            for fc in range(CORES):
                keys[m, pl.ds(pl.multiple_of(y * rows, rows), rows), fc * half : (fc + 1) * half] = x_all[slot, fc]
            return carry

        lax.fori_loop(j * chunk, (j + 1) * chunk, place, 0)
        start(y_copy(0, y, j, to_a))
        start(y_copy(1, y, j, to_b))

    def y_forward(j):
        y_copy(0, y_b, j, to_a).wait_recv()
        start(y_copy(2, y_b, j, to_a))

    def make_query(h):
        for mine, ref in ((True, query), (False, query_out)):
            at = pl.ds(pl.multiple_of((c if mine else 1 - c) * block_len, block_len), block_len)
            ref[h, :, :latent] = jnp.dot(
                q_ref[h, at, :nope], up_ref[h], preferred_element_type=jnp.float32
            ).astype(query.dtype)
            entry_end = latent + q_ref.shape[2] - nope
            ref[h, :, latent:entry_end] = q_ref[h, at, nope:]
            ref[h, :, entry_end:] = jnp.zeros((block_len, width - entry_end), query.dtype)

    def prepare():
        @pl.when(moves)
        def move():
            remote(iq_ref, my_iq_ref, ms_sem.at[0], mr_sem.at[0], (ctx, row_to)).start()
            remote(iw_ref, my_iw_ref, ms_sem.at[1], mr_sem.at[1], (ctx, row_to)).start()

        @pl.when(jnp.logical_not(moves))
        def stay():
            my_iq_ref[...] = iq_ref[...]
            my_iw_ref[...] = iw_ref[...]

        q_ref[...] = jnp.swapaxes(raw_ref[...], 0, 1)
        own_shard = lax.rem(position_ref[c], shards)
        own_place = jnp.sum(jnp.where(lane_id == own_shard, my_place, 0), axis=1, keepdims=True) - 1
        parts, unused, part_keys = bias_ref.shape
        key_id = lax.broadcasted_iota(jnp.int32, (8, part_keys), 1)
        token = lax.broadcasted_iota(jnp.int32, (8, part_keys), 0)
        for j in range(parts):
            pick_of = lax.div(key_id, block_len) + j * (part_keys // block_len)
            inside = lax.rem(key_id, block_len)
            for i in range(block_len // 8):
                after = (pick_of == own_place) & (inside > token + i * 8)
                bias_ref[j, i * 8 : (i + 1) * 8, :] = jnp.where(after, -jnp.inf, 0.0)
            mask_ref[:, j * part_keys : (j + 1) * part_keys] = bias_ref[j, mine_rows, :]

    swap = remote(query_out, query.at[pl.ds(local_heads, local_heads)], qs_sem, qr_sem, to_core)
    hops = len(plan)
    arrived = X
    started = forwarded = 0
    x_step(0)
    prepare()
    made = 0
    for hop in range(1, hops + 1):
        while made * hops < local_heads * hop:
            make_query(made)
            made += 1
        if hop == hops:
            start(swap)
        for direction, d, f, i in z_lanes(hop - 1):
            z_copy(direction, d, f, i).wait_recv()
            if hop < hops:
                for lane in z_lanes(hop):
                    if lane[0] == direction and lane[2] == d and lane[3] == i:
                        start(z_copy(*lane))
        x_step(hop)
        x_finish(hop - 1)
        before = started
        ready = max(0, picks - (shards - arrived)) // chunk
        arrived += X * len(sources(hop))
        while started < ready:
            y_start(started)
            started += 1
        while forwarded < before:
            y_forward(forwarded)
            forwarded += 1
    x_finish(hops)
    before = started
    while started < chunks:
        y_start(started)
        started += 1
    start(index_copy(0, y, to_a))
    start(index_copy(1, y, to_b))
    while forwarded < before:
        y_forward(forwarded)
        forwarded += 1
    swap.wait_recv()

    group = logits_a.shape[0] // block_len
    groups = query.shape[0] // group
    parts = expo.shape[0]
    per_part = picks // parts
    pieces = per_part * block_len // LANES

    def dot(j, g, dst):
        block = query[pl.ds(g * group, group)].reshape(group * block_len, width)
        these = keys[pl.ds(j * per_part, per_part), :, :width].reshape(per_part * block_len, width)
        dst[...] = lax.dot_general(
            block, these, (((1,), (1,)), ((), ())), preferred_element_type=jnp.float32
        )

    def soften(j, g, src):
        for i in range(block_len // 8):
            bias = bias_ref[j, i * 8 : (i + 1) * 8, :]
            for h in range(group):
                value = src[h * block_len + i * 8 : h * block_len + i * 8 + 8, :] * scale + bias
                cuts = [value[:, n * LANES : (n + 1) * LANES] for n in range(pieces)]
                high = functools.reduce(jnp.maximum, cuts)
                high = jnp.maximum(high, -1e30)
                raised = [jnp.exp2(cut - high) for cut in cuts]
                at = pl.ds(pl.multiple_of((g * group + h) * block_len + i * 8, 8), 8)
                for n in range(pieces):
                    expo[j, at, n * LANES : (n + 1) * LANES] = raised[n]
                top[j, at, :] = high
                total[j, at, :] = functools.reduce(jnp.add, raised)

    def attend_chunk(j, carry):
        for i in range(chunks // parts):
            y_copy(1, y_a, j * (chunks // parts) + i, to_a).wait_recv()
            y_copy(2, y_far, j * (chunks // parts) + i, to_a).wait_recv()
        dot(j, 0, logits_a)

        for p in range(groups // 2):
            dot(j, 2 * p + 1, logits_b)
            soften(j, 2 * p, logits_a)
            if p + 1 < groups // 2:
                dot(j, 2 * p + 2, logits_a)
            soften(j, 2 * p + 1, logits_b)
        return carry

    lax.fori_loop(0, 1, attend_chunk, 0)
    while forwarded < chunks:
        y_forward(forwarded)
        forwarded += 1
    lax.fori_loop(1, parts, attend_chunk, 0)
    index_copy(0, y_b, to_a).wait_recv()
    start(index_copy(2, y_b, to_a))
    def sum_heads(at):
        def one(h, sums):
            here = pl.ds(pl.multiple_of(h * block_len + at, 8), 8)
            highs = [top[j, here, :] for j in range(parts)]
            high = jnp.max(functools.reduce(jnp.maximum, highs), axis=1, keepdims=True)
            factors = [jnp.exp2(value - high) for value in highs]
            mass = functools.reduce(
                jnp.add, [total[j, here, :] * factors[j] for j in range(parts)]
            )
            share = 1.0 / jnp.sum(mass, axis=1, keepdims=True)
            sums = list(sums)
            for j in range(parts):
                factor = factors[j] * share
                for n in range(pieces):
                    sums[j * pieces + n] += expo[j, here, n * LANES : (n + 1) * LANES] * factor
            return tuple(sums)

        zero = jnp.zeros((8, LANES), jnp.float32)
        return lax.fori_loop(0, query.shape[0], one, (zero,) * (parts * pieces), unroll=4)

    def quarter(owner, dst):
        for i in range(rows // 8):
            sums = sum_heads(pl.multiple_of(owner * rows + i * 8, 8))
            for n, value in enumerate(sums):
                dst[i * 8 : (i + 1) * 8, n * LANES : (n + 1) * LANES] = value

    for n, (owner, device) in enumerate(((y_far, to_far), (y_a, to_a), (y_b, to_b))):
        quarter(owner, part.at[n])
        start(remote(part.at[n], t_in.at[n], ps_sem.at[n], pr_sem.at[n], device))
    quarter(y, target_ref)
    index_copy(1, y_a, to_a).wait_recv()
    index_copy(2, y_far, to_a).wait_recv()
    index_keys_ref[...] = keys[:, :, width:]
    for n in range(ys - 1):
        remote(part.at[n], t_in.at[n], ps_sem.at[n], pr_sem.at[n], to_a).wait_recv()
    target_ref[...] = (target_ref[...] + t_in[0] + t_in[1] + t_in[2]) * (1.0 / heads_total)
    @pl.when(moves)
    def moved():
        for n, (src, dst) in enumerate(((iq_ref, my_iq_ref), (iw_ref, my_iw_ref))):
            copy = remote(src, dst, ms_sem.at[n], mr_sem.at[n], (ctx, row_to))
            copy.wait_send()
            copy.wait_recv()

    for copy in pending:
        copy.wait_send()


def attend(picked, position, cache, index_key, queries, up_weight, index_query, index_weight, zs, ys, heads_total):
    own_blocks, block_len, entry = cache.shape
    query_rows, picks = picked.shape
    rows = block_len // ys
    tokens, local_heads, q_width = queries.shape
    scale = q_width ** (-0.5) * 1.4426950408889634
    nope, latent = up_weight.shape[1:]
    width = -(-entry // LANES) * LANES
    full = width + index_key.shape[2]
    half = full // CORES
    parts = 4
    part_keys = picks * block_len // parts
    heads = local_heads * CORES
    steps = zs // 2
    hops = len(z_plan(steps))
    peers = X * CORES - 1
    chunks = 8
    group = 8
    keep = cache.dtype
    single = jnp.float32
    dma = pltpu.SemaphoreType.DMA
    return pl.pallas_call(
        functools.partial(attend_kernel, zs, ys, scale, heads_total),
        out_shape=(
            jax.ShapeDtypeStruct((rows, picks * block_len), single),
            jax.ShapeDtypeStruct((picks, block_len, full - width), keep),
            jax.ShapeDtypeStruct((X, 8, LANES), jnp.int32),
            jax.ShapeDtypeStruct((rows, picks * block_len), single),
            jax.ShapeDtypeStruct(index_query.shape, index_query.dtype),
            jax.ShapeDtypeStruct(index_weight.shape, index_weight.dtype),
        ),
        in_specs=[pl.BlockSpec(memory_space=pltpu.SMEM)] * 2 + [pl.BlockSpec(memory_space=pltpu.VMEM)] * 6,
        out_specs=[pl.BlockSpec(memory_space=pltpu.VMEM)] * 6,
        scratch_shapes=[
            pltpu.VMEM((X, 8, LANES), jnp.int32),
            pltpu.SMEM((X, 8, LANES), jnp.int32),
            pltpu.VMEM((picks, LANES), jnp.int32),
            pltpu.SMEM((picks, LANES), jnp.int32),
            pltpu.VMEM((own_blocks, rows, half), keep),
            pltpu.VMEM((local_heads, tokens, q_width), keep),
            pltpu.VMEM((parts, block_len, part_keys), single),
            [pltpu.VMEM((own_blocks, rows, half), keep) for k in range(steps)],
            [pltpu.VMEM((own_blocks, rows, half), keep) for k in range(steps - 1)],
            pltpu.VMEM((hops + 1, peers, 4, rows, half), keep),
            pltpu.VMEM((hops + 1, peers, 4, rows, half), keep),
            pltpu.VMEM((zs * X, CORES, rows, half), keep),
            pltpu.VMEM((picks, block_len, full), keep),
            pltpu.VMEM((heads, block_len, width), keep),
            pltpu.VMEM((local_heads, block_len, width), keep),
            pltpu.VMEM((group * block_len, part_keys), single),
            pltpu.VMEM((group * block_len, part_keys), single),
            pltpu.VMEM((parts, heads * block_len, part_keys), single),
            pltpu.VMEM((parts, heads * block_len, LANES), single),
            pltpu.VMEM((parts, heads * block_len, LANES), single),
            pltpu.VMEM((3, rows, picks * block_len), single),
            pltpu.VMEM((3, rows, picks * block_len), single),
            dma((2, steps, 2)), dma((2, steps, 2)),
            dma((hops + 1, peers)), dma((hops + 1, peers)),
            dma((X - 1,)), dma((X - 1,)),
            dma((3, chunks)), dma((3, chunks)), dma((3,)), dma((3,)),
            dma, dma, dma((3,)), dma((3,)), dma((2,)), dma((2,)), dma,
        ],
        compiler_params=pltpu.CompilerParams(
            collective_id=0, has_side_effects=True, vmem_limit_bytes=56 * 2**20
        ),
        name="attend",
    )(picked, position, cache, index_key, queries, up_weight, index_query, index_weight)


def return_kernel(
    zs, ys, tabs_ref, part_ref, out_ref,
    y_out, y_in, quarter, x_out, x_in, z_out, z_in, mine, theirs,
    ys_sem, yr_sem, xs_sem, xr_sem, zs_sem, zr_sem, cs_sem, cr_sem, os_sem, or_sem,
):
    ctx = lax.axis_index("ctx")
    z, x = ctx // X, ctx % X
    y, c, y_a, y_b, y_far = y_sides(ys)
    head = y * CORES + c
    picks, block_len, width = part_ref.shape
    own_blocks = out_ref.shape[0]
    rows = block_len // ys
    slots = X * rows
    to_a, to_b, to_far = (ctx, y_a * CORES + c), (ctx, y_b * CORES + c), (ctx, y_far * CORES + c)
    to_core = (ctx, y * CORES + 1 - c)
    x_peers = [(lax.rem(x + d, X), (z * X + lax.rem(x + d, X), head)) for d in range(1, X)]
    z_peers = [(lax.rem(z + d, zs), (lax.rem(z + d, zs) * X + x, head)) for d in range(1, zs)]
    enter([to_a, to_b, to_far, to_core] + [p[1] for p in x_peers] + [p[1] for p in z_peers])

    def span(k):
        return pl.ds(pl.multiple_of(k * rows, rows), rows)

    y_copies = []
    for n, (owner, device) in enumerate(((y_far, to_far), (y_a, to_a), (y_b, to_b))):
        y_out[n] = part_ref[:, span(owner), :].astype(y_out.dtype)
        copy = remote(y_out.at[n], y_in.at[n], ys_sem.at[n], yr_sem.at[n], device)
        copy.start()
        y_copies.append(copy)
    for n in range(ys - 1):
        remote(y_out.at[n], y_in.at[n], ys_sem.at[n], yr_sem.at[n], to_a).wait_recv()
    quarter[...] = (
        part_ref[:, span(y), :]
        + y_in[0].astype(jnp.float32)
        + y_in[1].astype(jnp.float32)
        + y_in[2].astype(jnp.float32)
    )

    def choose(tx, dst):
        def body(owner, carry):
            place = tabs_ref[x, 3 * CORES + c, owner * X + tx]
            value = quarter[jnp.maximum(place - 1, 0)]
            dst[owner] = jnp.where(place > 0, value, 0.0).astype(dst.dtype)
            return carry

        lax.fori_loop(0, zs, body, 0)

    x_copies = []
    for n, (tx, device) in enumerate(x_peers):
        choose(tx, x_out.at[n])
        copy = remote(x_out.at[n], x_in.at[x], xs_sem.at[n], xr_sem.at[n], device)
        copy.start()
        x_copies.append(copy)
    choose(x, x_in.at[x])
    for n in range(X - 1):
        fx = lax.rem(x + X - n - 1, X)
        remote(x_out.at[n], x_in.at[fx], xs_sem.at[n], xr_sem.at[n], to_a).wait_recv()

    line = lax.broadcasted_iota(jnp.int32, (rows, width), 0)

    def gather(owner, dst):
        ids = jnp.zeros((rows, width), jnp.float32)
        for fx in range(X):
            dst[fx * rows : (fx + 1) * rows] = x_in[fx, owner]
            block = tabs_ref[fx, 2 * CORES + c, owner * X + x]
            ids = jnp.where(line == fx, block.astype(jnp.float32), ids)
        dst[slots : slots + rows] = ids.astype(dst.dtype)

    z_copies = []
    order = sorted(range(1, zs), key=lambda d: -min(d, zs - d))
    for d in order:
        tz, device = z_peers[d - 1]
        gather(tz, z_out.at[d - 1])
        copy = remote(z_out.at[d - 1], z_in.at[z], zs_sem.at[d - 1], zr_sem.at[d - 1], device)
        copy.start()
        z_copies.append(copy)
    gather(z, z_in.at[z])
    for d in order:
        fz = lax.rem(z + zs - d, zs)
        remote(z_out.at[d - 1], z_in.at[fz], zs_sem.at[d - 1], zr_sem.at[d - 1], to_a).wait_recv()

    def add(fz, totals):
        ids = z_in[fz, slots : slots + rows].astype(jnp.float32)
        totals = list(totals)
        for fx in range(X):
            value = z_in[fz, fx * rows : (fx + 1) * rows].astype(jnp.float32)
            block = jnp.broadcast_to(ids[fx : fx + 1], value.shape)
            for r in range(own_blocks):
                totals[r] = totals[r] + jnp.where(block == r + 1.0, value, 0.0)
        return tuple(totals)

    totals = lax.fori_loop(
        0, zs, add, tuple(jnp.zeros((rows, width), jnp.float32) for r in range(own_blocks))
    )
    for r in range(own_blocks):
        mine[r] = totals[r]
    core = remote(mine, theirs, cs_sem, cr_sem, to_core)
    core.start()
    core.wait_recv()
    out_ref[:, span(y), :] = mine[...] + theirs[...]
    o_copies = []
    for n, device in enumerate((to_a, to_b, to_far)):
        ref = out_ref.at[:, span(y), :]
        copy = remote(ref, ref, os_sem.at[n], or_sem.at[n], device)
        copy.start()
        o_copies.append(copy)
    for n, fy in enumerate((y_b, y_a, y_far)):
        ref = out_ref.at[:, span(fy), :]
        remote(ref, ref, os_sem.at[n], or_sem.at[n], to_a).wait_recv()
    for copy in y_copies + [core] + x_copies + z_copies + o_copies:
        copy.wait_send()


def give_back(tables, key_part, zs, ys, own_blocks):
    picks, block_len, width = key_part.shape
    rows = block_len // ys
    half = jnp.bfloat16
    dma = pltpu.SemaphoreType.DMA
    return pl.pallas_call(
        functools.partial(return_kernel, zs, ys),
        out_shape=jax.ShapeDtypeStruct((own_blocks, block_len, width), jnp.float32),
        in_specs=[
            pl.BlockSpec(memory_space=pltpu.SMEM),
            pl.BlockSpec(memory_space=pltpu.VMEM),
        ],
        out_specs=pl.BlockSpec(memory_space=pltpu.VMEM),
        scratch_shapes=[
            pltpu.VMEM((3, picks, rows, width), half),
            pltpu.VMEM((3, picks, rows, width), half),
            pltpu.VMEM((picks, rows, width), jnp.float32),
            pltpu.VMEM((X - 1, zs, rows, width), half),
            pltpu.VMEM((X, zs, rows, width), half),
            pltpu.VMEM((zs - 1, (X + 1) * rows, width), half),
            pltpu.VMEM((zs, (X + 1) * rows, width), half),
            pltpu.VMEM((own_blocks, rows, width), jnp.float32),
            pltpu.VMEM((own_blocks, rows, width), jnp.float32),
            dma((3,)), dma((3,)), dma((X - 1,)), dma((X - 1,)), dma((zs - 1,)), dma((zs - 1,)),
            dma, dma, dma((3,)), dma((3,)),
        ],
        compiler_params=pltpu.CompilerParams(
            collective_id=2, has_side_effects=True, vmem_limit_bytes=40 * 2**20
        ),
        name="give_back",
    )(tables, key_part)


def masked_softmax(values, allowed):
    shifted = jnp.where(allowed, values, -jnp.inf)
    row_max = jnp.max(shifted, axis=-1, keepdims=True)
    expo = jnp.exp(shifted - row_max)
    return expo / jnp.sum(expo, axis=-1, keepdims=True)


def local(
    queries,
    up_weight,
    index_query,
    index_weight,
    cache_entry,
    index_key,
    block_position,
    picked_blocks,
):
    owners = lax.axis_size("ctx")
    head_devices = lax.axis_size("head")
    zs, ys = owners // X, head_devices // CORES
    picks = picked_blocks.shape[1]
    own_blocks, unused, block_len, entry_width = cache_entry.shape
    index_width = index_key.shape[3]
    key_count = picks * block_len
    rows = block_len // ys
    local_heads = queries.shape[1]
    target, index_keys, tables, mask, my_index_query, my_index_weight = attend(
        picked_blocks, block_position, cache_entry[:, 0], index_key[:, 0], queries, up_weight,
        index_query, index_weight, zs, ys, local_heads * head_devices,
    )
    to_row = [((i % CORES) * ys + i // CORES, i) for i in range(head_devices)]
    index_keys = index_keys.reshape(key_count, index_width)
    my_allowed = mask == 0.0
    index_scale = index_width ** (-0.5)
    raw = jnp.einsum("ijd,sd->ijs", my_index_query, index_keys, preferred_element_type=jnp.float32)
    act = jnp.maximum(raw, 0.0) * index_scale
    score = jnp.sum(my_index_weight[:, :, None] * act, axis=1)
    soft = masked_softmax(score, my_allowed)
    score_grad = jnp.where(my_allowed, soft - target, 0.0)
    weight_part = jnp.sum(score_grad[:, None, :] * act, axis=2)
    coefficient = jnp.where(
        raw > 0, score_grad[:, None, :] * my_index_weight[:, :, None] * index_scale, 0.0
    ).astype(jnp.bfloat16)
    key_part = jnp.einsum(
        "ijs,ijd->sd", coefficient, my_index_query, preferred_element_type=jnp.float32
    )
    weight_grad = lax.ppermute(weight_part, "head", [(b, a) for a, b in to_row])

    key_grad = give_back(
        tables, key_part.reshape(picks, block_len, index_width), zs, ys, own_blocks
    ).reshape(own_blocks, 1, block_len, index_width)
    return (key_grad, weight_grad)


def solution(mesh):
    return jax.shard_map(
        local,
        mesh=mesh,
        in_specs=(
            P("ctx", "head", None),
            P("head", None, None),
            P(("ctx", "head"), None, None),
            P(("ctx", "head"), None),
            P(None, "ctx", None, None),
            P(None, "ctx", None, None),
            P("ctx"),
            P("ctx", None),
        ),
        out_specs=(P(None, "ctx", None, None), P(("ctx", "head"), None)),
        check_vma=False,
    )
```

```python
import functools

import jax
import jax.numpy as jnp
from jax import lax
from jax.experimental import pallas as pl
from jax.experimental.pallas import tpu as pltpu
from jax.sharding import PartitionSpec as P

MESH = pl.DeviceIdType.MESH
X = 4
CORES = 2
LANES = 128
JUMP = 1


def z_plan(steps):
    jump = min(JUMP, steps)
    plan = []
    for hop in range(1, max(jump, steps - jump + 2)):
        plan.append(
            ([(hop, hop - 1)] if hop < jump else [])
            + ([(jump + hop - 1, jump + hop - 2 if hop > 1 else 0)] if jump + hop - 1 <= steps else [])
        )
    return plan


def remote(src, dst, s_sem, r_sem, device):
    return pltpu.make_async_remote_copy(
        src_ref=src, dst_ref=dst, send_sem=s_sem, recv_sem=r_sem, device_id=device, device_id_type=MESH
    )


def enter(peers, more=0):
    barrier = pltpu.get_barrier_semaphore()
    for peer in peers:
        pl.semaphore_signal(barrier, inc=1, device_id=peer, device_id_type=MESH)
    pl.semaphore_wait(barrier, len(peers) + more)


def y_sides(ys):
    head = lax.axis_index("head")
    y, c = head // CORES, head % CORES
    step = 1 - 2 * c
    return y, c, lax.rem(y + step + ys, ys), lax.rem(y - step + ys, ys), lax.rem(y + 2, ys)


def attend_kernel(
    zs, ys, scale, heads_total,
    picked_ref, position_ref, cache_ref, index_ref, raw_ref, up_ref, iq_ref, iw_ref,
    target_ref, index_keys_ref, tabs_ref, mask_ref, my_iq_ref, my_iw_ref,
    tabs_v, tabs_s, slots_v, slots_s, own_ref, q_ref, bias_ref, z_low, z_high, x_out, x_in, x_all, keys, query, query_out,
    logits_a, logits_b, expo, top, total, part, t_in,
    zs_sem, zr_sem, xs_sem, xr_sem, ts_sem, tr_sem, ys_sem, yr_sem, is_sem, ir_sem, qs_sem, qr_sem, ps_sem, pr_sem, ms_sem, mr_sem, local_sem,
):
    ctx = lax.axis_index("ctx")
    z, x = ctx // X, ctx % X
    y, c, y_a, y_b, y_far = y_sides(ys)
    head = y * CORES + c
    own_blocks, rows, half = own_ref.shape
    picks, block_len, full = keys.shape
    local_heads, unused, nope = up_ref.shape[0], up_ref.shape[2], up_ref.shape[1]
    latent = up_ref.shape[2]
    width = query.shape[2]
    steps = zs // 2
    halves = 2
    part_blocks = own_blocks // halves
    plan = z_plan(steps)
    jumps = sorted({d - f for hop in plan for d, f in hop})

    def z_device(shift):
        return (lax.rem(z + shift + zs, zs) * X + x, head)

    to_a, to_b, to_far = [(ctx, k * CORES + c) for k in (y_a, y_b, y_far)]
    to_core = (ctx, y * CORES + 1 - c)
    x_peers = []
    for dx in range(X):
        for dc in range(CORES):
            if dx or dc:
                tx, tc = lax.rem(x + dx, X), lax.rem(c + dc, CORES)
                x_peers.append((dx, dc, tx, tc, (z * X + tx, y * CORES + tc)))
    row_to = lax.rem(head, ys) * CORES + head // ys
    row_from = c * ys + y
    moves = row_to != head

    entry = cache_ref.shape[2]
    mine_rows = pl.ds(pl.multiple_of(y * rows, rows), rows)

    @pl.when(c == 0)
    def low_half():
        own_ref[...] = cache_ref[:, mine_rows, :half]

    @pl.when(c == 1)
    def high_half():
        own_ref[:, :, : entry - half] = cache_ref[:, mine_rows, half:]
        own_ref[:, :, entry - half : width - half] = jnp.zeros(
            (own_blocks, rows, width - entry), own_ref.dtype
        )
        own_ref[:, :, width - half :] = index_ref[:, mine_rows, :]

    z_peers = [z_device(sign * jump) for jump in jumps for sign in (1, -1)]
    barrier = pltpu.get_barrier_semaphore()

    @pl.when(moves)
    def greet_movers():
        for other in (row_to, row_from):
            pl.semaphore_signal(barrier, inc=1, device_id=(ctx, other), device_id_type=MESH)

    enter(z_peers + [to_a, to_b, to_far] + [p[4] for p in x_peers], 2 * moves.astype(jnp.int32))

    pending = []

    def start(copy):
        copy.start()
        pending.append(copy)

    def piece(direction, k, i):
        span = pl.ds(i * part_blocks, part_blocks)
        if k == 0:
            return own_ref.at[span]
        if direction == 0 or k == steps:
            return z_low[k - 1].at[span]
        return z_high[k - 1].at[span]

    def z_copy(direction, d, f, i):
        return remote(
            piece(direction, f, i), piece(direction, d, i),
            zs_sem.at[direction, d - 1, i], zr_sem.at[direction, d - 1, i],
            z_device(d - f if direction == 0 else f - d),
        )

    def z_lanes(hop):
        return [
            (direction, d, f, i)
            for i in range(halves)
            for d, f in plan[hop]
            for direction in range(2)
            if d < steps or i == direction
        ]

    for lane in z_lanes(0):
        start(z_copy(*lane))

    shards = zs * X
    lane_id = lax.broadcasted_iota(jnp.int32, (8, LANES), 1)
    line_id = lax.broadcasted_iota(jnp.int32, (8, LANES), 0)

    def ring(shard):
        behind = lax.rem(lax.div(shard, X) - z + zs, zs)
        return behind, jnp.minimum(behind, zs - behind)

    lane_shard = jnp.minimum(lane_id, shards - 1)
    lane_behind, lane_far = ring(lane_shard)
    lane_key = lane_far * LANES + lane_shard
    requests, places = [], []
    for row in range(CORES):
        request = jnp.zeros((8, LANES), jnp.int32)
        place = jnp.zeros((8, LANES), jnp.int32)
        for m in range(picks):
            block = picked_ref[row, m]
            shard = lax.rem(block, shards)
            key = ring(shard)[1] * LANES + shard
            request = jnp.where(lane_id == shard, lax.div(block, shards) + 1, request)
            place = place + jnp.where(key < lane_key, 1, 0)
        requests.append(request)
        places.append(jnp.where(request > 0, place + 1, 0))
    table = jnp.zeros((8, LANES), jnp.int32)
    for row in range(CORES):
        table = jnp.where(line_id == row, jnp.maximum(requests[row] - 1, 0), table)
        table = jnp.where(line_id == 2 * CORES + row, requests[row], table)
        table = jnp.where(line_id == 3 * CORES + row, places[row], table)
    tabs_v[x] = table
    for dx in range(1, X):
        tx = lax.rem(x + dx, X)
        start(remote(tabs_v.at[x], tabs_v.at[x], ts_sem.at[dx - 1], tr_sem.at[dx - 1], (z * X + tx, head)))
    def sources(hop):
        if hop == 0:
            return [(own_ref, 0)]
        found = []
        for d, f in plan[hop - 1]:
            found.append((z_low[d - 1], zs - d))
            if d < steps:
                found.append((z_high[d - 1], d))
        return found

    def x_step(k):
        found = [(ref, rel, lax.rem(z + rel, zs) * X + x) for ref, rel in sources(k)]
        for n, (dx, dc, tx, tc, device) in enumerate(x_peers):
            for i, (ref, rel, shard) in enumerate(found):
                x_out[k, n, i] = ref[tabs_s[tx, tc, shard]]
            span = pl.ds(0, len(found))
            start(remote(x_out.at[k, n, span], x_in.at[k, n, span], xs_sem.at[k, n], xr_sem.at[k, n], device))
        for ref, rel, shard in found:
            x_all[rel * X + x, c] = ref[tabs_s[x, c, shard]]

    def x_finish(k):
        for n, (dx, dc, tx, tc, device) in enumerate(x_peers):
            fx, fc = lax.rem(x + X - dx, X), lax.rem(c + dc, CORES)
            span = pl.ds(0, len(sources(k)))
            remote(x_out.at[k, n, span], x_in.at[k, n, span], xs_sem.at[k, n], xr_sem.at[k, n], device).wait_recv()
            for i, (unused_ref, rel) in enumerate(sources(k)):
                x_all[rel * X + fx, fc] = x_in[k, n, i]

    chunks = ys_sem.shape[1]
    chunk = picks // chunks

    def y_copy(kind, owner, j, device):
        here = pl.ds(pl.multiple_of(owner * rows, rows), rows)
        ref = keys.at[pl.ds(j * chunk, chunk), here, pl.ds(0, width)]
        return remote(ref, ref, ys_sem.at[kind, j], yr_sem.at[kind, j], device)

    def index_copy(kind, owner, device):
        here = pl.ds(pl.multiple_of(owner * rows, rows), rows)
        ref = keys.at[:, here, pl.ds(width, full - width)]
        return remote(ref, ref, is_sem.at[kind], ir_sem.at[kind], device)

    def y_start(j):
        def place(m, carry):
            slot = slots_s[m, 0]
            for fc in range(CORES):
                keys[m, pl.ds(pl.multiple_of(y * rows, rows), rows), fc * half : (fc + 1) * half] = x_all[slot, fc]
            return carry

        lax.fori_loop(j * chunk, (j + 1) * chunk, place, 0)
        start(y_copy(0, y, j, to_a))
        start(y_copy(1, y, j, to_b))
        if j == chunks - 1:
            start(y_copy(2, y, j, to_far))

    def y_forward(j):
        y_copy(0, y_b, j, to_a).wait_recv()
        start(y_copy(2, y_b, j, to_a))

    def make_query(h):
        q_ref[h] = raw_ref[h].T
        for mine, ref in ((True, query), (False, query_out)):
            at = pl.ds(pl.multiple_of((c if mine else 1 - c) * block_len, block_len), block_len)
            ref[h, :, :latent] = jnp.dot(
                q_ref[h, at, :nope], up_ref[h], preferred_element_type=jnp.float32
            ).astype(query.dtype)
            entry_end = latent + q_ref.shape[2] - nope
            ref[h, :, latent:entry_end] = q_ref[h, at, nope:]
            ref[h, :, entry_end:] = jnp.zeros((block_len, width - entry_end), query.dtype)

    my_place = jnp.where(c == 0, places[0], places[1])

    def tables_wait():
        for dx in range(1, X):
            fx = lax.rem(x + X - dx, X)
            remote(tabs_v.at[fx], tabs_v.at[fx], ts_sem.at[dx - 1], tr_sem.at[dx - 1], to_a).wait_recv()
        lane_slot = lane_behind * X + lax.rem(lane_shard, X)
        for i in range(picks // 8):
            hit = my_place == line_id + (i * 8 + 1)
            slot = jnp.sum(jnp.where(hit, lane_slot, 0), axis=1, keepdims=True)
            slots_v[i * 8 : (i + 1) * 8, :] = jnp.broadcast_to(slot, (8, LANES))
        slots_copy = pltpu.make_async_copy(slots_v, slots_s, local_sem)
        slots_copy.start()
        slots_copy.wait()
        to_scalar = pltpu.make_async_copy(tabs_v, tabs_s, local_sem)
        to_scalar.start()
        to_scalar.wait()
        tabs_ref[...] = tabs_v[...]

    def prepare():
        @pl.when(moves)
        def move():
            remote(iq_ref, my_iq_ref, ms_sem.at[0], mr_sem.at[0], (ctx, row_to)).start()
            remote(iw_ref, my_iw_ref, ms_sem.at[1], mr_sem.at[1], (ctx, row_to)).start()

        @pl.when(jnp.logical_not(moves))
        def stay():
            my_iq_ref[...] = iq_ref[...]
            my_iw_ref[...] = iw_ref[...]

        own_shard = lax.rem(position_ref[c], shards)
        own_place = jnp.sum(jnp.where(lane_id == own_shard, my_place, 0), axis=1, keepdims=True) - 1
        parts, unused, part_keys = bias_ref.shape
        key_id = lax.broadcasted_iota(jnp.int32, (8, part_keys), 1)
        token = lax.broadcasted_iota(jnp.int32, (8, part_keys), 0)
        for j in range(parts):
            pick_of = lax.div(key_id, block_len) + j * (part_keys // block_len)
            inside = lax.rem(key_id, block_len)
            for i in range(block_len // 8):
                after = (pick_of == own_place) & (inside > token + i * 8)
                bias_ref[j, i * 8 : (i + 1) * 8, :] = jnp.where(after, -jnp.inf, 0.0)
            mask_ref[:, j * part_keys : (j + 1) * part_keys] = bias_ref[j, mine_rows, :]

    swap = remote(query_out, query.at[pl.ds(local_heads, local_heads)], qs_sem, qr_sem, to_core)
    hops = len(plan)
    arrived = X
    started = forwarded = 0
    made = 0
    for hop in range(1, hops + 1):
        while made * hops < local_heads * hop:
            make_query(made)
            made += 1
        if hop == hops:
            start(swap)
        for direction, d, f, i in z_lanes(hop - 1):
            z_copy(direction, d, f, i).wait_recv()
            if hop < hops:
                for lane in z_lanes(hop):
                    if lane[0] == direction and lane[2] == d and lane[3] == i:
                        start(z_copy(*lane))
        if hop == 1:
            tables_wait()
            x_step(0)
        x_step(hop)
        if hop == 1:
            prepare()
        x_finish(hop - 1)
        before = started
        ready = max(0, picks - (shards - arrived)) // chunk
        arrived += X * len(sources(hop))
        while started < ready:
            y_start(started)
            started += 1
        while forwarded < before:
            y_forward(forwarded)
            forwarded += 1
    x_finish(hops)
    before = started
    while started < chunks:
        y_start(started)
        started += 1
    while forwarded < before:
        y_forward(forwarded)
        forwarded += 1
    start(index_copy(0, y, to_a))
    start(index_copy(1, y, to_b))
    start(index_copy(2, y, to_far))
    swap.wait_recv()

    group = logits_a.shape[0] // block_len
    groups = query.shape[0] // group
    parts = expo.shape[0]
    per_part = picks // parts
    pieces = per_part * block_len // LANES

    def dot(j, g, dst):
        block = query[pl.ds(g * group, group)].reshape(group * block_len, width)
        these = keys[pl.ds(j * per_part, per_part), :, :width].reshape(per_part * block_len, width)
        dst[...] = lax.dot_general(
            block, these, (((1,), (1,)), ((), ())), preferred_element_type=jnp.float32
        )

    def soften(j, g, src):
        for i in range(block_len // 8):
            bias = bias_ref[j, i * 8 : (i + 1) * 8, :]
            for h in range(group):
                value = src[h * block_len + i * 8 : h * block_len + i * 8 + 8, :] * scale + bias
                cuts = [value[:, n * LANES : (n + 1) * LANES] for n in range(pieces)]
                high = functools.reduce(jnp.maximum, cuts)
                high = jnp.maximum(high, -1e30)
                raised = [jnp.exp2(cut - high) for cut in cuts]
                at = pl.ds(pl.multiple_of((g * group + h) * block_len + i * 8, 8), 8)
                for n in range(pieces):
                    expo[j, at, n * LANES : (n + 1) * LANES] = raised[n]
                top[j, at, :] = high
                total[j, at, :] = functools.reduce(jnp.add, raised)

    def attend_chunk(j, carry):
        @pl.when(j == parts - 1)
        def last_chunk():
            y_copy(0, y_b, chunks - 1, to_a).wait_recv()

        for i in range(chunks // parts):
            y_copy(1, y_a, j * (chunks // parts) + i, to_a).wait_recv()
            y_copy(2, y_far, j * (chunks // parts) + i, to_a).wait_recv()
        dot(j, 0, logits_a)

        for p in range(groups // 2):
            dot(j, 2 * p + 1, logits_b)
            soften(j, 2 * p, logits_a)
            if p + 1 < groups // 2:
                dot(j, 2 * p + 2, logits_a)
            soften(j, 2 * p + 1, logits_b)
        return carry

    lax.fori_loop(0, parts, attend_chunk, 0)
    def sum_heads(at):
        def one(h, sums):
            here = pl.ds(pl.multiple_of(h * block_len + at, 8), 8)
            highs = [top[j, here, :] for j in range(parts)]
            high = jnp.max(functools.reduce(jnp.maximum, highs), axis=1, keepdims=True)
            factors = [jnp.exp2(value - high) for value in highs]
            mass = functools.reduce(
                jnp.add, [total[j, here, :] * factors[j] for j in range(parts)]
            )
            share = 1.0 / jnp.sum(mass, axis=1, keepdims=True)
            sums = list(sums)
            for j in range(parts):
                factor = factors[j] * share
                for n in range(pieces):
                    sums[j * pieces + n] += expo[j, here, n * LANES : (n + 1) * LANES] * factor
            return tuple(sums)

        zero = jnp.zeros((8, LANES), jnp.float32)
        return lax.fori_loop(0, query.shape[0], one, (zero,) * (parts * pieces), unroll=4)

    def quarter(owner, dst):
        for i in range(rows // 8):
            sums = sum_heads(pl.multiple_of(owner * rows + i * 8, 8))
            for n, value in enumerate(sums):
                dst[i * 8 : (i + 1) * 8, n * LANES : (n + 1) * LANES] = value

    for n, (owner, device) in enumerate(((y_far, to_far), (y_a, to_a), (y_b, to_b))):
        quarter(owner, part.at[n])
        start(remote(part.at[n], t_in.at[n], ps_sem.at[n], pr_sem.at[n], device))
    quarter(y, target_ref)
    index_copy(0, y_b, to_a).wait_recv()
    index_copy(1, y_a, to_a).wait_recv()
    index_copy(2, y_far, to_a).wait_recv()
    index_keys_ref[...] = keys[:, :, width:]
    for n in range(ys - 1):
        remote(part.at[n], t_in.at[n], ps_sem.at[n], pr_sem.at[n], to_a).wait_recv()
    target_ref[...] = (target_ref[...] + t_in[0] + t_in[1] + t_in[2]) * (1.0 / heads_total)
    @pl.when(moves)
    def moved():
        for n, (src, dst) in enumerate(((iq_ref, my_iq_ref), (iw_ref, my_iw_ref))):
            copy = remote(src, dst, ms_sem.at[n], mr_sem.at[n], (ctx, row_to))
            copy.wait_send()
            copy.wait_recv()

    my_iw_ref[...] = my_iw_ref[...] * index_ref.shape[2] ** (-0.5)
    for copy in pending:
        copy.wait_send()


def attend(picked, position, cache, index_key, queries, up_weight, index_query, index_weight, zs, ys, heads_total):
    own_blocks, block_len, entry = cache.shape
    query_rows, picks = picked.shape
    rows = block_len // ys
    local_heads, q_width, tokens = queries.shape
    scale = q_width ** (-0.5) * 1.4426950408889634
    nope, latent = up_weight.shape[1:]
    width = -(-entry // LANES) * LANES
    full = width + index_key.shape[2]
    half = full // CORES
    parts = 4
    part_keys = picks * block_len // parts
    heads = local_heads * CORES
    steps = zs // 2
    hops = len(z_plan(steps))
    peers = X * CORES - 1
    chunks = 8
    group = 8
    keep = cache.dtype
    single = jnp.float32
    dma = pltpu.SemaphoreType.DMA
    return pl.pallas_call(
        functools.partial(attend_kernel, zs, ys, scale, heads_total),
        out_shape=(
            jax.ShapeDtypeStruct((rows, picks * block_len), single),
            jax.ShapeDtypeStruct((picks, block_len, full - width), keep),
            jax.ShapeDtypeStruct((X, 8, LANES), jnp.int32),
            jax.ShapeDtypeStruct((rows, picks * block_len), single),
            jax.ShapeDtypeStruct(index_query.shape, index_query.dtype),
            jax.ShapeDtypeStruct(index_weight.shape, index_weight.dtype),
        ),
        in_specs=[pl.BlockSpec(memory_space=pltpu.SMEM)] * 2 + [pl.BlockSpec(memory_space=pltpu.VMEM)] * 6,
        out_specs=[pl.BlockSpec(memory_space=pltpu.VMEM)] * 6,
        scratch_shapes=[
            pltpu.VMEM((X, 8, LANES), jnp.int32),
            pltpu.SMEM((X, 8, LANES), jnp.int32),
            pltpu.VMEM((picks, LANES), jnp.int32),
            pltpu.SMEM((picks, LANES), jnp.int32),
            pltpu.VMEM((own_blocks, rows, half), keep),
            pltpu.VMEM((local_heads, tokens, q_width), keep),
            pltpu.VMEM((parts, block_len, part_keys), single),
            [pltpu.VMEM((own_blocks, rows, half), keep) for k in range(steps)],
            [pltpu.VMEM((own_blocks, rows, half), keep) for k in range(steps - 1)],
            pltpu.VMEM((hops + 1, peers, 4, rows, half), keep),
            pltpu.VMEM((hops + 1, peers, 4, rows, half), keep),
            pltpu.VMEM((zs * X, CORES, rows, half), keep),
            pltpu.VMEM((picks, block_len, full), keep),
            pltpu.VMEM((heads, block_len, width), keep),
            pltpu.VMEM((local_heads, block_len, width), keep),
            pltpu.VMEM((group * block_len, part_keys), single),
            pltpu.VMEM((group * block_len, part_keys), single),
            pltpu.VMEM((parts, heads * block_len, part_keys), single),
            pltpu.VMEM((parts, heads * block_len, LANES), single),
            pltpu.VMEM((parts, heads * block_len, LANES), single),
            pltpu.VMEM((3, rows, picks * block_len), single),
            pltpu.VMEM((3, rows, picks * block_len), single),
            dma((2, steps, 2)), dma((2, steps, 2)),
            dma((hops + 1, peers)), dma((hops + 1, peers)),
            dma((X - 1,)), dma((X - 1,)),
            dma((3, chunks)), dma((3, chunks)), dma((3,)), dma((3,)),
            dma, dma, dma((3,)), dma((3,)), dma((2,)), dma((2,)), dma,
        ],
        compiler_params=pltpu.CompilerParams(
            collective_id=0, has_side_effects=True, vmem_limit_bytes=56 * 2**20
        ),
        name="attend",
    )(picked, position, cache, index_key, queries, up_weight, index_query, index_weight)


def return_kernel(
    zs, ys, tabs_ref, ids_ref, part_ref, out_ref,
    y_out, y_in, quarter, x_out, x_in, z_out, z_in, id_out, id_in, mine, theirs,
    is_sem, ir_sem, ys_sem, yr_sem, xs_sem, xr_sem, zs_sem, zr_sem, cs_sem, cr_sem, os_sem, or_sem,
):
    ctx = lax.axis_index("ctx")
    z, x = ctx // X, ctx % X
    y, c, y_a, y_b, y_far = y_sides(ys)
    head = y * CORES + c
    picks, block_len, width = part_ref.shape
    own_blocks = out_ref.shape[0]
    rows = block_len // ys
    to_a, to_b, to_far = (ctx, y_a * CORES + c), (ctx, y_b * CORES + c), (ctx, y_far * CORES + c)
    to_core = (ctx, y * CORES + 1 - c)
    x_peers = [(lax.rem(x + d, X), (z * X + lax.rem(x + d, X), head)) for d in range(1, X)]
    z_peers = [(lax.rem(z + d, zs), (lax.rem(z + d, zs) * X + x, head)) for d in range(1, zs)]
    enter([to_a, to_b, to_far, to_core] + [p[1] for p in x_peers] + [p[1] for p in z_peers])

    def span(k):
        return pl.ds(pl.multiple_of(k * rows, rows), rows)

    y_copies = []
    order = sorted(range(1, zs), key=lambda d: -min(d, zs - d))
    line = lax.broadcasted_iota(jnp.int32, id_out.shape, 0)
    lane = lax.broadcasted_iota(jnp.int32, id_out.shape, 1)
    asked = jnp.zeros(id_out.shape, jnp.int32)
    for fx in range(X):
        row = jnp.where(
            c == 0, ids_ref[fx, 2 * CORES : 2 * CORES + 1, :], ids_ref[fx, 2 * CORES + 1 : 2 * CORES + 2, :]
        )
        asked = jnp.where(line == fx, jnp.broadcast_to(row, id_out.shape), asked)
    id_out[...] = asked
    id_in[z] = asked
    for n, (owner, device) in enumerate(((y_far, to_far), (y_a, to_a), (y_b, to_b))):
        y_out[n] = part_ref[:, span(owner), :].astype(y_out.dtype)
        copy = remote(y_out.at[n], y_in.at[n], ys_sem.at[n], yr_sem.at[n], device)
        copy.start()
        y_copies.append(copy)
    for d in order:
        copy = remote(id_out, id_in.at[z], is_sem.at[d - 1], ir_sem.at[d - 1], z_peers[d - 1][1])
        copy.start()
        y_copies.append(copy)
    for n in range(ys - 1):
        remote(y_out.at[n], y_in.at[n], ys_sem.at[n], yr_sem.at[n], to_a).wait_recv()
    quarter[...] = (
        part_ref[:, span(y), :]
        + y_in[0].astype(jnp.float32)
        + y_in[1].astype(jnp.float32)
        + y_in[2].astype(jnp.float32)
    )

    def choose(tx, dst):
        def body(owner, carry):
            place = tabs_ref[x, 3 * CORES + c, owner * X + tx]
            value = quarter[jnp.maximum(place - 1, 0)]
            dst[owner] = jnp.where(place > 0, value, 0.0).astype(dst.dtype)
            return carry

        lax.fori_loop(0, zs, body, 0)

    x_copies = []
    for n, (tx, device) in enumerate(x_peers):
        choose(tx, x_out.at[n])
        copy = remote(x_out.at[n], x_in.at[x], xs_sem.at[n], xr_sem.at[n], device)
        copy.start()
        x_copies.append(copy)
    choose(x, x_in.at[x])
    for n in range(X - 1):
        fx = lax.rem(x + X - n - 1, X)
        remote(x_out.at[n], x_in.at[fx], xs_sem.at[n], xr_sem.at[n], to_a).wait_recv()

    def gather(owner, dst):
        for fx in range(X):
            dst[fx * rows : (fx + 1) * rows] = x_in[fx, owner]

    z_copies = []
    for d in order:
        tz, device = z_peers[d - 1]
        gather(tz, z_out.at[d - 1])
        copy = remote(z_out.at[d - 1], z_in.at[z], zs_sem.at[d - 1], zr_sem.at[d - 1], device)
        copy.start()
        z_copies.append(copy)
    gather(z, z_in.at[z])
    for d in order:
        fz = lax.rem(z + zs - d, zs)
        remote(id_out, id_in.at[fz], is_sem.at[d - 1], ir_sem.at[d - 1], to_a).wait_recv()
        remote(z_out.at[d - 1], z_in.at[fz], zs_sem.at[d - 1], zr_sem.at[d - 1], to_a).wait_recv()

    def add(fz, totals):
        ids = jnp.sum(jnp.where(lane == ctx, id_in[fz], 0), axis=1, keepdims=True)
        totals = list(totals)
        for fx in range(X):
            value = z_in[fz, fx * rows : (fx + 1) * rows].astype(jnp.float32)
            block = jnp.broadcast_to(ids[fx : fx + 1], value.shape)
            for r in range(own_blocks):
                totals[r] = totals[r] + jnp.where(block == r + 1, value, 0.0)
        return tuple(totals)

    totals = lax.fori_loop(
        0, zs, add, tuple(jnp.zeros((rows, width), jnp.float32) for r in range(own_blocks))
    )
    for r in range(own_blocks):
        mine[r] = totals[r]
    core = remote(mine, theirs, cs_sem, cr_sem, to_core)
    core.start()
    core.wait_recv()
    out_ref[:, span(y), :] = mine[...] + theirs[...]
    o_copies = []
    for n, device in enumerate((to_a, to_b, to_far)):
        ref = out_ref.at[:, span(y), :]
        copy = remote(ref, ref, os_sem.at[n], or_sem.at[n], device)
        copy.start()
        o_copies.append(copy)
    for n, fy in enumerate((y_b, y_a, y_far)):
        ref = out_ref.at[:, span(fy), :]
        remote(ref, ref, os_sem.at[n], or_sem.at[n], to_a).wait_recv()
    for copy in y_copies + [core] + x_copies + z_copies + o_copies:
        copy.wait_send()


def give_back(tables, key_part, zs, ys, own_blocks):
    picks, block_len, width = key_part.shape
    rows = block_len // ys
    half = jnp.bfloat16
    dma = pltpu.SemaphoreType.DMA
    return pl.pallas_call(
        functools.partial(return_kernel, zs, ys),
        out_shape=jax.ShapeDtypeStruct((own_blocks, block_len, width), jnp.float32),
        in_specs=[
            pl.BlockSpec(memory_space=pltpu.SMEM),
            pl.BlockSpec(memory_space=pltpu.VMEM),
            pl.BlockSpec(memory_space=pltpu.VMEM),
        ],
        out_specs=pl.BlockSpec(memory_space=pltpu.VMEM),
        scratch_shapes=[
            pltpu.VMEM((3, picks, rows, width), half),
            pltpu.VMEM((3, picks, rows, width), half),
            pltpu.VMEM((picks, rows, width), jnp.float32),
            pltpu.VMEM((X - 1, zs, rows, width), half),
            pltpu.VMEM((X, zs, rows, width), half),
            pltpu.VMEM((zs - 1, X * rows, width), half),
            pltpu.VMEM((zs, X * rows, width), half),
            pltpu.VMEM((8, LANES), jnp.int32),
            pltpu.VMEM((zs, 8, LANES), jnp.int32),
            pltpu.VMEM((own_blocks, rows, width), jnp.float32),
            pltpu.VMEM((own_blocks, rows, width), jnp.float32),
            dma((zs - 1,)), dma((zs - 1,)),
            dma((3,)), dma((3,)), dma((X - 1,)), dma((X - 1,)), dma((zs - 1,)), dma((zs - 1,)),
            dma, dma, dma((3,)), dma((3,)),
        ],
        compiler_params=pltpu.CompilerParams(
            collective_id=2, has_side_effects=True, vmem_limit_bytes=40 * 2**20
        ),
        name="give_back",
    )(tables, tables, key_part)


def masked_softmax(values, allowed):
    shifted = jnp.where(allowed, values, -jnp.inf)
    row_max = jnp.max(shifted, axis=-1, keepdims=True)
    expo = jnp.exp(shifted - row_max)
    return expo / jnp.sum(expo, axis=-1, keepdims=True)


def local(
    queries,
    up_weight,
    index_query,
    index_weight,
    cache_entry,
    index_key,
    block_position,
    picked_blocks,
):
    owners = lax.axis_size("ctx")
    head_devices = lax.axis_size("head")
    zs, ys = owners // X, head_devices // CORES
    picks = picked_blocks.shape[1]
    own_blocks, unused, block_len, entry_width = cache_entry.shape
    index_width = index_key.shape[3]
    key_count = picks * block_len
    rows = block_len // ys
    local_heads = queries.shape[1]
    target, index_keys, tables, mask, my_index_query, my_index_weight = attend(
        picked_blocks, block_position, cache_entry[:, 0], index_key[:, 0], jnp.transpose(queries, (1, 2, 0)), up_weight,
        index_query, index_weight, zs, ys, local_heads * head_devices,
    )
    to_row = [((i % CORES) * ys + i // CORES, i) for i in range(head_devices)]
    index_keys = index_keys.reshape(key_count, index_width)
    my_allowed = mask == 0.0
    raw = jnp.einsum("ijd,sd->ijs", my_index_query, index_keys, preferred_element_type=jnp.float32)
    positive = jnp.maximum(raw, 0.0)
    score = jnp.sum(my_index_weight[:, :, None] * positive, axis=1)
    soft = masked_softmax(score, my_allowed)
    score_grad = jnp.where(my_allowed, soft - target, 0.0)
    weight_part = jnp.sum(score_grad[:, None, :] * positive, axis=2) * index_width ** (-0.5)
    coefficient = jnp.where(
        raw > 0, score_grad[:, None, :] * my_index_weight[:, :, None], 0.0
    ).astype(jnp.bfloat16)
    key_part = jnp.einsum(
        "ijs,ijd->sd", coefficient, my_index_query, preferred_element_type=jnp.float32
    )
    weight_grad = lax.ppermute(weight_part, "head", [(b, a) for a, b in to_row])

    key_grad = give_back(
        tables, key_part.reshape(picks, block_len, index_width), zs, ys, own_blocks
    ).reshape(own_blocks, 1, block_len, index_width)
    return (key_grad, weight_grad)


def solution(mesh):
    return jax.shard_map(
        local,
        mesh=mesh,
        in_specs=(
            P("ctx", "head", None),
            P("head", None, None),
            P(("ctx", "head"), None, None),
            P(("ctx", "head"), None),
            P(None, "ctx", None, None),
            P(None, "ctx", None, None),
            P("ctx"),
            P("ctx", None),
        ),
        out_specs=(P(None, "ctx", None, None), P(("ctx", "head"), None)),
        check_vma=False,
    )
```

```python
import functools

import jax
import jax.numpy as jnp
from jax import lax
from jax.experimental import pallas as pl
from jax.experimental.pallas import tpu as pltpu
from jax.sharding import PartitionSpec as P

MESH = pl.DeviceIdType.MESH
X = 4
CORES = 2
LANES = 128
JUMP = 1


def z_plan(steps):
    jump = min(JUMP, steps)
    plan = []
    for hop in range(1, max(jump, steps - jump + 2)):
        plan.append(
            ([(hop, hop - 1)] if hop < jump else [])
            + ([(jump + hop - 1, jump + hop - 2 if hop > 1 else 0)] if jump + hop - 1 <= steps else [])
        )
    return plan


def remote(src, dst, s_sem, r_sem, device):
    return pltpu.make_async_remote_copy(
        src_ref=src, dst_ref=dst, send_sem=s_sem, recv_sem=r_sem, device_id=device, device_id_type=MESH
    )


def enter(peers, more=0):
    barrier = pltpu.get_barrier_semaphore()
    for peer in peers:
        pl.semaphore_signal(barrier, inc=1, device_id=peer, device_id_type=MESH)
    pl.semaphore_wait(barrier, len(peers) + more)


def y_sides(ys):
    head = lax.axis_index("head")
    y, c = head // CORES, head % CORES
    step = 1 - 2 * c
    return y, c, lax.rem(y + step + ys, ys), lax.rem(y - step + ys, ys), lax.rem(y + 2, ys)


def attend_kernel(
    zs, ys, scale, heads_total,
    picked_ref, position_ref, cache_ref, index_ref, raw_hbm, up_hbm, iq_ref, iw_ref,
    target_ref, index_keys_ref, tabs_ref, mask_ref, my_iq_ref, my_iw_ref,
    raw_ref, up_ref, load_sem, tabs_v, tabs_s, slots_v, slots_s, own_ref, q_ref, bias_ref, z_low, z_high, x_out, x_in, x_all, keys, query, query_out,
    logits_a, logits_b, expo, top, total, part, t_in,
    zs_sem, zr_sem, xs_sem, xr_sem, ts_sem, tr_sem, ys_sem, yr_sem, is_sem, ir_sem, qs_sem, qr_sem, ps_sem, pr_sem, ms_sem, mr_sem, local_sem,
):
    ctx = lax.axis_index("ctx")
    z, x = ctx // X, ctx % X
    y, c, y_a, y_b, y_far = y_sides(ys)
    head = y * CORES + c
    own_blocks, rows, half = own_ref.shape
    picks, block_len, full = keys.shape
    local_heads, unused, nope = up_ref.shape[0], up_ref.shape[2], up_ref.shape[1]
    latent = up_ref.shape[2]
    width = query.shape[2]
    steps = zs // 2
    halves = 2
    part_blocks = own_blocks // halves
    plan = z_plan(steps)
    jumps = sorted({d - f for hop in plan for d, f in hop})

    def z_device(shift):
        return (lax.rem(z + shift + zs, zs) * X + x, head)

    to_a, to_b, to_far = [(ctx, k * CORES + c) for k in (y_a, y_b, y_far)]
    to_core = (ctx, y * CORES + 1 - c)
    x_peers = []
    for dx in range(X):
        for dc in range(CORES):
            if dx or dc:
                tx, tc = lax.rem(x + dx, X), lax.rem(c + dc, CORES)
                x_peers.append((dx, dc, tx, tc, (z * X + tx, y * CORES + tc)))
    loads = [
        pltpu.make_async_copy(raw_hbm, raw_ref, load_sem.at[0]),
        pltpu.make_async_copy(up_hbm, up_ref, load_sem.at[1]),
    ]
    for load in loads:
        load.start()

    row_to = lax.rem(head, ys) * CORES + head // ys
    row_from = c * ys + y
    moves = row_to != head

    entry = cache_ref.shape[2]
    mine_rows = pl.ds(pl.multiple_of(y * rows, rows), rows)

    @pl.when(c == 0)
    def low_half():
        own_ref[...] = cache_ref[:, mine_rows, :half]

    @pl.when(c == 1)
    def high_half():
        own_ref[:, :, : entry - half] = cache_ref[:, mine_rows, half:]
        own_ref[:, :, entry - half : width - half] = jnp.zeros(
            (own_blocks, rows, width - entry), own_ref.dtype
        )
        own_ref[:, :, width - half :] = index_ref[:, mine_rows, :]

    z_peers = [z_device(sign * jump) for jump in jumps for sign in (1, -1)]
    barrier = pltpu.get_barrier_semaphore()

    @pl.when(moves)
    def greet_movers():
        for other in (row_to, row_from):
            pl.semaphore_signal(barrier, inc=1, device_id=(ctx, other), device_id_type=MESH)

    enter(z_peers + [to_a, to_b, to_far] + [p[4] for p in x_peers], 2 * moves.astype(jnp.int32))

    pending = []

    def start(copy):
        copy.start()
        pending.append(copy)

    def piece(direction, k, i):
        span = pl.ds(i * part_blocks, part_blocks)
        if k == 0:
            return own_ref.at[span]
        if direction == 0 or k == steps:
            return z_low[k - 1].at[span]
        return z_high[k - 1].at[span]

    def z_copy(direction, d, f, i):
        return remote(
            piece(direction, f, i), piece(direction, d, i),
            zs_sem.at[direction, d - 1, i], zr_sem.at[direction, d - 1, i],
            z_device(d - f if direction == 0 else f - d),
        )

    def z_lanes(hop):
        return [
            (direction, d, f, i)
            for i in range(halves)
            for d, f in plan[hop]
            for direction in range(2)
            if d < steps or i == direction
        ]

    for lane in z_lanes(0):
        start(z_copy(*lane))

    shards = zs * X
    lane_id = lax.broadcasted_iota(jnp.int32, (8, LANES), 1)
    line_id = lax.broadcasted_iota(jnp.int32, (8, LANES), 0)

    def ring(shard):
        behind = lax.rem(lax.div(shard, X) - z + zs, zs)
        return behind, jnp.minimum(behind, zs - behind)

    lane_shard = jnp.minimum(lane_id, shards - 1)
    lane_behind, lane_far = ring(lane_shard)
    lane_key = lane_far * LANES + lane_shard
    requests, places = [], []
    for row in range(CORES):
        request = jnp.zeros((8, LANES), jnp.int32)
        place = jnp.zeros((8, LANES), jnp.int32)
        for m in range(picks):
            block = picked_ref[row, m]
            shard = lax.rem(block, shards)
            key = ring(shard)[1] * LANES + shard
            request = jnp.where(lane_id == shard, lax.div(block, shards) + 1, request)
            place = place + jnp.where(key < lane_key, 1, 0)
        requests.append(request)
        places.append(jnp.where(request > 0, place + 1, 0))
    table = jnp.zeros((8, LANES), jnp.int32)
    for row in range(CORES):
        table = jnp.where(line_id == row, jnp.maximum(requests[row] - 1, 0), table)
        table = jnp.where(line_id == 2 * CORES + row, requests[row], table)
        table = jnp.where(line_id == 3 * CORES + row, places[row], table)
    tabs_v[x] = table
    for dx in range(1, X):
        tx = lax.rem(x + dx, X)
        start(remote(tabs_v.at[x], tabs_v.at[x], ts_sem.at[dx - 1], tr_sem.at[dx - 1], (z * X + tx, head)))
    def sources(hop):
        if hop == 0:
            return [(own_ref, 0)]
        found = []
        for d, f in plan[hop - 1]:
            found.append((z_low[d - 1], zs - d))
            if d < steps:
                found.append((z_high[d - 1], d))
        return found

    def x_step(k):
        found = [(ref, rel, lax.rem(z + rel, zs) * X + x) for ref, rel in sources(k)]
        for n, (dx, dc, tx, tc, device) in enumerate(x_peers):
            for i, (ref, rel, shard) in enumerate(found):
                x_out[k, n, i] = ref[tabs_s[tx, tc, shard]]
            span = pl.ds(0, len(found))
            start(remote(x_out.at[k, n, span], x_in.at[k, n, span], xs_sem.at[k, n], xr_sem.at[k, n], device))
        for ref, rel, shard in found:
            x_all[rel * X + x, c] = ref[tabs_s[x, c, shard]]

    def x_finish(k):
        for n, (dx, dc, tx, tc, device) in enumerate(x_peers):
            fx, fc = lax.rem(x + X - dx, X), lax.rem(c + dc, CORES)
            span = pl.ds(0, len(sources(k)))
            remote(x_out.at[k, n, span], x_in.at[k, n, span], xs_sem.at[k, n], xr_sem.at[k, n], device).wait_recv()
            for i, (unused_ref, rel) in enumerate(sources(k)):
                x_all[rel * X + fx, fc] = x_in[k, n, i]

    chunks = ys_sem.shape[1]
    chunk = picks // chunks

    def y_copy(kind, owner, j, device):
        here = pl.ds(pl.multiple_of(owner * rows, rows), rows)
        ref = keys.at[pl.ds(j * chunk, chunk), here, pl.ds(0, width)]
        return remote(ref, ref, ys_sem.at[kind, j], yr_sem.at[kind, j], device)

    def index_copy(kind, owner, device):
        here = pl.ds(pl.multiple_of(owner * rows, rows), rows)
        ref = keys.at[:, here, pl.ds(width, full - width)]
        return remote(ref, ref, is_sem.at[kind], ir_sem.at[kind], device)

    def y_start(j):
        def place(m, carry):
            slot = slots_s[m, 0]
            for fc in range(CORES):
                keys[m, pl.ds(pl.multiple_of(y * rows, rows), rows), fc * half : (fc + 1) * half] = x_all[slot, fc]
            return carry

        lax.fori_loop(j * chunk, (j + 1) * chunk, place, 0)
        start(y_copy(0, y, j, to_a))
        start(y_copy(1, y, j, to_b))
        if j == chunks - 1:
            start(y_copy(2, y, j, to_far))

    def y_forward(j):
        y_copy(0, y_b, j, to_a).wait_recv()
        start(y_copy(2, y_b, j, to_a))

    def make_query(h):
        q_ref[h] = raw_ref[h].T
        for mine, ref in ((True, query), (False, query_out)):
            at = pl.ds(pl.multiple_of((c if mine else 1 - c) * block_len, block_len), block_len)
            ref[h, :, :latent] = jnp.dot(
                q_ref[h, at, :nope], up_ref[h], preferred_element_type=jnp.float32
            ).astype(query.dtype)
            entry_end = latent + q_ref.shape[2] - nope
            ref[h, :, latent:entry_end] = q_ref[h, at, nope:]
            ref[h, :, entry_end:] = jnp.zeros((block_len, width - entry_end), query.dtype)

    my_place = jnp.where(c == 0, places[0], places[1])

    def tables_wait():
        for dx in range(1, X):
            fx = lax.rem(x + X - dx, X)
            remote(tabs_v.at[fx], tabs_v.at[fx], ts_sem.at[dx - 1], tr_sem.at[dx - 1], to_a).wait_recv()
        lane_slot = lane_behind * X + lax.rem(lane_shard, X)
        for i in range(picks // 8):
            hit = my_place == line_id + (i * 8 + 1)
            slot = jnp.sum(jnp.where(hit, lane_slot, 0), axis=1, keepdims=True)
            slots_v[i * 8 : (i + 1) * 8, :] = jnp.broadcast_to(slot, (8, LANES))
        slots_copy = pltpu.make_async_copy(slots_v, slots_s, local_sem)
        slots_copy.start()
        slots_copy.wait()
        to_scalar = pltpu.make_async_copy(tabs_v, tabs_s, local_sem)
        to_scalar.start()
        to_scalar.wait()
        tabs_ref[...] = tabs_v[...]

    def prepare():
        @pl.when(moves)
        def move():
            remote(iq_ref, my_iq_ref, ms_sem.at[0], mr_sem.at[0], (ctx, row_to)).start()
            remote(iw_ref, my_iw_ref, ms_sem.at[1], mr_sem.at[1], (ctx, row_to)).start()

        @pl.when(jnp.logical_not(moves))
        def stay():
            my_iq_ref[...] = iq_ref[...]
            my_iw_ref[...] = iw_ref[...]

        own_shard = lax.rem(position_ref[c], shards)
        own_place = jnp.sum(jnp.where(lane_id == own_shard, my_place, 0), axis=1, keepdims=True) - 1
        parts, unused, part_keys = bias_ref.shape
        key_id = lax.broadcasted_iota(jnp.int32, (8, part_keys), 1)
        token = lax.broadcasted_iota(jnp.int32, (8, part_keys), 0)
        for j in range(parts):
            pick_of = lax.div(key_id, block_len) + j * (part_keys // block_len)
            inside = lax.rem(key_id, block_len)
            for i in range(block_len // 8):
                after = (pick_of == own_place) & (inside > token + i * 8)
                bias_ref[j, i * 8 : (i + 1) * 8, :] = jnp.where(after, -jnp.inf, 0.0)
            mask_ref[:, j * part_keys : (j + 1) * part_keys] = bias_ref[j, mine_rows, :]

    swap = remote(query_out, query.at[pl.ds(local_heads, local_heads)], qs_sem, qr_sem, to_core)
    hops = len(plan)
    arrived = X
    started = forwarded = 0
    made = 0
    for hop in range(1, hops + 1):
        if hop == 1:
            for load in loads:
                load.wait()
        while made * hops < local_heads * hop:
            make_query(made)
            made += 1
        if hop == hops:
            start(swap)
        for direction, d, f, i in z_lanes(hop - 1):
            z_copy(direction, d, f, i).wait_recv()
            if hop < hops:
                for lane in z_lanes(hop):
                    if lane[0] == direction and lane[2] == d and lane[3] == i:
                        start(z_copy(*lane))
        if hop == 1:
            tables_wait()
            x_step(0)
        x_step(hop)
        if hop == 1:
            prepare()
        x_finish(hop - 1)
        before = started
        ready = max(0, picks - (shards - arrived)) // chunk
        arrived += X * len(sources(hop))
        while started < ready:
            y_start(started)
            started += 1
        while forwarded < before:
            y_forward(forwarded)
            forwarded += 1
    x_finish(hops)
    before = started
    while started < chunks:
        y_start(started)
        started += 1
    while forwarded < before:
        y_forward(forwarded)
        forwarded += 1
    start(index_copy(0, y, to_a))
    start(index_copy(1, y, to_b))
    start(index_copy(2, y, to_far))
    swap.wait_recv()

    group = logits_a.shape[0] // block_len
    groups = query.shape[0] // group
    parts = expo.shape[0]
    per_part = picks // parts
    pieces = per_part * block_len // LANES

    def dot(j, g, dst):
        block = query[pl.ds(g * group, group)].reshape(group * block_len, width)
        these = keys[pl.ds(j * per_part, per_part), :, :width].reshape(per_part * block_len, width)
        dst[...] = lax.dot_general(
            block, these, (((1,), (1,)), ((), ())), preferred_element_type=jnp.float32
        )

    def soften(j, g, src):
        for i in range(block_len // 8):
            bias = bias_ref[j, i * 8 : (i + 1) * 8, :]
            for h in range(group):
                value = src[h * block_len + i * 8 : h * block_len + i * 8 + 8, :] * scale + bias
                cuts = [value[:, n * LANES : (n + 1) * LANES] for n in range(pieces)]
                high = functools.reduce(jnp.maximum, cuts)
                high = jnp.maximum(high, -1e30)
                raised = [jnp.exp2(cut - high) for cut in cuts]
                at = pl.ds(pl.multiple_of((g * group + h) * block_len + i * 8, 8), 8)
                for n in range(pieces):
                    expo[j, at, n * LANES : (n + 1) * LANES] = raised[n]
                top[j, at, :] = high
                total[j, at, :] = functools.reduce(jnp.add, raised)

    def attend_chunk(j, carry):
        @pl.when(j == parts - 1)
        def last_chunk():
            y_copy(0, y_b, chunks - 1, to_a).wait_recv()

        for i in range(chunks // parts):
            y_copy(1, y_a, j * (chunks // parts) + i, to_a).wait_recv()
            y_copy(2, y_far, j * (chunks // parts) + i, to_a).wait_recv()
        dot(j, 0, logits_a)

        for p in range(groups // 2):
            dot(j, 2 * p + 1, logits_b)
            soften(j, 2 * p, logits_a)
            if p + 1 < groups // 2:
                dot(j, 2 * p + 2, logits_a)
            soften(j, 2 * p + 1, logits_b)
        return carry

    lax.fori_loop(0, parts, attend_chunk, 0)
    def sum_heads(at):
        def one(h, sums):
            here = pl.ds(pl.multiple_of(h * block_len + at, 8), 8)
            highs = [top[j, here, :] for j in range(parts)]
            high = jnp.max(functools.reduce(jnp.maximum, highs), axis=1, keepdims=True)
            factors = [jnp.exp2(value - high) for value in highs]
            mass = functools.reduce(
                jnp.add, [total[j, here, :] * factors[j] for j in range(parts)]
            )
            share = 1.0 / jnp.sum(mass, axis=1, keepdims=True)
            sums = list(sums)
            for j in range(parts):
                factor = factors[j] * share
                for n in range(pieces):
                    sums[j * pieces + n] += expo[j, here, n * LANES : (n + 1) * LANES] * factor
            return tuple(sums)

        zero = jnp.zeros((8, LANES), jnp.float32)
        return lax.fori_loop(0, query.shape[0], one, (zero,) * (parts * pieces), unroll=4)

    def quarter(owner, dst):
        for i in range(rows // 8):
            sums = sum_heads(pl.multiple_of(owner * rows + i * 8, 8))
            for n, value in enumerate(sums):
                dst[i * 8 : (i + 1) * 8, n * LANES : (n + 1) * LANES] = value

    for n, (owner, device) in enumerate(((y_far, to_far), (y_a, to_a), (y_b, to_b))):
        quarter(owner, part.at[n])
        start(remote(part.at[n], t_in.at[n], ps_sem.at[n], pr_sem.at[n], device))
    quarter(y, target_ref)
    index_copy(0, y_b, to_a).wait_recv()
    index_copy(1, y_a, to_a).wait_recv()
    index_copy(2, y_far, to_a).wait_recv()
    index_keys_ref[...] = keys[:, :, width:]
    for n in range(ys - 1):
        remote(part.at[n], t_in.at[n], ps_sem.at[n], pr_sem.at[n], to_a).wait_recv()
    target_ref[...] = (target_ref[...] + t_in[0] + t_in[1] + t_in[2]) * (1.0 / heads_total)
    @pl.when(moves)
    def moved():
        for n, (src, dst) in enumerate(((iq_ref, my_iq_ref), (iw_ref, my_iw_ref))):
            copy = remote(src, dst, ms_sem.at[n], mr_sem.at[n], (ctx, row_to))
            copy.wait_send()
            copy.wait_recv()

    my_iw_ref[...] = my_iw_ref[...] * index_ref.shape[2] ** (-0.5)
    for copy in pending:
        copy.wait_send()


def attend(picked, position, cache, index_key, queries, up_weight, index_query, index_weight, zs, ys, heads_total):
    own_blocks, block_len, entry = cache.shape
    query_rows, picks = picked.shape
    rows = block_len // ys
    local_heads, q_width, tokens = queries.shape
    scale = q_width ** (-0.5) * 1.4426950408889634
    nope, latent = up_weight.shape[1:]
    width = -(-entry // LANES) * LANES
    full = width + index_key.shape[2]
    half = full // CORES
    parts = 4
    part_keys = picks * block_len // parts
    heads = local_heads * CORES
    steps = zs // 2
    hops = len(z_plan(steps))
    peers = X * CORES - 1
    chunks = 8
    group = 8
    keep = cache.dtype
    single = jnp.float32
    dma = pltpu.SemaphoreType.DMA
    return pl.pallas_call(
        functools.partial(attend_kernel, zs, ys, scale, heads_total),
        out_shape=(
            jax.ShapeDtypeStruct((rows, picks * block_len), single),
            jax.ShapeDtypeStruct((picks, block_len, full - width), keep),
            jax.ShapeDtypeStruct((X, 8, LANES), jnp.int32),
            jax.ShapeDtypeStruct((rows, picks * block_len), single),
            jax.ShapeDtypeStruct(index_query.shape, index_query.dtype),
            jax.ShapeDtypeStruct(index_weight.shape, index_weight.dtype),
        ),
        in_specs=[pl.BlockSpec(memory_space=pltpu.SMEM)] * 2
        + [pl.BlockSpec(memory_space=pltpu.VMEM)] * 2
        + [pl.BlockSpec(memory_space=pl.ANY)] * 2
        + [pl.BlockSpec(memory_space=pltpu.VMEM)] * 2,
        out_specs=[pl.BlockSpec(memory_space=pltpu.VMEM)] * 6,
        scratch_shapes=[
            pltpu.VMEM(queries.shape, keep),
            pltpu.VMEM(up_weight.shape, keep),
            dma((2,)),
            pltpu.VMEM((X, 8, LANES), jnp.int32),
            pltpu.SMEM((X, 8, LANES), jnp.int32),
            pltpu.VMEM((picks, LANES), jnp.int32),
            pltpu.SMEM((picks, LANES), jnp.int32),
            pltpu.VMEM((own_blocks, rows, half), keep),
            pltpu.VMEM((local_heads, tokens, q_width), keep),
            pltpu.VMEM((parts, block_len, part_keys), single),
            [pltpu.VMEM((own_blocks, rows, half), keep) for k in range(steps)],
            [pltpu.VMEM((own_blocks, rows, half), keep) for k in range(steps - 1)],
            pltpu.VMEM((hops + 1, peers, 4, rows, half), keep),
            pltpu.VMEM((hops + 1, peers, 4, rows, half), keep),
            pltpu.VMEM((zs * X, CORES, rows, half), keep),
            pltpu.VMEM((picks, block_len, full), keep),
            pltpu.VMEM((heads, block_len, width), keep),
            pltpu.VMEM((local_heads, block_len, width), keep),
            pltpu.VMEM((group * block_len, part_keys), single),
            pltpu.VMEM((group * block_len, part_keys), single),
            pltpu.VMEM((parts, heads * block_len, part_keys), single),
            pltpu.VMEM((parts, heads * block_len, LANES), single),
            pltpu.VMEM((parts, heads * block_len, LANES), single),
            pltpu.VMEM((3, rows, picks * block_len), single),
            pltpu.VMEM((3, rows, picks * block_len), single),
            dma((2, steps, 2)), dma((2, steps, 2)),
            dma((hops + 1, peers)), dma((hops + 1, peers)),
            dma((X - 1,)), dma((X - 1,)),
            dma((3, chunks)), dma((3, chunks)), dma((3,)), dma((3,)),
            dma, dma, dma((3,)), dma((3,)), dma((2,)), dma((2,)), dma,
        ],
        compiler_params=pltpu.CompilerParams(
            collective_id=0, has_side_effects=True, vmem_limit_bytes=56 * 2**20
        ),
        name="attend",
    )(picked, position, cache, index_key, queries, up_weight, index_query, index_weight)


def return_kernel(
    zs, ys, tabs_ref, ids_ref, part_ref, weight_ref, out_ref, home_ref,
    y_out, y_in, quarter, x_out, x_in, z_out, z_in, id_out, id_in, mine, theirs,
    ws_sem, wr_sem, is_sem, ir_sem, ys_sem, yr_sem, xs_sem, xr_sem, zs_sem, zr_sem, cs_sem, cr_sem, os_sem, or_sem,
):
    ctx = lax.axis_index("ctx")
    z, x = ctx // X, ctx % X
    y, c, y_a, y_b, y_far = y_sides(ys)
    head = y * CORES + c
    picks, block_len, width = part_ref.shape
    own_blocks = out_ref.shape[0]
    rows = block_len // ys
    to_a, to_b, to_far = (ctx, y_a * CORES + c), (ctx, y_b * CORES + c), (ctx, y_far * CORES + c)
    to_core = (ctx, y * CORES + 1 - c)
    x_peers = [(lax.rem(x + d, X), (z * X + lax.rem(x + d, X), head)) for d in range(1, X)]
    z_peers = [(lax.rem(z + d, zs), (lax.rem(z + d, zs) * X + x, head)) for d in range(1, zs)]
    home = c * ys + y
    comes_from = lax.rem(head, ys) * CORES + head // ys
    moves = home != head
    barrier = pltpu.get_barrier_semaphore()

    @pl.when(moves)
    def greet_movers():
        for other in (home, comes_from):
            pl.semaphore_signal(barrier, inc=1, device_id=(ctx, other), device_id_type=MESH)

    enter(
        [to_a, to_b, to_far, to_core] + [p[1] for p in x_peers] + [p[1] for p in z_peers],
        2 * moves.astype(jnp.int32),
    )

    def span(k):
        return pl.ds(pl.multiple_of(k * rows, rows), rows)

    y_copies = []
    order = sorted(range(1, zs), key=lambda d: -min(d, zs - d))
    line = lax.broadcasted_iota(jnp.int32, id_out.shape, 0)
    lane = lax.broadcasted_iota(jnp.int32, id_out.shape, 1)
    asked = jnp.zeros(id_out.shape, jnp.int32)
    for fx in range(X):
        row = jnp.where(
            c == 0, ids_ref[fx, 2 * CORES : 2 * CORES + 1, :], ids_ref[fx, 2 * CORES + 1 : 2 * CORES + 2, :]
        )
        asked = jnp.where(line == fx, jnp.broadcast_to(row, id_out.shape), asked)
    id_out[...] = asked
    id_in[z] = asked
    for n, (owner, device) in enumerate(((y_far, to_far), (y_a, to_a), (y_b, to_b))):
        y_out[n] = part_ref[:, span(owner), :].astype(y_out.dtype)
        copy = remote(y_out.at[n], y_in.at[n], ys_sem.at[n], yr_sem.at[n], device)
        copy.start()
        y_copies.append(copy)
    weight_copy = remote(weight_ref, home_ref, ws_sem, wr_sem, (ctx, home))

    @pl.when(moves)
    def move():
        weight_copy.start()

    @pl.when(jnp.logical_not(moves))
    def stay():
        home_ref[...] = weight_ref[...]

    for d in order:
        copy = remote(id_out, id_in.at[z], is_sem.at[d - 1], ir_sem.at[d - 1], z_peers[d - 1][1])
        copy.start()
        y_copies.append(copy)
    for n in range(ys - 1):
        remote(y_out.at[n], y_in.at[n], ys_sem.at[n], yr_sem.at[n], to_a).wait_recv()
    quarter[...] = (
        part_ref[:, span(y), :]
        + y_in[0].astype(jnp.float32)
        + y_in[1].astype(jnp.float32)
        + y_in[2].astype(jnp.float32)
    )

    def choose(tx, dst):
        def body(owner, carry):
            place = tabs_ref[x, 3 * CORES + c, owner * X + tx]
            value = quarter[jnp.maximum(place - 1, 0)]
            dst[owner] = jnp.where(place > 0, value, 0.0).astype(dst.dtype)
            return carry

        lax.fori_loop(0, zs, body, 0)

    x_copies = []
    for n, (tx, device) in enumerate(x_peers):
        choose(tx, x_out.at[n])
        copy = remote(x_out.at[n], x_in.at[x], xs_sem.at[n], xr_sem.at[n], device)
        copy.start()
        x_copies.append(copy)
    choose(x, x_in.at[x])
    for n in range(X - 1):
        fx = lax.rem(x + X - n - 1, X)
        remote(x_out.at[n], x_in.at[fx], xs_sem.at[n], xr_sem.at[n], to_a).wait_recv()

    def gather(owner, dst):
        for fx in range(X):
            dst[fx * rows : (fx + 1) * rows] = x_in[fx, owner]

    z_copies = []
    for d in order:
        tz, device = z_peers[d - 1]
        gather(tz, z_out.at[d - 1])
        copy = remote(z_out.at[d - 1], z_in.at[z], zs_sem.at[d - 1], zr_sem.at[d - 1], device)
        copy.start()
        z_copies.append(copy)
    gather(z, z_in.at[z])
    for d in order:
        fz = lax.rem(z + zs - d, zs)
        remote(id_out, id_in.at[fz], is_sem.at[d - 1], ir_sem.at[d - 1], to_a).wait_recv()
        remote(z_out.at[d - 1], z_in.at[fz], zs_sem.at[d - 1], zr_sem.at[d - 1], to_a).wait_recv()

    def add(fz, totals):
        ids = jnp.sum(jnp.where(lane == ctx, id_in[fz], 0), axis=1, keepdims=True)
        totals = list(totals)
        for fx in range(X):
            value = z_in[fz, fx * rows : (fx + 1) * rows].astype(jnp.float32)
            block = jnp.broadcast_to(ids[fx : fx + 1], value.shape)
            for r in range(own_blocks):
                totals[r] = totals[r] + jnp.where(block == r + 1, value, 0.0)
        return tuple(totals)

    totals = lax.fori_loop(
        0, zs, add, tuple(jnp.zeros((rows, width), jnp.float32) for r in range(own_blocks))
    )
    for r in range(own_blocks):
        mine[r] = totals[r]
    core = remote(mine, theirs, cs_sem, cr_sem, to_core)
    core.start()
    core.wait_recv()
    out_ref[:, span(y), :] = mine[...] + theirs[...]
    o_copies = []
    for n, device in enumerate((to_a, to_b, to_far)):
        ref = out_ref.at[:, span(y), :]
        copy = remote(ref, ref, os_sem.at[n], or_sem.at[n], device)
        copy.start()
        o_copies.append(copy)
    for n, fy in enumerate((y_b, y_a, y_far)):
        ref = out_ref.at[:, span(fy), :]
        remote(ref, ref, os_sem.at[n], or_sem.at[n], to_a).wait_recv()
    @pl.when(moves)
    def moved():
        weight_copy.wait_send()
        weight_copy.wait_recv()

    for copy in y_copies + [core] + x_copies + z_copies + o_copies:
        copy.wait_send()


def give_back(tables, key_part, weight_part, zs, ys, own_blocks):
    picks, block_len, width = key_part.shape
    rows = block_len // ys
    half = jnp.bfloat16
    dma = pltpu.SemaphoreType.DMA
    return pl.pallas_call(
        functools.partial(return_kernel, zs, ys),
        out_shape=(
            jax.ShapeDtypeStruct((own_blocks, block_len, width), jnp.float32),
            jax.ShapeDtypeStruct(weight_part.shape, jnp.float32),
        ),
        in_specs=[
            pl.BlockSpec(memory_space=pltpu.SMEM),
            pl.BlockSpec(memory_space=pltpu.VMEM),
            pl.BlockSpec(memory_space=pltpu.VMEM),
            pl.BlockSpec(memory_space=pltpu.VMEM),
        ],
        out_specs=[pl.BlockSpec(memory_space=pltpu.VMEM)] * 2,
        scratch_shapes=[
            pltpu.VMEM((3, picks, rows, width), half),
            pltpu.VMEM((3, picks, rows, width), half),
            pltpu.VMEM((picks, rows, width), jnp.float32),
            pltpu.VMEM((X - 1, zs, rows, width), half),
            pltpu.VMEM((X, zs, rows, width), half),
            pltpu.VMEM((zs - 1, X * rows, width), half),
            pltpu.VMEM((zs, X * rows, width), half),
            pltpu.VMEM((8, LANES), jnp.int32),
            pltpu.VMEM((zs, 8, LANES), jnp.int32),
            pltpu.VMEM((own_blocks, rows, width), jnp.float32),
            pltpu.VMEM((own_blocks, rows, width), jnp.float32),
            dma, dma, dma((zs - 1,)), dma((zs - 1,)),
            dma((3,)), dma((3,)), dma((X - 1,)), dma((X - 1,)), dma((zs - 1,)), dma((zs - 1,)),
            dma, dma, dma((3,)), dma((3,)),
        ],
        compiler_params=pltpu.CompilerParams(
            collective_id=2, has_side_effects=True, vmem_limit_bytes=40 * 2**20
        ),
        name="give_back",
    )(tables, tables, key_part, weight_part)


def masked_softmax(values, allowed):
    shifted = jnp.where(allowed, values, -jnp.inf)
    row_max = jnp.max(shifted, axis=-1, keepdims=True)
    expo = jnp.exp(shifted - row_max)
    return expo / jnp.sum(expo, axis=-1, keepdims=True)


def local(
    queries,
    up_weight,
    index_query,
    index_weight,
    cache_entry,
    index_key,
    block_position,
    picked_blocks,
):
    owners = lax.axis_size("ctx")
    head_devices = lax.axis_size("head")
    zs, ys = owners // X, head_devices // CORES
    picks = picked_blocks.shape[1]
    own_blocks, unused, block_len, entry_width = cache_entry.shape
    index_width = index_key.shape[3]
    key_count = picks * block_len
    rows = block_len // ys
    local_heads = queries.shape[1]
    target, index_keys, tables, mask, my_index_query, my_index_weight = attend(
        picked_blocks, block_position, cache_entry[:, 0], index_key[:, 0], jnp.transpose(queries, (1, 2, 0)), up_weight,
        index_query, index_weight, zs, ys, local_heads * head_devices,
    )
    index_keys = index_keys.reshape(key_count, index_width)
    my_allowed = mask == 0.0
    raw = jnp.einsum("ijd,sd->ijs", my_index_query, index_keys, preferred_element_type=jnp.float32)
    positive = jnp.maximum(raw, 0.0)
    score = jnp.sum(my_index_weight[:, :, None] * positive, axis=1)
    soft = masked_softmax(score, my_allowed)
    score_grad = jnp.where(my_allowed, soft - target, 0.0)
    weight_part = jnp.sum(score_grad[:, None, :] * positive, axis=2) * index_width ** (-0.5)
    coefficient = jnp.where(
        raw > 0, score_grad[:, None, :] * my_index_weight[:, :, None], 0.0
    ).astype(jnp.bfloat16)
    key_part = jnp.einsum(
        "ijs,ijd->sd", coefficient, my_index_query, preferred_element_type=jnp.float32
    )
    key_grad, weight_grad = give_back(
        tables, key_part.reshape(picks, block_len, index_width), weight_part, zs, ys, own_blocks
    )
    key_grad = key_grad.reshape(own_blocks, 1, block_len, index_width)
    return (key_grad, weight_grad)


def solution(mesh):
    return jax.shard_map(
        local,
        mesh=mesh,
        in_specs=(
            P("ctx", "head", None),
            P("head", None, None),
            P(("ctx", "head"), None, None),
            P(("ctx", "head"), None),
            P(None, "ctx", None, None),
            P(None, "ctx", None, None),
            P("ctx"),
            P("ctx", None),
        ),
        out_specs=(P(None, "ctx", None, None), P(("ctx", "head"), None)),
        check_vma=False,
    )
```

```python
import functools

import jax
import jax.numpy as jnp
from jax import lax
from jax.experimental import pallas as pl
from jax.experimental.pallas import tpu as pltpu
from jax.sharding import PartitionSpec as P

MESH = pl.DeviceIdType.MESH
X = 4
CORES = 2
LANES = 128
DIRECT = 3
JUMP = 1


def z_plan(steps):
    jump = min(JUMP, steps)
    plan = []
    for hop in range(1, max(jump, steps - jump + 2)):
        plan.append(
            ([(hop, hop - 1)] if hop < jump else [])
            + ([(jump + hop - 1, jump + hop - 2 if hop > 1 else 0)] if jump + hop - 1 <= steps else [])
        )
    return plan


def remote(src, dst, s_sem, r_sem, device):
    return pltpu.make_async_remote_copy(
        src_ref=src, dst_ref=dst, send_sem=s_sem, recv_sem=r_sem, device_id=device, device_id_type=MESH
    )


def enter(peers, more=0):
    barrier = pltpu.get_barrier_semaphore()
    for peer in peers:
        pl.semaphore_signal(barrier, inc=1, device_id=peer, device_id_type=MESH)
    pl.semaphore_wait(barrier, len(peers) + more)


def y_sides(ys):
    head = lax.axis_index("head")
    y, c = head // CORES, head % CORES
    step = 1 - 2 * c
    return y, c, lax.rem(y + step + ys, ys), lax.rem(y - step + ys, ys), lax.rem(y + 2, ys)


def attend_kernel(
    zs, ys, scale, heads_total,
    picked_ref, position_ref, cache_ref, index_ref, raw_hbm, up_hbm, iq_ref, iw_ref,
    target_ref, index_keys_ref, tabs_ref, mask_ref, my_iq_ref, my_iw_ref,
    raw_ref, up_ref, load_sem, tabs_v, tabs_s, slots_v, slots_s, own_ref, q_ref, bias_ref, z_low, z_high, x_out, x_in, x_all, keys, query, query_out,
    logits_a, logits_b, expo, top, total, part, t_in,
    zs_sem, zr_sem, xs_sem, xr_sem, ts_sem, tr_sem, ys_sem, yr_sem, is_sem, ir_sem, qs_sem, qr_sem, ps_sem, pr_sem, ms_sem, mr_sem, local_sem,
):
    ctx = lax.axis_index("ctx")
    z, x = ctx // X, ctx % X
    y, c, y_a, y_b, y_far = y_sides(ys)
    head = y * CORES + c
    own_blocks, rows, half = own_ref.shape
    picks, block_len, full = keys.shape
    local_heads, unused, nope = up_ref.shape[0], up_ref.shape[2], up_ref.shape[1]
    latent = up_ref.shape[2]
    width = query.shape[2]
    steps = zs // 2
    halves = 2
    part_blocks = own_blocks // halves
    plan = z_plan(steps)
    jumps = sorted({d - f for hop in plan for d, f in hop})

    def z_device(shift):
        return (lax.rem(z + shift + zs, zs) * X + x, head)

    to_a, to_b, to_far = [(ctx, k * CORES + c) for k in (y_a, y_b, y_far)]
    to_core = (ctx, y * CORES + 1 - c)
    x_peers = []
    for dx in range(X):
        for dc in range(CORES):
            if dx or dc:
                tx, tc = lax.rem(x + dx, X), lax.rem(c + dc, CORES)
                x_peers.append((dx, dc, tx, tc, (z * X + tx, y * CORES + tc)))
    loads = [
        pltpu.make_async_copy(raw_hbm, raw_ref, load_sem.at[0]),
        pltpu.make_async_copy(up_hbm, up_ref, load_sem.at[1]),
    ]
    for load in loads:
        load.start()

    row_to = lax.rem(head, ys) * CORES + head // ys
    row_from = c * ys + y
    moves = row_to != head

    entry = cache_ref.shape[2]
    mine_rows = pl.ds(pl.multiple_of(y * rows, rows), rows)

    @pl.when(c == 0)
    def low_half():
        own_ref[...] = cache_ref[:, mine_rows, :half]

    @pl.when(c == 1)
    def high_half():
        own_ref[:, :, : entry - half] = cache_ref[:, mine_rows, half:]
        own_ref[:, :, entry - half : width - half] = jnp.zeros(
            (own_blocks, rows, width - entry), own_ref.dtype
        )
        own_ref[:, :, width - half :] = index_ref[:, mine_rows, :]

    z_peers = [z_device(sign * jump) for jump in jumps for sign in (1, -1)]
    barrier = pltpu.get_barrier_semaphore()

    @pl.when(moves)
    def greet_movers():
        for other in (row_to, row_from):
            pl.semaphore_signal(barrier, inc=1, device_id=(ctx, other), device_id_type=MESH)

    enter(z_peers + [to_a, to_b, to_far] + [p[4] for p in x_peers], 2 * moves.astype(jnp.int32))

    pending = []

    def start(copy):
        copy.start()
        pending.append(copy)

    def piece(direction, k, i):
        span = pl.ds(i * part_blocks, part_blocks)
        if k == 0:
            return own_ref.at[span]
        if direction == 0 or k == steps:
            return z_low[k - 1].at[span]
        return z_high[k - 1].at[span]

    def z_copy(direction, d, f, i):
        return remote(
            piece(direction, f, i), piece(direction, d, i),
            zs_sem.at[direction, d - 1, i], zr_sem.at[direction, d - 1, i],
            z_device(d - f if direction == 0 else f - d),
        )

    def z_lanes(hop):
        return [
            (direction, d, f, i)
            for i in range(halves)
            for d, f in plan[hop]
            for direction in range(2)
            if d < steps or i == direction
        ]

    for lane in z_lanes(0):
        start(z_copy(*lane))

    shards = zs * X
    lane_id = lax.broadcasted_iota(jnp.int32, (8, LANES), 1)
    line_id = lax.broadcasted_iota(jnp.int32, (8, LANES), 0)

    def ring(shard):
        behind = lax.rem(lax.div(shard, X) - z + zs, zs)
        return behind, jnp.minimum(behind, zs - behind)

    lane_shard = jnp.minimum(lane_id, shards - 1)
    lane_behind, lane_far = ring(lane_shard)
    lane_key = lane_far * LANES + lane_shard
    requests, places = [], []
    for row in range(CORES):
        request = jnp.zeros((8, LANES), jnp.int32)
        place = jnp.zeros((8, LANES), jnp.int32)
        for m in range(picks):
            block = picked_ref[row, m]
            shard = lax.rem(block, shards)
            key = ring(shard)[1] * LANES + shard
            request = jnp.where(lane_id == shard, lax.div(block, shards) + 1, request)
            place = place + jnp.where(key < lane_key, 1, 0)
        requests.append(request)
        places.append(jnp.where(request > 0, place + 1, 0))
    table = jnp.zeros((8, LANES), jnp.int32)
    for row in range(CORES):
        table = jnp.where(line_id == row, jnp.maximum(requests[row] - 1, 0), table)
        table = jnp.where(line_id == 2 * CORES + row, requests[row], table)
        table = jnp.where(line_id == 3 * CORES + row, places[row], table)
    tabs_v[x] = table
    for dx in range(1, X):
        tx = lax.rem(x + dx, X)
        start(remote(tabs_v.at[x], tabs_v.at[x], ts_sem.at[dx - 1], tr_sem.at[dx - 1], (z * X + tx, head)))
    def sources(hop):
        if hop == 0:
            return [(own_ref, 0)]
        found = []
        for d, f in plan[hop - 1]:
            found.append((z_low[d - 1], zs - d))
            if d < steps:
                found.append((z_high[d - 1], d))
        return found

    def x_step(k):
        found = [(ref, rel, lax.rem(z + rel, zs) * X + x) for ref, rel in sources(k)]
        for n, (dx, dc, tx, tc, device) in enumerate(x_peers):
            for i, (ref, rel, shard) in enumerate(found):
                x_out[k, n, i] = ref[tabs_s[tx, tc, shard]]
            span = pl.ds(0, len(found))
            start(remote(x_out.at[k, n, span], x_in.at[k, n, span], xs_sem.at[k, n], xr_sem.at[k, n], device))
        for ref, rel, shard in found:
            x_all[rel * X + x, c] = ref[tabs_s[x, c, shard]]

    def x_finish(k):
        for n, (dx, dc, tx, tc, device) in enumerate(x_peers):
            fx, fc = lax.rem(x + X - dx, X), lax.rem(c + dc, CORES)
            span = pl.ds(0, len(sources(k)))
            remote(x_out.at[k, n, span], x_in.at[k, n, span], xs_sem.at[k, n], xr_sem.at[k, n], device).wait_recv()
            for i, (unused_ref, rel) in enumerate(sources(k)):
                x_all[rel * X + fx, fc] = x_in[k, n, i]

    chunks = ys_sem.shape[1]
    chunk = picks // chunks
    straight = chunks - DIRECT

    def y_copy(kind, owner, j, device):
        here = pl.ds(pl.multiple_of(owner * rows, rows), rows)
        ref = keys.at[pl.ds(j * chunk, chunk), here, pl.ds(0, width)]
        return remote(ref, ref, ys_sem.at[kind, j], yr_sem.at[kind, j], device)

    def index_copy(kind, owner, device):
        here = pl.ds(pl.multiple_of(owner * rows, rows), rows)
        ref = keys.at[:, here, pl.ds(width, full - width)]
        return remote(ref, ref, is_sem.at[kind], ir_sem.at[kind], device)

    def y_start(j):
        def place(m, carry):
            slot = slots_s[m, 0]
            for fc in range(CORES):
                keys[m, pl.ds(pl.multiple_of(y * rows, rows), rows), fc * half : (fc + 1) * half] = x_all[slot, fc]
            return carry

        lax.fori_loop(j * chunk, (j + 1) * chunk, place, 0)
        start(y_copy(0, y, j, to_a))
        start(y_copy(1, y, j, to_b))
        if j >= straight:
            start(y_copy(2, y, j, to_far))

    def y_forward(j):
        y_copy(0, y_b, j, to_a).wait_recv()
        start(y_copy(2, y_b, j, to_a))

    def make_query(h):
        q_ref[h] = raw_ref[h].T
        for mine, ref in ((True, query), (False, query_out)):
            at = pl.ds(pl.multiple_of((c if mine else 1 - c) * block_len, block_len), block_len)
            ref[h, :, :latent] = jnp.dot(
                q_ref[h, at, :nope], up_ref[h], preferred_element_type=jnp.float32
            ).astype(query.dtype)
            entry_end = latent + q_ref.shape[2] - nope
            ref[h, :, latent:entry_end] = q_ref[h, at, nope:]
            ref[h, :, entry_end:] = jnp.zeros((block_len, width - entry_end), query.dtype)

    my_place = jnp.where(c == 0, places[0], places[1])

    def tables_wait():
        for dx in range(1, X):
            fx = lax.rem(x + X - dx, X)
            remote(tabs_v.at[fx], tabs_v.at[fx], ts_sem.at[dx - 1], tr_sem.at[dx - 1], to_a).wait_recv()
        lane_slot = lane_behind * X + lax.rem(lane_shard, X)
        for i in range(picks // 8):
            hit = my_place == line_id + (i * 8 + 1)
            slot = jnp.sum(jnp.where(hit, lane_slot, 0), axis=1, keepdims=True)
            slots_v[i * 8 : (i + 1) * 8, :] = jnp.broadcast_to(slot, (8, LANES))
        slots_copy = pltpu.make_async_copy(slots_v, slots_s, local_sem)
        slots_copy.start()
        slots_copy.wait()
        to_scalar = pltpu.make_async_copy(tabs_v, tabs_s, local_sem)
        to_scalar.start()
        to_scalar.wait()
        tabs_ref[...] = tabs_v[...]

    def prepare():
        @pl.when(moves)
        def move():
            remote(iq_ref, my_iq_ref, ms_sem.at[0], mr_sem.at[0], (ctx, row_to)).start()
            remote(iw_ref, my_iw_ref, ms_sem.at[1], mr_sem.at[1], (ctx, row_to)).start()

        @pl.when(jnp.logical_not(moves))
        def stay():
            my_iq_ref[...] = iq_ref[...]
            my_iw_ref[...] = iw_ref[...]

        own_shard = lax.rem(position_ref[c], shards)
        own_place = jnp.sum(jnp.where(lane_id == own_shard, my_place, 0), axis=1, keepdims=True) - 1
        parts, unused, part_keys = bias_ref.shape
        key_id = lax.broadcasted_iota(jnp.int32, (8, part_keys), 1)
        token = lax.broadcasted_iota(jnp.int32, (8, part_keys), 0)
        for j in range(parts):
            pick_of = lax.div(key_id, block_len) + j * (part_keys // block_len)
            inside = lax.rem(key_id, block_len)
            for i in range(block_len // 8):
                after = (pick_of == own_place) & (inside > token + i * 8)
                bias_ref[j, i * 8 : (i + 1) * 8, :] = jnp.where(after, -jnp.inf, 0.0)
            mask_ref[:, j * part_keys : (j + 1) * part_keys] = bias_ref[j, mine_rows, :]

    swap = remote(query_out, query.at[pl.ds(local_heads, local_heads)], qs_sem, qr_sem, to_core)
    hops = len(plan)
    arrived = X
    started = forwarded = 0
    made = 0
    for hop in range(1, hops + 1):
        if hop == 1:
            for load in loads:
                load.wait()
        while made * hops < local_heads * hop:
            make_query(made)
            made += 1
        if hop == hops:
            start(swap)
        for direction, d, f, i in z_lanes(hop - 1):
            z_copy(direction, d, f, i).wait_recv()
            if hop < hops:
                for lane in z_lanes(hop):
                    if lane[0] == direction and lane[2] == d and lane[3] == i:
                        start(z_copy(*lane))
        if hop == 1:
            tables_wait()
            x_step(0)
        x_step(hop)
        if hop == 1:
            prepare()
        x_finish(hop - 1)
        before = started
        ready = max(0, picks - (shards - arrived)) // chunk
        arrived += X * len(sources(hop))
        while started < ready:
            y_start(started)
            started += 1
        while forwarded < min(before, straight):
            y_forward(forwarded)
            forwarded += 1
    x_finish(hops)
    before = started
    while started < chunks:
        y_start(started)
        started += 1
    while forwarded < min(before, straight):
        y_forward(forwarded)
        forwarded += 1
    start(index_copy(0, y, to_a))
    start(index_copy(1, y, to_b))
    start(index_copy(2, y, to_far))
    swap.wait_recv()

    group = logits_a.shape[0] // block_len
    groups = query.shape[0] // group
    parts = expo.shape[0]
    per_part = picks // parts
    pieces = per_part * block_len // LANES

    def dot(j, g, dst):
        block = query[pl.ds(g * group, group)].reshape(group * block_len, width)
        these = keys[pl.ds(j * per_part, per_part), :, :width].reshape(per_part * block_len, width)
        dst[...] = lax.dot_general(
            block, these, (((1,), (1,)), ((), ())), preferred_element_type=jnp.float32
        )

    def soften(j, g, src):
        for i in range(block_len // 8):
            bias = bias_ref[j, i * 8 : (i + 1) * 8, :]
            for h in range(group):
                value = src[h * block_len + i * 8 : h * block_len + i * 8 + 8, :] * scale + bias
                cuts = [value[:, n * LANES : (n + 1) * LANES] for n in range(pieces)]
                high = functools.reduce(jnp.maximum, cuts)
                high = jnp.maximum(high, -1e30)
                raised = [jnp.exp2(cut - high) for cut in cuts]
                at = pl.ds(pl.multiple_of((g * group + h) * block_len + i * 8, 8), 8)
                for n in range(pieces):
                    expo[j, at, n * LANES : (n + 1) * LANES] = raised[n]
                top[j, at, :] = high
                total[j, at, :] = functools.reduce(jnp.add, raised)

    def attend_chunk(j, carry):
        for i in range(chunks // parts):
            here = j * (chunks // parts) + i

            @pl.when(here >= straight)
            def not_forwarded():
                y_copy(0, y_b, here, to_a).wait_recv()

            y_copy(1, y_a, here, to_a).wait_recv()
            y_copy(2, y_far, here, to_a).wait_recv()
        dot(j, 0, logits_a)

        for p in range(groups // 2):
            dot(j, 2 * p + 1, logits_b)
            soften(j, 2 * p, logits_a)
            if p + 1 < groups // 2:
                dot(j, 2 * p + 2, logits_a)
            soften(j, 2 * p + 1, logits_b)
        return carry

    lax.fori_loop(0, parts, attend_chunk, 0)
    def sum_heads(at):
        def one(h, sums):
            here = pl.ds(pl.multiple_of(h * block_len + at, 8), 8)
            highs = [top[j, here, :] for j in range(parts)]
            high = jnp.max(functools.reduce(jnp.maximum, highs), axis=1, keepdims=True)
            factors = [jnp.exp2(value - high) for value in highs]
            mass = functools.reduce(
                jnp.add, [total[j, here, :] * factors[j] for j in range(parts)]
            )
            share = 1.0 / jnp.sum(mass, axis=1, keepdims=True)
            sums = list(sums)
            for j in range(parts):
                factor = factors[j] * share
                for n in range(pieces):
                    sums[j * pieces + n] += expo[j, here, n * LANES : (n + 1) * LANES] * factor
            return tuple(sums)

        zero = jnp.zeros((8, LANES), jnp.float32)
        return lax.fori_loop(0, query.shape[0], one, (zero,) * (parts * pieces), unroll=4)

    def quarter(owner, dst):
        for i in range(rows // 8):
            sums = sum_heads(pl.multiple_of(owner * rows + i * 8, 8))
            for n, value in enumerate(sums):
                dst[i * 8 : (i + 1) * 8, n * LANES : (n + 1) * LANES] = value

    for n, (owner, device) in enumerate(((y_far, to_far), (y_a, to_a), (y_b, to_b))):
        quarter(owner, part.at[n])
        start(remote(part.at[n], t_in.at[n], ps_sem.at[n], pr_sem.at[n], device))
    quarter(y, target_ref)
    index_copy(0, y_b, to_a).wait_recv()
    index_copy(1, y_a, to_a).wait_recv()
    index_copy(2, y_far, to_a).wait_recv()
    index_keys_ref[...] = keys[:, :, width:]
    for n in range(ys - 1):
        remote(part.at[n], t_in.at[n], ps_sem.at[n], pr_sem.at[n], to_a).wait_recv()
    target_ref[...] = (target_ref[...] + t_in[0] + t_in[1] + t_in[2]) * (1.0 / heads_total)
    @pl.when(moves)
    def moved():
        for n, (src, dst) in enumerate(((iq_ref, my_iq_ref), (iw_ref, my_iw_ref))):
            copy = remote(src, dst, ms_sem.at[n], mr_sem.at[n], (ctx, row_to))
            copy.wait_send()
            copy.wait_recv()

    my_iw_ref[...] = my_iw_ref[...] * index_ref.shape[2] ** (-0.5)
    for copy in pending:
        copy.wait_send()


def attend(picked, position, cache, index_key, queries, up_weight, index_query, index_weight, zs, ys, heads_total):
    own_blocks, block_len, entry = cache.shape
    query_rows, picks = picked.shape
    rows = block_len // ys
    local_heads, q_width, tokens = queries.shape
    scale = q_width ** (-0.5) * 1.4426950408889634
    nope, latent = up_weight.shape[1:]
    width = -(-entry // LANES) * LANES
    full = width + index_key.shape[2]
    half = full // CORES
    parts = 4
    part_keys = picks * block_len // parts
    heads = local_heads * CORES
    steps = zs // 2
    hops = len(z_plan(steps))
    peers = X * CORES - 1
    chunks = 8
    group = 8
    keep = cache.dtype
    single = jnp.float32
    dma = pltpu.SemaphoreType.DMA
    return pl.pallas_call(
        functools.partial(attend_kernel, zs, ys, scale, heads_total),
        out_shape=(
            jax.ShapeDtypeStruct((rows, picks * block_len), single),
            jax.ShapeDtypeStruct((picks, block_len, full - width), keep),
            jax.ShapeDtypeStruct((X, 8, LANES), jnp.int32),
            jax.ShapeDtypeStruct((rows, picks * block_len), single),
            jax.ShapeDtypeStruct(index_query.shape, index_query.dtype),
            jax.ShapeDtypeStruct(index_weight.shape, index_weight.dtype),
        ),
        in_specs=[pl.BlockSpec(memory_space=pltpu.SMEM)] * 2
        + [pl.BlockSpec(memory_space=pltpu.VMEM)] * 2
        + [pl.BlockSpec(memory_space=pl.ANY)] * 2
        + [pl.BlockSpec(memory_space=pltpu.VMEM)] * 2,
        out_specs=[pl.BlockSpec(memory_space=pltpu.VMEM)] * 6,
        scratch_shapes=[
            pltpu.VMEM(queries.shape, keep),
            pltpu.VMEM(up_weight.shape, keep),
            dma((2,)),
            pltpu.VMEM((X, 8, LANES), jnp.int32),
            pltpu.SMEM((X, 8, LANES), jnp.int32),
            pltpu.VMEM((picks, LANES), jnp.int32),
            pltpu.SMEM((picks, LANES), jnp.int32),
            pltpu.VMEM((own_blocks, rows, half), keep),
            pltpu.VMEM((local_heads, tokens, q_width), keep),
            pltpu.VMEM((parts, block_len, part_keys), single),
            [pltpu.VMEM((own_blocks, rows, half), keep) for k in range(steps)],
            [pltpu.VMEM((own_blocks, rows, half), keep) for k in range(steps - 1)],
            pltpu.VMEM((hops + 1, peers, 4, rows, half), keep),
            pltpu.VMEM((hops + 1, peers, 4, rows, half), keep),
            pltpu.VMEM((zs * X, CORES, rows, half), keep),
            pltpu.VMEM((picks, block_len, full), keep),
            pltpu.VMEM((heads, block_len, width), keep),
            pltpu.VMEM((local_heads, block_len, width), keep),
            pltpu.VMEM((group * block_len, part_keys), single),
            pltpu.VMEM((group * block_len, part_keys), single),
            pltpu.VMEM((parts, heads * block_len, part_keys), single),
            pltpu.VMEM((parts, heads * block_len, LANES), single),
            pltpu.VMEM((parts, heads * block_len, LANES), single),
            pltpu.VMEM((3, rows, picks * block_len), single),
            pltpu.VMEM((3, rows, picks * block_len), single),
            dma((2, steps, 2)), dma((2, steps, 2)),
            dma((hops + 1, peers)), dma((hops + 1, peers)),
            dma((X - 1,)), dma((X - 1,)),
            dma((3, chunks)), dma((3, chunks)), dma((3,)), dma((3,)),
            dma, dma, dma((3,)), dma((3,)), dma((2,)), dma((2,)), dma,
        ],
        compiler_params=pltpu.CompilerParams(
            collective_id=0, has_side_effects=True, vmem_limit_bytes=56 * 2**20
        ),
        name="attend",
    )(picked, position, cache, index_key, queries, up_weight, index_query, index_weight)


def return_kernel(
    zs, ys, tabs_ref, ids_ref, part_ref, weight_ref, out_ref, home_ref,
    y_out, y_in, quarter, x_out, x_in, z_out, z_in, id_out, id_in, mine, theirs,
    ws_sem, wr_sem, is_sem, ir_sem, ys_sem, yr_sem, xs_sem, xr_sem, zs_sem, zr_sem, cs_sem, cr_sem, os_sem, or_sem,
):
    ctx = lax.axis_index("ctx")
    z, x = ctx // X, ctx % X
    y, c, y_a, y_b, y_far = y_sides(ys)
    head = y * CORES + c
    picks, block_len, width = part_ref.shape
    own_blocks = out_ref.shape[0]
    rows = block_len // ys
    to_a, to_b, to_far = (ctx, y_a * CORES + c), (ctx, y_b * CORES + c), (ctx, y_far * CORES + c)
    to_core = (ctx, y * CORES + 1 - c)
    x_peers = [(lax.rem(x + d, X), (z * X + lax.rem(x + d, X), head)) for d in range(1, X)]
    z_peers = [(lax.rem(z + d, zs), (lax.rem(z + d, zs) * X + x, head)) for d in range(1, zs)]
    home = c * ys + y
    comes_from = lax.rem(head, ys) * CORES + head // ys
    moves = home != head
    barrier = pltpu.get_barrier_semaphore()

    @pl.when(moves)
    def greet_movers():
        for other in (home, comes_from):
            pl.semaphore_signal(barrier, inc=1, device_id=(ctx, other), device_id_type=MESH)

    enter(
        [to_a, to_b, to_far, to_core] + [p[1] for p in x_peers] + [p[1] for p in z_peers],
        2 * moves.astype(jnp.int32),
    )

    def span(k):
        return pl.ds(pl.multiple_of(k * rows, rows), rows)

    y_copies = []
    order = sorted(range(1, zs), key=lambda d: -min(d, zs - d))
    line = lax.broadcasted_iota(jnp.int32, id_out.shape, 0)
    lane = lax.broadcasted_iota(jnp.int32, id_out.shape, 1)
    asked = jnp.zeros(id_out.shape, jnp.int32)
    for fx in range(X):
        row = jnp.where(
            c == 0, ids_ref[fx, 2 * CORES : 2 * CORES + 1, :], ids_ref[fx, 2 * CORES + 1 : 2 * CORES + 2, :]
        )
        asked = jnp.where(line == fx, jnp.broadcast_to(row, id_out.shape), asked)
    id_out[...] = asked
    id_in[z] = asked
    for n, (owner, device) in enumerate(((y_far, to_far), (y_a, to_a), (y_b, to_b))):
        y_out[n] = part_ref[:, span(owner), :].astype(y_out.dtype)
        copy = remote(y_out.at[n], y_in.at[n], ys_sem.at[n], yr_sem.at[n], device)
        copy.start()
        y_copies.append(copy)
    weight_copy = remote(weight_ref, home_ref, ws_sem, wr_sem, (ctx, home))

    @pl.when(moves)
    def move():
        weight_copy.start()

    @pl.when(jnp.logical_not(moves))
    def stay():
        home_ref[...] = weight_ref[...]

    for d in order:
        copy = remote(id_out, id_in.at[z], is_sem.at[d - 1], ir_sem.at[d - 1], z_peers[d - 1][1])
        copy.start()
        y_copies.append(copy)
    for n in range(ys - 1):
        remote(y_out.at[n], y_in.at[n], ys_sem.at[n], yr_sem.at[n], to_a).wait_recv()
    quarter[...] = (
        part_ref[:, span(y), :]
        + y_in[0].astype(jnp.float32)
        + y_in[1].astype(jnp.float32)
        + y_in[2].astype(jnp.float32)
    )

    def choose(tx, dst):
        def body(owner, carry):
            place = tabs_ref[x, 3 * CORES + c, owner * X + tx]
            value = quarter[jnp.maximum(place - 1, 0)]
            dst[owner] = jnp.where(place > 0, value, 0.0).astype(dst.dtype)
            return carry

        lax.fori_loop(0, zs, body, 0)

    x_copies = []
    for n, (tx, device) in enumerate(x_peers):
        choose(tx, x_out.at[n])
        copy = remote(x_out.at[n], x_in.at[x], xs_sem.at[n], xr_sem.at[n], device)
        copy.start()
        x_copies.append(copy)
    choose(x, x_in.at[x])
    for n in range(X - 1):
        fx = lax.rem(x + X - n - 1, X)
        remote(x_out.at[n], x_in.at[fx], xs_sem.at[n], xr_sem.at[n], to_a).wait_recv()

    def gather(owner, dst):
        for fx in range(X):
            dst[fx * rows : (fx + 1) * rows] = x_in[fx, owner]

    z_copies = []
    for d in order:
        tz, device = z_peers[d - 1]
        gather(tz, z_out.at[d - 1])
        copy = remote(z_out.at[d - 1], z_in.at[z], zs_sem.at[d - 1], zr_sem.at[d - 1], device)
        copy.start()
        z_copies.append(copy)
    gather(z, z_in.at[z])
    for d in order:
        fz = lax.rem(z + zs - d, zs)
        remote(id_out, id_in.at[fz], is_sem.at[d - 1], ir_sem.at[d - 1], to_a).wait_recv()
        remote(z_out.at[d - 1], z_in.at[fz], zs_sem.at[d - 1], zr_sem.at[d - 1], to_a).wait_recv()

    def add(fz, totals):
        ids = jnp.sum(jnp.where(lane == ctx, id_in[fz], 0), axis=1, keepdims=True)
        totals = list(totals)
        for fx in range(X):
            value = z_in[fz, fx * rows : (fx + 1) * rows].astype(jnp.float32)
            block = jnp.broadcast_to(ids[fx : fx + 1], value.shape)
            for r in range(own_blocks):
                totals[r] = totals[r] + jnp.where(block == r + 1, value, 0.0)
        return tuple(totals)

    totals = lax.fori_loop(
        0, zs, add, tuple(jnp.zeros((rows, width), jnp.float32) for r in range(own_blocks))
    )
    for r in range(own_blocks):
        mine[r] = totals[r]
    core = remote(mine, theirs, cs_sem, cr_sem, to_core)
    core.start()
    core.wait_recv()
    out_ref[:, span(y), :] = mine[...] + theirs[...]
    o_copies = []
    for n, device in enumerate((to_a, to_b, to_far)):
        ref = out_ref.at[:, span(y), :]
        copy = remote(ref, ref, os_sem.at[n], or_sem.at[n], device)
        copy.start()
        o_copies.append(copy)
    for n, fy in enumerate((y_b, y_a, y_far)):
        ref = out_ref.at[:, span(fy), :]
        remote(ref, ref, os_sem.at[n], or_sem.at[n], to_a).wait_recv()
    @pl.when(moves)
    def moved():
        weight_copy.wait_send()
        weight_copy.wait_recv()

    for copy in y_copies + [core] + x_copies + z_copies + o_copies:
        copy.wait_send()


def give_back(tables, key_part, weight_part, zs, ys, own_blocks):
    picks, block_len, width = key_part.shape
    rows = block_len // ys
    half = jnp.bfloat16
    dma = pltpu.SemaphoreType.DMA
    return pl.pallas_call(
        functools.partial(return_kernel, zs, ys),
        out_shape=(
            jax.ShapeDtypeStruct((own_blocks, block_len, width), jnp.float32),
            jax.ShapeDtypeStruct(weight_part.shape, jnp.float32),
        ),
        in_specs=[
            pl.BlockSpec(memory_space=pltpu.SMEM),
            pl.BlockSpec(memory_space=pltpu.VMEM),
            pl.BlockSpec(memory_space=pltpu.VMEM),
            pl.BlockSpec(memory_space=pltpu.VMEM),
        ],
        out_specs=[pl.BlockSpec(memory_space=pltpu.VMEM)] * 2,
        scratch_shapes=[
            pltpu.VMEM((3, picks, rows, width), half),
            pltpu.VMEM((3, picks, rows, width), half),
            pltpu.VMEM((picks, rows, width), jnp.float32),
            pltpu.VMEM((X - 1, zs, rows, width), half),
            pltpu.VMEM((X, zs, rows, width), half),
            pltpu.VMEM((zs - 1, X * rows, width), half),
            pltpu.VMEM((zs, X * rows, width), half),
            pltpu.VMEM((8, LANES), jnp.int32),
            pltpu.VMEM((zs, 8, LANES), jnp.int32),
            pltpu.VMEM((own_blocks, rows, width), jnp.float32),
            pltpu.VMEM((own_blocks, rows, width), jnp.float32),
            dma, dma, dma((zs - 1,)), dma((zs - 1,)),
            dma((3,)), dma((3,)), dma((X - 1,)), dma((X - 1,)), dma((zs - 1,)), dma((zs - 1,)),
            dma, dma, dma((3,)), dma((3,)),
        ],
        compiler_params=pltpu.CompilerParams(
            collective_id=2, has_side_effects=True, vmem_limit_bytes=40 * 2**20
        ),
        name="give_back",
    )(tables, tables, key_part, weight_part)


def masked_softmax(values, allowed):
    shifted = jnp.where(allowed, values, -jnp.inf)
    row_max = jnp.max(shifted, axis=-1, keepdims=True)
    expo = jnp.exp(shifted - row_max)
    return expo / jnp.sum(expo, axis=-1, keepdims=True)


def local(
    queries,
    up_weight,
    index_query,
    index_weight,
    cache_entry,
    index_key,
    block_position,
    picked_blocks,
):
    owners = lax.axis_size("ctx")
    head_devices = lax.axis_size("head")
    zs, ys = owners // X, head_devices // CORES
    picks = picked_blocks.shape[1]
    own_blocks, unused, block_len, entry_width = cache_entry.shape
    index_width = index_key.shape[3]
    key_count = picks * block_len
    rows = block_len // ys
    local_heads = queries.shape[1]
    target, index_keys, tables, mask, my_index_query, my_index_weight = attend(
        picked_blocks, block_position, cache_entry[:, 0], index_key[:, 0], jnp.transpose(queries, (1, 2, 0)), up_weight,
        index_query, index_weight, zs, ys, local_heads * head_devices,
    )
    index_keys = index_keys.reshape(key_count, index_width)
    my_allowed = mask == 0.0
    raw = jnp.einsum("ijd,sd->ijs", my_index_query, index_keys, preferred_element_type=jnp.float32)
    positive = jnp.maximum(raw, 0.0)
    score = jnp.sum(my_index_weight[:, :, None] * positive, axis=1)
    soft = masked_softmax(score, my_allowed)
    score_grad = jnp.where(my_allowed, soft - target, 0.0)
    weight_part = jnp.sum(score_grad[:, None, :] * positive, axis=2) * index_width ** (-0.5)
    coefficient = jnp.where(
        raw > 0, score_grad[:, None, :] * my_index_weight[:, :, None], 0.0
    ).astype(jnp.bfloat16)
    key_part = jnp.einsum(
        "ijs,ijd->sd", coefficient, my_index_query, preferred_element_type=jnp.float32
    )
    key_grad, weight_grad = give_back(
        tables, key_part.reshape(picks, block_len, index_width), weight_part, zs, ys, own_blocks
    )
    key_grad = key_grad.reshape(own_blocks, 1, block_len, index_width)
    return (key_grad, weight_grad)


def solution(mesh):
    return jax.shard_map(
        local,
        mesh=mesh,
        in_specs=(
            P("ctx", "head", None),
            P("head", None, None),
            P(("ctx", "head"), None, None),
            P(("ctx", "head"), None),
            P(None, "ctx", None, None),
            P(None, "ctx", None, None),
            P("ctx"),
            P("ctx", None),
        ),
        out_specs=(P(None, "ctx", None, None), P(("ctx", "head"), None)),
        check_vma=False,
    )
```

```python
import functools

import jax
import jax.numpy as jnp
from jax import lax
from jax.experimental import pallas as pl
from jax.experimental.pallas import tpu as pltpu
from jax.sharding import PartitionSpec as P

MESH = pl.DeviceIdType.MESH
X = 4
CORES = 2
LANES = 128
JUMP = 1


def z_plan(steps):
    jump = min(JUMP, steps)
    plan = []
    for hop in range(1, max(jump, steps - jump + 2)):
        plan.append(
            ([(hop, hop - 1)] if hop < jump else [])
            + ([(jump + hop - 1, jump + hop - 2 if hop > 1 else 0)] if jump + hop - 1 <= steps else [])
        )
    return plan


def remote(src, dst, s_sem, r_sem, device):
    return pltpu.make_async_remote_copy(
        src_ref=src, dst_ref=dst, send_sem=s_sem, recv_sem=r_sem, device_id=device, device_id_type=MESH
    )


def enter(peers, more=0):
    barrier = pltpu.get_barrier_semaphore()
    for peer in peers:
        pl.semaphore_signal(barrier, inc=1, device_id=peer, device_id_type=MESH)
    pl.semaphore_wait(barrier, len(peers) + more)


def y_sides(ys):
    head = lax.axis_index("head")
    y, c = head // CORES, head % CORES
    step = 1 - 2 * c
    return y, c, lax.rem(y + step + ys, ys), lax.rem(y - step + ys, ys), lax.rem(y + 2, ys)


def attend_kernel(
    zs, ys, scale, heads_total,
    picked_ref, position_ref, cache_ref, index_ref, raw_hbm, up_hbm, iq_ref, iw_ref,
    target_ref, index_keys_ref, tabs_ref, mask_ref, my_iq_ref, my_iw_ref,
    raw_ref, up_ref, load_sem, tabs_v, tabs_s, slots_v, slots_s, own_ref, q_ref, bias_ref, z_low, z_high, x_out, x_in, x_all, keys, query, query_out,
    logits_a, logits_b, expo, top, total, part, t_in,
    zs_sem, zr_sem, xs_sem, xr_sem, ts_sem, tr_sem, ys_sem, yr_sem, is_sem, ir_sem, qs_sem, qr_sem, ps_sem, pr_sem, ms_sem, mr_sem, local_sem,
):
    ctx = lax.axis_index("ctx")
    z, x = ctx // X, ctx % X
    y, c, y_a, y_b, y_far = y_sides(ys)
    head = y * CORES + c
    own_blocks, rows, half = own_ref.shape
    picks, block_len, full = keys.shape
    local_heads, unused, nope = up_ref.shape[0], up_ref.shape[2], up_ref.shape[1]
    latent = up_ref.shape[2]
    width = query.shape[2]
    steps = zs // 2
    halves = 2
    part_blocks = own_blocks // halves
    plan = z_plan(steps)
    jumps = sorted({d - f for hop in plan for d, f in hop})

    def z_device(shift):
        return (lax.rem(z + shift + zs, zs) * X + x, head)

    to_a, to_b, to_far = [(ctx, k * CORES + c) for k in (y_a, y_b, y_far)]
    to_core = (ctx, y * CORES + 1 - c)
    x_peers = []
    for dx in range(X):
        for dc in range(CORES):
            if dx or dc:
                tx, tc = lax.rem(x + dx, X), lax.rem(c + dc, CORES)
                x_peers.append((dx, dc, tx, tc, (z * X + tx, y * CORES + tc)))
    loads = [
        pltpu.make_async_copy(raw_hbm, raw_ref, load_sem.at[0]),
        pltpu.make_async_copy(up_hbm, up_ref, load_sem.at[1]),
    ]
    for load in loads:
        load.start()

    row_to = lax.rem(head, ys) * CORES + head // ys
    row_from = c * ys + y
    moves = row_to != head

    entry = cache_ref.shape[2]
    mine_rows = pl.ds(pl.multiple_of(y * rows, rows), rows)

    @pl.when(c == 0)
    def low_half():
        own_ref[...] = cache_ref[:, mine_rows, :half]

    @pl.when(c == 1)
    def high_half():
        own_ref[:, :, : entry - half] = cache_ref[:, mine_rows, half:]
        own_ref[:, :, entry - half : width - half] = jnp.zeros(
            (own_blocks, rows, width - entry), own_ref.dtype
        )
        own_ref[:, :, width - half :] = index_ref[:, mine_rows, :]

    z_peers = [z_device(sign * jump) for jump in jumps for sign in (1, -1)]
    barrier = pltpu.get_barrier_semaphore()

    @pl.when(moves)
    def greet_movers():
        for other in (row_to, row_from):
            pl.semaphore_signal(barrier, inc=1, device_id=(ctx, other), device_id_type=MESH)

    enter(z_peers + [to_a, to_b, to_far] + [p[4] for p in x_peers], 2 * moves.astype(jnp.int32))

    pending = []

    def start(copy):
        copy.start()
        pending.append(copy)

    def piece(direction, k, i):
        span = pl.ds(i * part_blocks, part_blocks)
        if k == 0:
            return own_ref.at[span]
        if direction == 0 or k == steps:
            return z_low[k - 1].at[span]
        return z_high[k - 1].at[span]

    def z_copy(direction, d, f, i):
        return remote(
            piece(direction, f, i), piece(direction, d, i),
            zs_sem.at[direction, d - 1, i], zr_sem.at[direction, d - 1, i],
            z_device(d - f if direction == 0 else f - d),
        )

    def z_lanes(hop):
        return [
            (direction, d, f, i)
            for i in range(halves)
            for d, f in plan[hop]
            for direction in range(2)
            if d < steps or i == direction
        ]

    for lane in z_lanes(0):
        start(z_copy(*lane))

    shards = zs * X
    lane_id = lax.broadcasted_iota(jnp.int32, (8, LANES), 1)
    line_id = lax.broadcasted_iota(jnp.int32, (8, LANES), 0)

    def ring(shard):
        behind = lax.rem(lax.div(shard, X) - z + zs, zs)
        return behind, jnp.minimum(behind, zs - behind)

    lane_shard = jnp.minimum(lane_id, shards - 1)
    lane_behind, lane_far = ring(lane_shard)
    lane_key = lane_far * LANES + lane_shard
    requests, places = [], []
    for row in range(CORES):
        request = jnp.zeros((8, LANES), jnp.int32)
        place = jnp.zeros((8, LANES), jnp.int32)
        for m in range(picks):
            block = picked_ref[row, m]
            shard = lax.rem(block, shards)
            key = ring(shard)[1] * LANES + shard
            request = jnp.where(lane_id == shard, lax.div(block, shards) + 1, request)
            place = place + jnp.where(key < lane_key, 1, 0)
        requests.append(request)
        places.append(jnp.where(request > 0, place + 1, 0))
    table = jnp.zeros((8, LANES), jnp.int32)
    for row in range(CORES):
        table = jnp.where(line_id == row, jnp.maximum(requests[row] - 1, 0), table)
        table = jnp.where(line_id == 2 * CORES + row, requests[row], table)
        table = jnp.where(line_id == 3 * CORES + row, places[row], table)
    tabs_v[x] = table
    for dx in range(1, X):
        tx = lax.rem(x + dx, X)
        start(remote(tabs_v.at[x], tabs_v.at[x], ts_sem.at[dx - 1], tr_sem.at[dx - 1], (z * X + tx, head)))
    def sources(hop):
        if hop == 0:
            return [(own_ref, 0)]
        found = []
        for d, f in plan[hop - 1]:
            found.append((z_low[d - 1], zs - d))
            if d < steps:
                found.append((z_high[d - 1], d))
        return found

    def x_step(k):
        found = [(ref, rel, lax.rem(z + rel, zs) * X + x) for ref, rel in sources(k)]
        for n, (dx, dc, tx, tc, device) in enumerate(x_peers):
            for i, (ref, rel, shard) in enumerate(found):
                x_out[k, n, i] = ref[tabs_s[tx, tc, shard]]
            span = pl.ds(0, len(found))
            start(remote(x_out.at[k, n, span], x_in.at[k, n, span], xs_sem.at[k, n], xr_sem.at[k, n], device))
        for ref, rel, shard in found:
            x_all[rel * X + x, c] = ref[tabs_s[x, c, shard]]

    def x_finish(k):
        for n, (dx, dc, tx, tc, device) in enumerate(x_peers):
            fx, fc = lax.rem(x + X - dx, X), lax.rem(c + dc, CORES)
            span = pl.ds(0, len(sources(k)))
            remote(x_out.at[k, n, span], x_in.at[k, n, span], xs_sem.at[k, n], xr_sem.at[k, n], device).wait_recv()
            for i, (unused_ref, rel) in enumerate(sources(k)):
                x_all[rel * X + fx, fc] = x_in[k, n, i]

    chunks = ys_sem.shape[1]
    chunk = picks // chunks

    def y_copy(kind, owner, j, device):
        here = pl.ds(pl.multiple_of(owner * rows, rows), rows)
        ref = keys.at[pl.ds(j * chunk, chunk), here, pl.ds(0, width)]
        return remote(ref, ref, ys_sem.at[kind, j], yr_sem.at[kind, j], device)

    def index_copy(kind, owner, device):
        here = pl.ds(pl.multiple_of(owner * rows, rows), rows)
        ref = keys.at[:, here, pl.ds(width, full - width)]
        return remote(ref, ref, is_sem.at[kind], ir_sem.at[kind], device)

    def y_start(j):
        def place(m, carry):
            slot = slots_s[m, 0]
            for fc in range(CORES):
                keys[m, pl.ds(pl.multiple_of(y * rows, rows), rows), fc * half : (fc + 1) * half] = x_all[slot, fc]
            return carry

        lax.fori_loop(j * chunk, (j + 1) * chunk, place, 0)
        start(y_copy(0, y, j, to_a))
        start(y_copy(1, y, j, to_b))
        if j == chunks - 1:
            start(y_copy(2, y, j, to_far))

    def y_forward(j):
        y_copy(0, y_b, j, to_a).wait_recv()
        start(y_copy(2, y_b, j, to_a))

    def make_query(h):
        q_ref[h] = raw_ref[h].T
        for mine, ref in ((True, query), (False, query_out)):
            at = pl.ds(pl.multiple_of((c if mine else 1 - c) * block_len, block_len), block_len)
            ref[h, :, :latent] = jnp.dot(
                q_ref[h, at, :nope], up_ref[h], preferred_element_type=jnp.float32
            ).astype(query.dtype)
            entry_end = latent + q_ref.shape[2] - nope
            ref[h, :, latent:entry_end] = q_ref[h, at, nope:]
            ref[h, :, entry_end:] = jnp.zeros((block_len, width - entry_end), query.dtype)

    my_place = jnp.where(c == 0, places[0], places[1])

    def tables_wait():
        for dx in range(1, X):
            fx = lax.rem(x + X - dx, X)
            remote(tabs_v.at[fx], tabs_v.at[fx], ts_sem.at[dx - 1], tr_sem.at[dx - 1], to_a).wait_recv()
        lane_slot = lane_behind * X + lax.rem(lane_shard, X)
        for i in range(picks // 8):
            hit = my_place == line_id + (i * 8 + 1)
            slot = jnp.sum(jnp.where(hit, lane_slot, 0), axis=1, keepdims=True)
            slots_v[i * 8 : (i + 1) * 8, :] = jnp.broadcast_to(slot, (8, LANES))
        slots_copy = pltpu.make_async_copy(slots_v, slots_s, local_sem)
        slots_copy.start()
        slots_copy.wait()
        to_scalar = pltpu.make_async_copy(tabs_v, tabs_s, local_sem)
        to_scalar.start()
        to_scalar.wait()
        tabs_ref[...] = tabs_v[...]

    def prepare():
        @pl.when(moves)
        def move():
            remote(iq_ref, my_iq_ref, ms_sem.at[0], mr_sem.at[0], (ctx, row_to)).start()
            remote(iw_ref, my_iw_ref, ms_sem.at[1], mr_sem.at[1], (ctx, row_to)).start()

        @pl.when(jnp.logical_not(moves))
        def stay():
            my_iq_ref[...] = iq_ref[...]
            my_iw_ref[...] = iw_ref[...]

        own_shard = lax.rem(position_ref[c], shards)
        own_place = jnp.sum(jnp.where(lane_id == own_shard, my_place, 0), axis=1, keepdims=True) - 1
        parts, unused, part_keys = bias_ref.shape
        key_id = lax.broadcasted_iota(jnp.int32, (8, part_keys), 1)
        token = lax.broadcasted_iota(jnp.int32, (8, part_keys), 0)
        for j in range(parts):
            pick_of = lax.div(key_id, block_len) + j * (part_keys // block_len)
            inside = lax.rem(key_id, block_len)
            for i in range(block_len // 8):
                after = (pick_of == own_place) & (inside > token + i * 8)
                bias_ref[j, i * 8 : (i + 1) * 8, :] = jnp.where(after, -jnp.inf, 0.0)
            mask_ref[:, j * part_keys : (j + 1) * part_keys] = bias_ref[j, mine_rows, :]

    swap = remote(query_out, query.at[pl.ds(local_heads, local_heads)], qs_sem, qr_sem, to_core)
    hops = len(plan)
    arrived = X
    started = forwarded = before = 0
    made = 0
    for hop in range(1, hops + 1):
        if hop == 1:
            for load in loads:
                load.wait()
        while made * hops < local_heads * hop:
            make_query(made)
            made += 1
        if hop == hops:
            start(swap)
        for direction, d, f, i in z_lanes(hop - 1):
            z_copy(direction, d, f, i).wait_recv()
            if hop < hops:
                for lane in z_lanes(hop):
                    if lane[0] == direction and lane[2] == d and lane[3] == i:
                        start(z_copy(*lane))
        if hop == 1:
            tables_wait()
            x_step(0)
        x_step(hop)
        if hop == 1:
            prepare()
        x_finish(hop - 1)
        settled, before = before, started
        ready = max(0, picks - (shards - arrived)) // chunk
        arrived += X * len(sources(hop))
        while started < ready:
            y_start(started)
            started += 1
        while forwarded < settled:
            y_forward(forwarded)
            forwarded += 1
    x_finish(hops)
    while started < chunks:
        y_start(started)
        started += 1
    while forwarded < before:
        y_forward(forwarded)
        forwarded += 1
    start(index_copy(0, y, to_a))
    start(index_copy(1, y, to_b))
    start(index_copy(2, y, to_far))
    swap.wait_recv()

    group = logits_a.shape[0] // block_len
    groups = query.shape[0] // group
    parts = expo.shape[0]
    per_part = picks // parts
    pieces = per_part * block_len // LANES

    def dot(j, g, dst):
        block = query[pl.ds(g * group, group)].reshape(group * block_len, width)
        these = keys[pl.ds(j * per_part, per_part), :, :width].reshape(per_part * block_len, width)
        dst[...] = lax.dot_general(
            block, these, (((1,), (1,)), ((), ())), preferred_element_type=jnp.float32
        )

    def soften(j, g, src):
        for i in range(block_len // 8):
            bias = bias_ref[j, i * 8 : (i + 1) * 8, :]
            for h in range(group):
                value = src[h * block_len + i * 8 : h * block_len + i * 8 + 8, :] * scale + bias
                cuts = [value[:, n * LANES : (n + 1) * LANES] for n in range(pieces)]
                high = functools.reduce(jnp.maximum, cuts)
                high = jnp.maximum(high, -1e30)
                raised = [jnp.exp2(cut - high) for cut in cuts]
                at = pl.ds(pl.multiple_of((g * group + h) * block_len + i * 8, 8), 8)
                for n in range(pieces):
                    expo[j, at, n * LANES : (n + 1) * LANES] = raised[n]
                top[j, at, :] = high
                total[j, at, :] = functools.reduce(jnp.add, raised)

    def attend_chunk(j, carry):
        @pl.when(j == 1)
        def forward_rest():
            for late in range(forwarded, chunks - 1):
                y_copy(0, y_b, late, to_a).wait_recv()
                y_copy(2, y_b, late, to_a).start()

        @pl.when(j == parts - 1)
        def last_chunk():
            y_copy(0, y_b, chunks - 1, to_a).wait_recv()

        for i in range(chunks // parts):
            y_copy(1, y_a, j * (chunks // parts) + i, to_a).wait_recv()
            y_copy(2, y_far, j * (chunks // parts) + i, to_a).wait_recv()
        dot(j, 0, logits_a)

        for p in range(groups // 2):
            dot(j, 2 * p + 1, logits_b)
            soften(j, 2 * p, logits_a)
            if p + 1 < groups // 2:
                dot(j, 2 * p + 2, logits_a)
            soften(j, 2 * p + 1, logits_b)
        return carry

    lax.fori_loop(0, parts, attend_chunk, 0)
    def sum_heads(at):
        def one(h, sums):
            here = pl.ds(pl.multiple_of(h * block_len + at, 8), 8)
            highs = [top[j, here, :] for j in range(parts)]
            high = jnp.max(functools.reduce(jnp.maximum, highs), axis=1, keepdims=True)
            factors = [jnp.exp2(value - high) for value in highs]
            mass = functools.reduce(
                jnp.add, [total[j, here, :] * factors[j] for j in range(parts)]
            )
            share = 1.0 / jnp.sum(mass, axis=1, keepdims=True)
            sums = list(sums)
            for j in range(parts):
                factor = factors[j] * share
                for n in range(pieces):
                    sums[j * pieces + n] += expo[j, here, n * LANES : (n + 1) * LANES] * factor
            return tuple(sums)

        zero = jnp.zeros((8, LANES), jnp.float32)
        return lax.fori_loop(0, query.shape[0], one, (zero,) * (parts * pieces), unroll=4)

    def quarter(owner, dst):
        for i in range(rows // 8):
            sums = sum_heads(pl.multiple_of(owner * rows + i * 8, 8))
            for n, value in enumerate(sums):
                dst[i * 8 : (i + 1) * 8, n * LANES : (n + 1) * LANES] = value

    for n, (owner, device) in enumerate(((y_far, to_far), (y_a, to_a), (y_b, to_b))):
        quarter(owner, part.at[n])
        start(remote(part.at[n], t_in.at[n], ps_sem.at[n], pr_sem.at[n], device))
    quarter(y, target_ref)
    index_copy(0, y_b, to_a).wait_recv()
    index_copy(1, y_a, to_a).wait_recv()
    index_copy(2, y_far, to_a).wait_recv()
    index_keys_ref[...] = keys[:, :, width:]
    for n in range(ys - 1):
        remote(part.at[n], t_in.at[n], ps_sem.at[n], pr_sem.at[n], to_a).wait_recv()
    target_ref[...] = (target_ref[...] + t_in[0] + t_in[1] + t_in[2]) * (1.0 / heads_total)
    @pl.when(moves)
    def moved():
        for n, (src, dst) in enumerate(((iq_ref, my_iq_ref), (iw_ref, my_iw_ref))):
            copy = remote(src, dst, ms_sem.at[n], mr_sem.at[n], (ctx, row_to))
            copy.wait_send()
            copy.wait_recv()

    my_iw_ref[...] = my_iw_ref[...] * index_ref.shape[2] ** (-0.5)
    for late in range(forwarded, chunks - 1):
        y_copy(2, y_b, late, to_a).wait_send()
    for copy in pending:
        copy.wait_send()


def attend(picked, position, cache, index_key, queries, up_weight, index_query, index_weight, zs, ys, heads_total):
    own_blocks, block_len, entry = cache.shape
    query_rows, picks = picked.shape
    rows = block_len // ys
    local_heads, q_width, tokens = queries.shape
    scale = q_width ** (-0.5) * 1.4426950408889634
    nope, latent = up_weight.shape[1:]
    width = -(-entry // LANES) * LANES
    full = width + index_key.shape[2]
    half = full // CORES
    parts = 4
    part_keys = picks * block_len // parts
    heads = local_heads * CORES
    steps = zs // 2
    hops = len(z_plan(steps))
    peers = X * CORES - 1
    chunks = 8
    group = 8
    keep = cache.dtype
    single = jnp.float32
    dma = pltpu.SemaphoreType.DMA
    return pl.pallas_call(
        functools.partial(attend_kernel, zs, ys, scale, heads_total),
        out_shape=(
            jax.ShapeDtypeStruct((rows, picks * block_len), single),
            jax.ShapeDtypeStruct((picks, block_len, full - width), keep),
            jax.ShapeDtypeStruct((X, 8, LANES), jnp.int32),
            jax.ShapeDtypeStruct((rows, picks * block_len), single),
            jax.ShapeDtypeStruct(index_query.shape, index_query.dtype),
            jax.ShapeDtypeStruct(index_weight.shape, index_weight.dtype),
        ),
        in_specs=[pl.BlockSpec(memory_space=pltpu.SMEM)] * 2
        + [pl.BlockSpec(memory_space=pltpu.VMEM)] * 2
        + [pl.BlockSpec(memory_space=pl.ANY)] * 2
        + [pl.BlockSpec(memory_space=pltpu.VMEM)] * 2,
        out_specs=[pl.BlockSpec(memory_space=pltpu.VMEM)] * 6,
        scratch_shapes=[
            pltpu.VMEM(queries.shape, keep),
            pltpu.VMEM(up_weight.shape, keep),
            dma((2,)),
            pltpu.VMEM((X, 8, LANES), jnp.int32),
            pltpu.SMEM((X, 8, LANES), jnp.int32),
            pltpu.VMEM((picks, LANES), jnp.int32),
            pltpu.SMEM((picks, LANES), jnp.int32),
            pltpu.VMEM((own_blocks, rows, half), keep),
            pltpu.VMEM((local_heads, tokens, q_width), keep),
            pltpu.VMEM((parts, block_len, part_keys), single),
            [pltpu.VMEM((own_blocks, rows, half), keep) for k in range(steps)],
            [pltpu.VMEM((own_blocks, rows, half), keep) for k in range(steps - 1)],
            pltpu.VMEM((hops + 1, peers, 4, rows, half), keep),
            pltpu.VMEM((hops + 1, peers, 4, rows, half), keep),
            pltpu.VMEM((zs * X, CORES, rows, half), keep),
            pltpu.VMEM((picks, block_len, full), keep),
            pltpu.VMEM((heads, block_len, width), keep),
            pltpu.VMEM((local_heads, block_len, width), keep),
            pltpu.VMEM((group * block_len, part_keys), single),
            pltpu.VMEM((group * block_len, part_keys), single),
            pltpu.VMEM((parts, heads * block_len, part_keys), single),
            pltpu.VMEM((parts, heads * block_len, LANES), single),
            pltpu.VMEM((parts, heads * block_len, LANES), single),
            pltpu.VMEM((3, rows, picks * block_len), single),
            pltpu.VMEM((3, rows, picks * block_len), single),
            dma((2, steps, 2)), dma((2, steps, 2)),
            dma((hops + 1, peers)), dma((hops + 1, peers)),
            dma((X - 1,)), dma((X - 1,)),
            dma((3, chunks)), dma((3, chunks)), dma((3,)), dma((3,)),
            dma, dma, dma((3,)), dma((3,)), dma((2,)), dma((2,)), dma,
        ],
        compiler_params=pltpu.CompilerParams(
            collective_id=0, has_side_effects=True, vmem_limit_bytes=56 * 2**20
        ),
        name="attend",
    )(picked, position, cache, index_key, queries, up_weight, index_query, index_weight)


def return_kernel(
    zs, ys, tabs_ref, ids_ref, part_ref, weight_ref, out_ref, home_ref,
    y_out, y_in, quarter, x_out, x_in, z_out, z_in, id_out, id_in, mine, theirs,
    ws_sem, wr_sem, is_sem, ir_sem, ys_sem, yr_sem, xs_sem, xr_sem, zs_sem, zr_sem, cs_sem, cr_sem, os_sem, or_sem,
):
    ctx = lax.axis_index("ctx")
    z, x = ctx // X, ctx % X
    y, c, y_a, y_b, y_far = y_sides(ys)
    head = y * CORES + c
    picks, block_len, width = part_ref.shape
    own_blocks = out_ref.shape[0]
    rows = block_len // ys
    to_a, to_b, to_far = (ctx, y_a * CORES + c), (ctx, y_b * CORES + c), (ctx, y_far * CORES + c)
    to_core = (ctx, y * CORES + 1 - c)
    x_peers = [(lax.rem(x + d, X), (z * X + lax.rem(x + d, X), head)) for d in range(1, X)]
    z_peers = [(lax.rem(z + d, zs), (lax.rem(z + d, zs) * X + x, head)) for d in range(1, zs)]
    home = c * ys + y
    comes_from = lax.rem(head, ys) * CORES + head // ys
    moves = home != head
    barrier = pltpu.get_barrier_semaphore()

    @pl.when(moves)
    def greet_movers():
        for other in (home, comes_from):
            pl.semaphore_signal(barrier, inc=1, device_id=(ctx, other), device_id_type=MESH)

    enter(
        [to_a, to_b, to_far, to_core] + [p[1] for p in x_peers] + [p[1] for p in z_peers],
        2 * moves.astype(jnp.int32),
    )

    def span(k):
        return pl.ds(pl.multiple_of(k * rows, rows), rows)

    y_copies = []
    order = sorted(range(1, zs), key=lambda d: -min(d, zs - d))
    line = lax.broadcasted_iota(jnp.int32, id_out.shape, 0)
    lane = lax.broadcasted_iota(jnp.int32, id_out.shape, 1)
    asked = jnp.zeros(id_out.shape, jnp.int32)
    for fx in range(X):
        row = jnp.where(
            c == 0, ids_ref[fx, 2 * CORES : 2 * CORES + 1, :], ids_ref[fx, 2 * CORES + 1 : 2 * CORES + 2, :]
        )
        asked = jnp.where(line == fx, jnp.broadcast_to(row, id_out.shape), asked)
    id_out[...] = asked
    id_in[z] = asked
    for n, (owner, device) in enumerate(((y_far, to_far), (y_a, to_a), (y_b, to_b))):
        y_out[n] = part_ref[:, span(owner), :].astype(y_out.dtype)
        copy = remote(y_out.at[n], y_in.at[n], ys_sem.at[n], yr_sem.at[n], device)
        copy.start()
        y_copies.append(copy)
    weight_copy = remote(weight_ref, home_ref, ws_sem, wr_sem, (ctx, home))

    @pl.when(moves)
    def move():
        weight_copy.start()

    @pl.when(jnp.logical_not(moves))
    def stay():
        home_ref[...] = weight_ref[...]

    for d in order:
        copy = remote(id_out, id_in.at[z], is_sem.at[d - 1], ir_sem.at[d - 1], z_peers[d - 1][1])
        copy.start()
        y_copies.append(copy)
    for n in range(ys - 1):
        remote(y_out.at[n], y_in.at[n], ys_sem.at[n], yr_sem.at[n], to_a).wait_recv()
    quarter[...] = (
        part_ref[:, span(y), :]
        + y_in[0].astype(jnp.float32)
        + y_in[1].astype(jnp.float32)
        + y_in[2].astype(jnp.float32)
    )

    def choose(tx, dst):
        def body(owner, carry):
            place = tabs_ref[x, 3 * CORES + c, owner * X + tx]
            value = quarter[jnp.maximum(place - 1, 0)]
            dst[owner] = jnp.where(place > 0, value, 0.0).astype(dst.dtype)
            return carry

        lax.fori_loop(0, zs, body, 0)

    x_copies = []
    for n, (tx, device) in enumerate(x_peers):
        choose(tx, x_out.at[n])
        copy = remote(x_out.at[n], x_in.at[x], xs_sem.at[n], xr_sem.at[n], device)
        copy.start()
        x_copies.append(copy)
    choose(x, x_in.at[x])
    for n in range(X - 1):
        fx = lax.rem(x + X - n - 1, X)
        remote(x_out.at[n], x_in.at[fx], xs_sem.at[n], xr_sem.at[n], to_a).wait_recv()

    def gather(owner, dst):
        for fx in range(X):
            dst[fx * rows : (fx + 1) * rows] = x_in[fx, owner]

    z_copies = []
    for d in order:
        tz, device = z_peers[d - 1]
        gather(tz, z_out.at[d - 1])
        copy = remote(z_out.at[d - 1], z_in.at[z], zs_sem.at[d - 1], zr_sem.at[d - 1], device)
        copy.start()
        z_copies.append(copy)
    gather(z, z_in.at[z])
    for d in order:
        fz = lax.rem(z + zs - d, zs)
        remote(id_out, id_in.at[fz], is_sem.at[d - 1], ir_sem.at[d - 1], to_a).wait_recv()
        remote(z_out.at[d - 1], z_in.at[fz], zs_sem.at[d - 1], zr_sem.at[d - 1], to_a).wait_recv()

    def add(fz, totals):
        ids = jnp.sum(jnp.where(lane == ctx, id_in[fz], 0), axis=1, keepdims=True)
        totals = list(totals)
        for fx in range(X):
            value = z_in[fz, fx * rows : (fx + 1) * rows].astype(jnp.float32)
            block = jnp.broadcast_to(ids[fx : fx + 1], value.shape)
            for r in range(own_blocks):
                totals[r] = totals[r] + jnp.where(block == r + 1, value, 0.0)
        return tuple(totals)

    totals = lax.fori_loop(
        0, zs, add, tuple(jnp.zeros((rows, width), jnp.float32) for r in range(own_blocks))
    )
    for r in range(own_blocks):
        mine[r] = totals[r]
    core = remote(mine, theirs, cs_sem, cr_sem, to_core)
    core.start()
    core.wait_recv()
    out_ref[:, span(y), :] = mine[...] + theirs[...]
    o_copies = []
    for n, device in enumerate((to_a, to_b, to_far)):
        ref = out_ref.at[:, span(y), :]
        copy = remote(ref, ref, os_sem.at[n], or_sem.at[n], device)
        copy.start()
        o_copies.append(copy)
    for n, fy in enumerate((y_b, y_a, y_far)):
        ref = out_ref.at[:, span(fy), :]
        remote(ref, ref, os_sem.at[n], or_sem.at[n], to_a).wait_recv()
    @pl.when(moves)
    def moved():
        weight_copy.wait_send()
        weight_copy.wait_recv()

    for copy in y_copies + [core] + x_copies + z_copies + o_copies:
        copy.wait_send()


def give_back(tables, key_part, weight_part, zs, ys, own_blocks):
    picks, block_len, width = key_part.shape
    rows = block_len // ys
    half = jnp.bfloat16
    dma = pltpu.SemaphoreType.DMA
    return pl.pallas_call(
        functools.partial(return_kernel, zs, ys),
        out_shape=(
            jax.ShapeDtypeStruct((own_blocks, block_len, width), jnp.float32),
            jax.ShapeDtypeStruct(weight_part.shape, jnp.float32),
        ),
        in_specs=[
            pl.BlockSpec(memory_space=pltpu.SMEM),
            pl.BlockSpec(memory_space=pltpu.VMEM),
            pl.BlockSpec(memory_space=pltpu.VMEM),
            pl.BlockSpec(memory_space=pltpu.VMEM),
        ],
        out_specs=[pl.BlockSpec(memory_space=pltpu.VMEM)] * 2,
        scratch_shapes=[
            pltpu.VMEM((3, picks, rows, width), half),
            pltpu.VMEM((3, picks, rows, width), half),
            pltpu.VMEM((picks, rows, width), jnp.float32),
            pltpu.VMEM((X - 1, zs, rows, width), half),
            pltpu.VMEM((X, zs, rows, width), half),
            pltpu.VMEM((zs - 1, X * rows, width), half),
            pltpu.VMEM((zs, X * rows, width), half),
            pltpu.VMEM((8, LANES), jnp.int32),
            pltpu.VMEM((zs, 8, LANES), jnp.int32),
            pltpu.VMEM((own_blocks, rows, width), jnp.float32),
            pltpu.VMEM((own_blocks, rows, width), jnp.float32),
            dma, dma, dma((zs - 1,)), dma((zs - 1,)),
            dma((3,)), dma((3,)), dma((X - 1,)), dma((X - 1,)), dma((zs - 1,)), dma((zs - 1,)),
            dma, dma, dma((3,)), dma((3,)),
        ],
        compiler_params=pltpu.CompilerParams(
            collective_id=2, has_side_effects=True, vmem_limit_bytes=40 * 2**20
        ),
        name="give_back",
    )(tables, tables, key_part, weight_part)


def masked_softmax(values, allowed):
    shifted = jnp.where(allowed, values, -jnp.inf)
    row_max = jnp.max(shifted, axis=-1, keepdims=True)
    expo = jnp.exp(shifted - row_max)
    return expo / jnp.sum(expo, axis=-1, keepdims=True)


def local(
    queries,
    up_weight,
    index_query,
    index_weight,
    cache_entry,
    index_key,
    block_position,
    picked_blocks,
):
    owners = lax.axis_size("ctx")
    head_devices = lax.axis_size("head")
    zs, ys = owners // X, head_devices // CORES
    picks = picked_blocks.shape[1]
    own_blocks, unused, block_len, entry_width = cache_entry.shape
    index_width = index_key.shape[3]
    key_count = picks * block_len
    rows = block_len // ys
    local_heads = queries.shape[1]
    target, index_keys, tables, mask, my_index_query, my_index_weight = attend(
        picked_blocks, block_position, cache_entry[:, 0], index_key[:, 0], jnp.transpose(queries, (1, 2, 0)), up_weight,
        index_query, index_weight, zs, ys, local_heads * head_devices,
    )
    index_keys = index_keys.reshape(key_count, index_width)
    my_allowed = mask == 0.0
    raw = jnp.einsum("ijd,sd->ijs", my_index_query, index_keys, preferred_element_type=jnp.float32)
    positive = jnp.maximum(raw, 0.0)
    score = jnp.sum(my_index_weight[:, :, None] * positive, axis=1)
    soft = masked_softmax(score, my_allowed)
    score_grad = jnp.where(my_allowed, soft - target, 0.0)
    weight_part = jnp.sum(score_grad[:, None, :] * positive, axis=2) * index_width ** (-0.5)
    coefficient = jnp.where(
        raw > 0, score_grad[:, None, :] * my_index_weight[:, :, None], 0.0
    ).astype(jnp.bfloat16)
    key_part = jnp.einsum(
        "ijs,ijd->sd", coefficient, my_index_query, preferred_element_type=jnp.float32
    )
    key_grad, weight_grad = give_back(
        tables, key_part.reshape(picks, block_len, index_width), weight_part, zs, ys, own_blocks
    )
    key_grad = key_grad.reshape(own_blocks, 1, block_len, index_width)
    return (key_grad, weight_grad)


def solution(mesh):
    return jax.shard_map(
        local,
        mesh=mesh,
        in_specs=(
            P("ctx", "head", None),
            P("head", None, None),
            P(("ctx", "head"), None, None),
            P(("ctx", "head"), None),
            P(None, "ctx", None, None),
            P(None, "ctx", None, None),
            P("ctx"),
            P("ctx", None),
        ),
        out_specs=(P(None, "ctx", None, None), P(("ctx", "head"), None)),
        check_vma=False,
    )
```
